32 devices in a mesh: dp: 16 (over z, y, core), strip: 2 (over x).
Axes of the slice: x: 2, y: 2, z: 4, core: 2. Of those that a mesh axis runs over, the one named last changes fastest.
Arguments:
- low_tokens: bfloat16 [64, 576, 1024], P('dp', 'strip'), may hold values from -6 to 6
- high_map: bfloat16 [64, 32, 32, 1536], P('dp', 'strip'), may hold values from -6 to 6
- counts: int32 [16], P('dp'), may hold values from 1 to 4, as said below
- row_edges: int32 [25], replicated, may hold values from 0 to 32, as said below
- col_edges: int32 [25], replicated, may hold values from 0 to 32, as said below
- w_qkv: bfloat16 [1024, 3072], replicated, may hold values from -0.1875 to 0.1875
- w_attn_out: bfloat16 [1024, 1024], replicated, may hold values from -1.5 to 1.5
- w_fc1: bfloat16 [1024, 4096], replicated, may hold values from -0.1875 to 0.1875
- w_fc2: bfloat16 [4096, 1024], replicated, may hold values from -0.09375 to 0.09375
- vit_gains: float32 [2, 1024], replicated, may hold values from 0.5 to 1.5
- vit_shifts: float32 [2, 1024], replicated, may hold values from -3 to 3
- w_pw1: bfloat16 [1536, 6144], replicated, may hold values from -0.15625 to 0.15625
- w_pw2: bfloat16 [6144, 1536], replicated, may hold values from -0.078125 to 0.078125
- w_pool: bfloat16 [1536, 1024], replicated, may hold values from -0.15625 to 0.15625
- dw_kernel: float32 [49, 1536], replicated, may hold values from -0.875 to 0.875
- conv_gains: float32 [2, 1536], replicated, may hold values from 0.5 to 1.5
- conv_shifts: float32 [2, 1536], replicated, may hold values from -3 to 3
- w_gate: float32 [1536], replicated, may hold values from -0.15625 to 0.15625
- d_merged: bfloat16 [64, 576, 1024], P('dp', 'strip'), may hold values from -6 to 6
- d_conv: bfloat16 [64, 32, 32, 1536], P('dp', 'strip'), may hold values from -6 to 6
Outputs:
- merged: bfloat16 [64, 576, 1024], P('dp', 'strip')
- conv_out: bfloat16 [64, 32, 32, 1536], P('dp', 'strip')
- grad_tokens: bfloat16 [64, 576, 1024], P('dp', 'strip')
- grad_map: bfloat16 [64, 32, 32, 1536], P('dp', 'strip')
- vit_grads: float32 [12587008], P(('dp', 'strip'))
- conv_grads: float32 [20530176], P(('dp', 'strip'))
The draws below stay inside these ranges and needn't reach their ends.
Inputs may be any that keep to these rules, and one draw needn't show every extreme that they name: `counts`: some sample has 4 live images and some has 1; most have 1 or 2. `row_edges`: starts at 0, ends at 32, consecutive entries differ by 1 or 2; where the row strips of the strip axis meet, the entry of the first bin of a strip's token rows differs by exactly one from the first map row of that strip, with the same sign at every such boundary. `col_edges`: starts at 0, ends at 32, consecutive entries differ by 1 or 2.
All inputs are finite; a program needn't handle non-finite values.
Results may differ from the reference program's by a relative error of at most 0.013.
Values may be sent and summed in bfloat16 or wider, within the bound.
No kernel may reach another device: no remote copies, remote signals or barrier semaphores. Data moves between devices by JAX's collectives and lax.ppermute only.
A program may use at most 640 MiB of HBM per device.

```python
import math
import jax
import jax.numpy as jnp
from jax import lax

D = 1024
HEADS = 16
FFN = 4096
C = 1536
FFC = 6144
KS = 7
GRID = 24
HR = 32
MAXIMG = 4
LT = 576
SAMPLES = 16
SLOTS = 64
N_STRIP = 2


def bin_edges(key, bin_count, cell_count):
    orders = jax.random.permutation(key, bin_count)
    widths = 1 + (orders < cell_count - bin_count).astype(jnp.int32)
    return jnp.concatenate([jnp.zeros((1,), jnp.int32), jnp.cumsum(widths).astype(jnp.int32)])


def draw_counts(key, part):
    key = jax.random.fold_in(key, 11)
    pick_key, place_key = jax.random.split(key)
    levels = jax.random.randint(pick_key, (SAMPLES,), 0, 16)
    counts = 1 + (levels >= 8).astype(jnp.int32) + (levels >= 12).astype(jnp.int32) + (levels >= 14).astype(jnp.int32)
    counts = jnp.minimum(counts, MAXIMG)
    places = jax.random.permutation(place_key, SAMPLES)
    counts = jnp.where(places == 0, MAXIMG, counts)
    counts = jnp.where(places == 1, 1, counts)
    return counts.astype(jnp.int32)


def draw_row_edges(key, part):
    key = jax.random.fold_in(key, 23)
    sign_key, group_key = jax.random.split(key)
    group_bins = GRID // N_STRIP
    group_rows = HR // N_STRIP
    sign = 2 * jax.random.randint(sign_key, (), 0, 2).astype(jnp.int32) - 1
    places = jnp.arange(N_STRIP + 1, dtype=jnp.int32)
    interior = (places > 0) & (places < N_STRIP)
    offsets = jnp.where(interior, sign, 0).astype(jnp.int32)
    lengths = group_rows + offsets[1:] - offsets[:-1]
    group_keys = jax.random.split(group_key, N_STRIP)
    orders = jax.vmap(lambda one_key: jax.random.permutation(one_key, group_bins))(group_keys)
    widths = 1 + (orders < (lengths - group_bins)[:, None]).astype(jnp.int32)
    return jnp.concatenate([jnp.zeros((1,), jnp.int32), jnp.cumsum(widths.reshape(-1)).astype(jnp.int32)])


def draw_col_edges(key, part):
    key = jax.random.fold_in(key, 37)
    return bin_edges(key, GRID, HR)


def shard_levels(own_key, dims, cuts, smallest, high):
    def one(axis_at, blocks):
        heights = jax.random.uniform(jax.random.fold_in(jax.random.fold_in(own_key, 6), axis_at), (blocks,), jnp.float32, smallest / len(cuts), high / len(cuts))
        return jnp.repeat(jnp.exp(heights), dims[axis_at] // blocks).reshape((-1,) + (1,) * (len(dims) - axis_at - 1))

    level = one(*cuts[0])
    for cut in cuts[1:]:
        level = level * one(*cut)
    return level


def centred(own_key, dims, scale, limit, cuts=(), kind=jnp.bfloat16):
    entries = scale * jax.random.normal(own_key, dims, jnp.float32)
    if cuts:
        entries = entries * shard_levels(own_key, dims, cuts, -0.22, 0.18)
    return jnp.clip(entries, -limit, limit).astype(kind)


def setup_inputs(seed: int = 0) -> dict:
    key_of = jax.random.split(jax.random.key(seed), 21)
    low_tokens = centred(key_of[0], (SLOTS, LT, D), 1.0, 6.0, ((0, 16), (1, 2)))
    high_map = centred(key_of[1], (SLOTS, HR, HR, C), 1.0, 6.0, ((0, 16), (1, 2)))
    counts = draw_counts(jax.random.fold_in(key_of[20], 71), 0)
    row_edges = draw_row_edges(jax.random.fold_in(key_of[20], 71), 0)
    col_edges = draw_col_edges(jax.random.fold_in(key_of[20], 71), 0)
    w_qkv = centred(key_of[5], (D, 3 * D), D ** -0.5, 0.1875)
    w_attn_out = centred(key_of[6], (D, D), (D // 64) ** -0.5, 1.5)
    w_fc1 = centred(key_of[7], (D, FFN), D ** -0.5, 0.1875)
    w_fc2 = centred(key_of[8], (FFN, D), FFN ** -0.5, 0.09375)
    vit_gains = jnp.clip(1.0 + 0.1 * jax.random.normal(key_of[9], (2, D), jnp.float32), 0.5, 1.5)
    vit_shifts = centred(key_of[10], (2, D), 0.3, 3.0, (), jnp.float32)
    w_pw1 = centred(key_of[11], (C, FFC), C ** -0.5, 0.15625)
    w_pw2 = centred(key_of[12], (FFC, C), FFC ** -0.5, 0.078125)
    w_pool = centred(key_of[13], (C, D), C ** -0.5, 0.15625)
    dw_kernel = centred(key_of[14], (KS * KS, C), (KS * KS) ** -0.5, 0.875, (), jnp.float32)
    conv_gains = jnp.clip(1.0 + 0.1 * jax.random.normal(key_of[15], (2, C), jnp.float32), 0.5, 1.5)
    conv_shifts = centred(key_of[16], (2, C), 0.3, 3.0, (), jnp.float32)
    w_gate = centred(key_of[17], (C,), C ** -0.5, 0.15625, (), jnp.float32)
    d_merged = centred(key_of[18], (SLOTS, LT, D), 1.0, 6.0, ((0, 16), (1, 2)))
    d_conv = centred(key_of[19], (SLOTS, HR, HR, C), 1.0, 6.0, ((0, 16), (1, 2)))
    return {"low_tokens": low_tokens, "high_map": high_map, "counts": counts, "row_edges": row_edges, "col_edges": col_edges, "w_qkv": w_qkv, "w_attn_out": w_attn_out, "w_fc1": w_fc1, "w_fc2": w_fc2, "vit_gains": vit_gains, "vit_shifts": vit_shifts, "w_pw1": w_pw1, "w_pw2": w_pw2, "w_pool": w_pool, "dw_kernel": dw_kernel, "conv_gains": conv_gains, "conv_shifts": conv_shifts, "w_gate": w_gate, "d_merged": d_merged, "d_conv": d_conv}


exact_mode = lax.Precision.HIGHEST
EPSILON = 1e-05

@jax.custom_vjp
def low(v):
    return lax.optimization_barrier(v.astype(jnp.bfloat16)).astype(jnp.float32)

@jax.custom_vjp
def low_back(v):
    return v

def low_keep(v):
    return (low(v), None)

def low_pass(kept, grad):
    return (grad,)

def back_keep(v):
    return (v, None)

def back_low(kept, grad):
    return (low(grad),)
low.defvjp(low_keep, low_pass)
low_back.defvjp(back_keep, back_low)

def normed(values, gain, shift):
    center = values - lax.optimization_barrier(jnp.mean(values, axis=-1, keepdims=True))
    spread = lax.optimization_barrier(jnp.mean(center * center, axis=-1, keepdims=True))
    return center * lax.rsqrt(spread + EPSILON) * gain + shift

def bin_matrix(edges, cell_count):
    cells = jnp.arange(cell_count, dtype=jnp.int32)
    inside = (cells[None, :] >= edges[:-1, None]) & (cells[None, :] < edges[1:, None])
    widths = (edges[1:] - edges[:-1]).astype(jnp.float32)
    return inside.astype(jnp.float32) / widths[:, None]

def depthwise(framed, kernel, row_count, col_count):
    total = jnp.zeros(framed.shape[:1] + (row_count, col_count) + framed.shape[3:], jnp.float32)
    for tap_row in range(KS):
        for tap_col in range(KS):
            total = total + kernel[tap_row * KS + tap_col] * framed[:, tap_row:tap_row + row_count, tap_col:tap_col + col_count, :]
    return total

def sample_forward(params, tokens, high, live_mask, row_pool, col_pool):
    w_qkv, w_attn_out, w_fc1, w_fc2, vit_gains, vit_shifts, w_pw1, w_pw2, w_pool, dw_kernel, conv_gains, conv_shifts, w_gate = params
    images = tokens.shape[0]
    head_size = D // HEADS
    normed_in = low(normed(tokens, vit_gains[0], vit_shifts[0]))
    qkv = low(low_back(jnp.einsum('itd,de->ite', normed_in, w_qkv, precision=exact_mode)))
    query = qkv[..., :D].reshape(images, LT, HEADS, head_size)
    key_heads = qkv[..., D:2 * D].reshape(images, LT, HEADS, head_size)
    value_heads = qkv[..., 2 * D:].reshape(images, LT, HEADS, head_size)
    scores = low_back(jnp.einsum('ithe,iuhe->ihtu', query, key_heads, precision=exact_mode) * (1.0 / math.sqrt(head_size)))
    probs = low(jax.nn.softmax(scores, axis=-1))
    mixed = jnp.einsum('ihtu,iuhe->ithe', probs, value_heads, precision=exact_mode).reshape(images, LT, D)
    mixed = low(low_back(mixed))
    residual = tokens + low_back(jnp.einsum('itd,de->ite', mixed, w_attn_out, precision=exact_mode))
    inner = low(normed(residual, vit_gains[1], vit_shifts[1]))
    mlp_act = low(jax.nn.gelu(low_back(jnp.einsum('itd,df->itf', inner, w_fc1, precision=exact_mode))))
    low_out = residual + low_back(jnp.einsum('itf,fd->itd', mlp_act, w_fc2, precision=exact_mode))
    reach = KS // 2
    framed = jnp.pad(high, ((0, 0), (reach, reach), (reach, reach), (0, 0)))
    conv_mid = conv_shifts[0] + depthwise(framed, dw_kernel, HR, HR)
    spatial = low(normed(conv_mid, conv_gains[0], conv_shifts[1]))
    expand = low(jax.nn.gelu(low_back(jnp.einsum('iyxc,cf->iyxf', spatial, w_pw1, precision=exact_mode))))
    high_out = high + conv_gains[1] * low_back(jnp.einsum('iyxf,fc->iyxc', expand, w_pw2, precision=exact_mode))
    pooled = jnp.einsum('by,iyxc,ax->ibac', row_pool, high_out, col_pool, precision=exact_mode).reshape(images, LT, C)
    pooled = low(low_back(pooled))
    lifted = low_back(jnp.einsum('itc,cd->itd', pooled, w_pool, precision=exact_mode))
    gate_value = jax.nn.sigmoid(lax.optimization_barrier(jnp.sum(pooled * w_gate, axis=-1, keepdims=True)))
    merged = live_mask[:, None, None] * (low_out + gate_value * lifted)
    conv_out = live_mask[:, None, None, None] * high_out
    return (merged, conv_out)

def reference(low_tokens, high_map, counts, row_edges, col_edges, w_qkv, w_attn_out, w_fc1, w_fc2, vit_gains, vit_shifts, w_pw1, w_pw2, w_pool, dw_kernel, conv_gains, conv_shifts, w_gate, d_merged, d_conv):
    live_mask = (jnp.arange(MAXIMG, dtype=jnp.int32)[None, :] < counts[:, None]).astype(jnp.float32)
    row_pool = bin_matrix(row_edges, HR)
    col_pool = bin_matrix(col_edges, HR)
    params = tuple((member.astype(jnp.float32) for member in (w_qkv, w_attn_out, w_fc1, w_fc2, vit_gains, vit_shifts, w_pw1, w_pw2, w_pool, dw_kernel, conv_gains, conv_shifts, w_gate)))
    tokens = low_tokens.astype(jnp.float32).reshape(SAMPLES, MAXIMG, LT, D)
    high = high_map.astype(jnp.float32).reshape(SAMPLES, MAXIMG, HR, HR, C)

    def forward(weights, token_all, high_all):

        def per_sample(pieces):
            return sample_forward(weights, pieces[0], pieces[1], pieces[2], row_pool, col_pool)
        return lax.map(jax.checkpoint(per_sample), (token_all, high_all, live_mask))
    (merged, conv_out), pullback = jax.vjp(forward, params, tokens, high)
    cotangent = (d_merged.astype(jnp.float32).reshape(tokens.shape), d_conv.astype(jnp.float32).reshape(high.shape))
    grad_params, grad_tokens, grad_map = pullback(cotangent)
    vit_grads = jnp.concatenate([member.reshape(-1) for member in grad_params[:6]])
    conv_grads = jnp.concatenate([member.reshape(-1) for member in grad_params[6:]])
    return (merged.reshape(SLOTS, LT, D).astype(jnp.bfloat16), conv_out.reshape(SLOTS, HR, HR, C).astype(jnp.bfloat16), grad_tokens.reshape(SLOTS, LT, D).astype(jnp.bfloat16), grad_map.reshape(SLOTS, HR, HR, C).astype(jnp.bfloat16), vit_grads, conv_grads)
```

```python
import math

import jax
import jax.numpy as jnp
from jax import lax
from jax.experimental import pallas as pl
from jax.experimental.pallas import tpu as pltpu
from jax.sharding import PartitionSpec as P

HEADS = 16
KS = 7
REACH = KS // 2
EPSILON = 1e-05
LANES = 128
EDGE = 8
F32 = jnp.float32
BF16 = jnp.bfloat16
VMEM_BYTES = 60 * 1024 * 1024


def dot_nn(a, b):
    return jnp.dot(a, b, preferred_element_type=F32)


def dot_nt(a, b):
    return lax.dot_general(a, b, (((1,), (1,)), ((), ())), preferred_element_type=F32)


def dot_tn(a, b):
    return lax.dot_general(a, b, (((0,), (0,)), ((), ())), preferred_element_type=F32)


def flip(value):
    return value.astype(F32).T.astype(BF16)


def row_step(rows):
    for step in (128, 96, 64, 48, 32, 16):
        if rows % step == 0:
            return step
    return rows


def over_rows(rows, body):
    step = row_step(rows)

    def one(at, carry):
        body(pl.ds(pl.multiple_of(at * step, step), step))
        return carry

    if step == rows:
        body(pl.ds(0, rows))
    else:
        lax.fori_loop(0, rows // step, one, 0)


def lane_tile(at):
    return pl.ds(pl.multiple_of(at * LANES, LANES), LANES)


def unit(values):
    center = values - jnp.mean(values, axis=-1, keepdims=True)
    inverse = lax.rsqrt(jnp.mean(center * center, axis=-1, keepdims=True) + EPSILON)
    return center * inverse, inverse


def unit_back(unit_values, inverse, grad):
    return (
        grad
        - jnp.mean(grad, axis=-1, keepdims=True)
        - unit_values * jnp.mean(grad * unit_values, axis=-1, keepdims=True)
    ) * inverse


def gelu_pair(x):
    scale = math.sqrt(2.0 / math.pi)
    square = x * x
    bend = jnp.tanh(x * (scale + (scale * 0.044715) * square))
    half = 0.5 + 0.5 * bend
    slope = half + (0.5 * x) * (1.0 - bend * bend) * (scale + (3.0 * scale * 0.044715) * square)
    return x * half, slope


def col_sum(values):
    return jnp.sum(values, axis=0, keepdims=True)


def held(at, live):
    return jnp.maximum(jnp.minimum(at, live[0] - 1), 0)


def slot(*shape):
    return pl.BlockSpec(
        (1,) + shape, lambda *g: (held(g[0], g[-1]),) + (0,) * len(shape)
    )


def every_slot(*shape):
    return pl.BlockSpec((1,) + shape, lambda *g: (g[0],) + (0,) * len(shape))


def whole(*shape):
    return pl.BlockSpec(shape, lambda *g: (0,) * len(shape), pipeline_mode=pl.Buffered(1))


def result(*shape):
    return pl.BlockSpec(shape, lambda *g: (0,) * len(shape))


def run(name, body, grid, live, args, in_specs, outs, scratch=(), flops=0):
    out_shape = [jax.ShapeDtypeStruct(shape, dtype) for shape, dtype, _ in outs]
    moved = sum(a.size * a.dtype.itemsize for a in args)
    moved += sum(math.prod(s) * jnp.dtype(d).itemsize for s, d, _ in outs)
    return pl.pallas_call(
        body,
        grid_spec=pltpu.PrefetchScalarGridSpec(
            num_scalar_prefetch=1,
            grid=grid,
            in_specs=in_specs,
            out_specs=[spec for _, _, spec in outs],
            scratch_shapes=list(scratch),
        ),
        out_shape=out_shape,
        compiler_params=pltpu.CompilerParams(
            dimension_semantics=("arbitrary",) * len(grid), vmem_limit_bytes=VMEM_BYTES
        ),
        cost_estimate=pl.CostEstimate(
            flops=int(flops), bytes_accessed=int(moved), transcendentals=0
        ),
        name=name,
    )(live, *args)


def vit_front(live, tok_all, w_qkv, w_out, gains, shifts, tok_rows):
    slots, key_rows, width = tok_all.shape
    head = width // HEADS
    pairs = width // LANES
    per_tile = LANES // head

    def body(
        n, x_ref, wq_ref, wo_ref, g_ref, b_ref,
        normed_ref, q_ref, kv_ref, probs_ref, mixed_ref, res_ref, inner_ref, flip_ref,
    ):
        @pl.when(pl.program_id(0) < n[0])
        def _():
            def first_norm(rows):
                value, _ = unit(x_ref[0, rows, :].astype(F32))
                normed_ref[0, rows, :] = (value * g_ref[0:1, :] + b_ref[0:1, :]).astype(BF16)

            over_rows(key_rows, first_norm)
            q_ref[0] = dot_nn(normed_ref[0, 0:tok_rows, :], wq_ref[:, 0:width]).astype(BF16)
            for part in range(4):
                cols = slice(part * width // 2, (part + 1) * width // 2)
                w_cols = slice(width + cols.start, width + cols.stop)
                kv_ref[0, :, cols] = dot_nn(normed_ref[0], wq_ref[:, w_cols]).astype(BF16)

            lane = lax.broadcasted_iota(jnp.int32, (1, LANES), 1) // head

            def heads(pair, carry):
                q = q_ref[0, :, lane_tile(pair)] * jnp.asarray(1.0 / math.sqrt(head), BF16)
                k = kv_ref[0, :, lane_tile(pair)].astype(F32)
                v_flip = flip(kv_ref[0, :, lane_tile(pairs + pair)])
                mixed = []
                for h in range(per_tile):
                    scores = dot_nt(jnp.where(lane == h, k, 0.0).astype(BF16), q)
                    top = jnp.max(scores, axis=0, keepdims=True)
                    raised = jnp.exp(scores - top)
                    probs = (raised * (1.0 / col_sum(raised))).astype(BF16)
                    probs_ref[0, pair * per_tile + h] = probs
                    mixed.append(dot_nn(v_flip[h * head : (h + 1) * head, :], probs))
                mixed_ref[0, :, lane_tile(pair)] = jnp.concatenate(mixed, axis=0).T.astype(BF16)
                return carry

            lax.fori_loop(0, pairs, heads, 0)
            res_ref[0] = dot_nn(mixed_ref[0], wo_ref[...])

            def second_norm(rows):
                res = res_ref[0, rows, :] + x_ref[0, rows, :].astype(F32)
                res_ref[0, rows, :] = res
                value, _ = unit(res)
                inner_ref[0, rows, :] = (value * g_ref[1:2, :] + b_ref[1:2, :]).astype(BF16)

            over_rows(tok_rows, second_norm)
            flip_ref[0] = flip(inner_ref[0])

    macs = slots * (key_rows * width * 2 * width + tok_rows * width * 2 * width)
    macs += slots * 2 * HEADS * tok_rows * key_rows * LANES
    return run(
        "vit_front",
        body,
        (slots,),
        live,
        (tok_all, w_qkv, w_out, gains, shifts),
        [slot(key_rows, width), whole(*w_qkv.shape), whole(*w_out.shape)]
        + [whole(*gains.shape), whole(*shifts.shape)],
        [
            ((slots, key_rows, width), BF16, slot(key_rows, width)),
            ((slots, tok_rows, width), BF16, slot(tok_rows, width)),
            ((slots, key_rows, 2 * width), BF16, slot(key_rows, 2 * width)),
            ((slots, HEADS, key_rows, tok_rows), BF16, slot(HEADS, key_rows, tok_rows)),
            ((slots, tok_rows, width), BF16, slot(tok_rows, width)),
            ((slots, tok_rows, width), F32, slot(tok_rows, width)),
            ((slots, tok_rows, width), BF16, slot(tok_rows, width)),
            ((slots, width, tok_rows), BF16, slot(width, tok_rows)),
        ],
        flops=2 * macs,
    )


def vit_mlp(live, inner, inner_flip, d_mlp, residual, w_fc1, w_fc2):
    slots, tok_rows, width = inner.shape
    hidden = w_fc1.shape[1]
    block = 512
    steps = hidden // block

    def body(
        n, x_ref, xt_ref, dm_ref, res_ref, w1_ref, w2_ref, low_ref, din_ref, g1_ref, g2_ref, a1, a2
    ):
        @pl.when(pl.program_id(0) == 0)
        def _():
            low_ref[...] = res_ref[...]
            din_ref[...] = jnp.zeros(din_ref.shape, F32)

        a1[...] = jnp.zeros(a1.shape, F32)
        a2[...] = jnp.zeros(a2.shape, F32)

        def one(at, carry):
            act, slope = gelu_pair(dot_nn(x_ref[at], w1_ref[...]))
            act = act.astype(BF16)
            low_ref[at] += dot_nn(act, w2_ref[...])
            d_fc = (slope * dot_nt(dm_ref[at], w2_ref[...])).astype(BF16)
            a1[...] += dot_nn(xt_ref[at], d_fc)
            a2[...] += dot_tn(act, dm_ref[at])
            din_ref[at] += dot_nt(d_fc, w1_ref[...])
            return carry

        lax.fori_loop(0, n[0], one, 0)
        g1_ref[...] = a1[...].astype(BF16)
        g2_ref[...] = a2[...].astype(BF16)

    wide = (slots, tok_rows, width)
    by_col = pl.BlockSpec((width, block), lambda j, n: (0, j))
    by_row = pl.BlockSpec((block, width), lambda j, n: (j, 0))
    return run(
        "vit_mlp",
        body,
        (steps,),
        live,
        (inner, inner_flip, d_mlp, residual, w_fc1, w_fc2),
        [whole(*wide), whole(*inner_flip.shape), whole(*wide), whole(*wide), by_col, by_row],
        [
            (wide, F32, result(*wide)),
            (wide, F32, result(*wide)),
            (w_fc1.shape, BF16, by_col),
            (w_fc2.shape, BF16, by_row),
        ],
        [pltpu.VMEM((width, block), F32), pltpu.VMEM((block, width), F32)],
        flops=12 * slots * tok_rows * width * hidden,
    )


def vit_back(live, residual, d_inner, d_merged, mixed, w_out, gains):
    slots, tok_rows, width = residual.shape

    def body(
        n, res_ref, din_ref, dm_ref, mix_ref, wo_ref, g_ref,
        dres_ref, dmix_ref, gout_ref, sums_ref, low, acc,
    ):
        at = pl.program_id(0)

        @pl.when(at == 0)
        def _():
            acc[...] = jnp.zeros(acc.shape, F32)
            sums_ref[...] = jnp.zeros(sums_ref.shape, F32)

        @pl.when(at < n[0])
        def _():
            def back(rows):
                value, inverse = unit(res_ref[0, rows, :])
                e = din_ref[0, rows, :]
                sums_ref[0:1, :] += col_sum(e * value)
                sums_ref[1:2, :] += col_sum(e)
                d_res = dm_ref[0, rows, :].astype(F32) + unit_back(value, inverse, e * g_ref[1:2, :])
                dres_ref[0, rows, :] = d_res
                low[rows, :] = d_res.astype(BF16)

            over_rows(tok_rows, back)
            dmix_ref[0] = dot_nt(low[...], wo_ref[...]).astype(BF16)
            acc[...] += dot_tn(mix_ref[0], low[...])

        @pl.when(at == slots - 1)
        def _():
            gout_ref[...] = acc[...].astype(BF16)

    wide = (slots, tok_rows, width)
    one = slot(tok_rows, width)
    return run(
        "vit_back",
        body,
        (slots,),
        live,
        (residual, d_inner, d_merged, mixed, w_out, gains),
        [one, one, one, one, whole(*w_out.shape), whole(*gains.shape)],
        [
            (wide, F32, one),
            (wide, BF16, one),
            (w_out.shape, BF16, result(*w_out.shape)),
            ((8, width), F32, result(8, width)),
        ],
        [pltpu.VMEM((tok_rows, width), BF16), pltpu.VMEM(w_out.shape, F32)],
        flops=4 * slots * tok_rows * width * width,
    )


def attention_back(live, probs, q, kv, d_mixed):
    slots, _, key_rows, tok_rows = probs.shape
    width = q.shape[2]
    head = width // HEADS
    pairs = width // LANES
    per_tile = LANES // head
    scale = 1.0 / math.sqrt(head)

    def body(n, p_ref, q_ref, k_ref, v_ref, dm_ref, dq_ref, dk_ref, dv_ref):
        @pl.when(pl.program_id(0) < n[0])
        def _():
            lane = lax.broadcasted_iota(jnp.int32, (1, LANES), 1) // head
            q = q_ref[0].astype(F32) * scale
            v = v_ref[0].astype(F32)
            dm = dm_ref[0].astype(F32)
            dm_low = dm_ref[0]
            k_flip = flip(k_ref[0].astype(F32) * scale)
            d_keys = jnp.zeros((key_rows, LANES), F32)
            d_values = jnp.zeros((key_rows, LANES), F32)
            d_query = []
            for h in range(per_tile):
                own = lane == h
                probs_low = p_ref[0, h]
                d_probs = dot_nt(jnp.where(own, v, 0.0).astype(BF16), dm_low)
                d_values += dot_nn(probs_low, jnp.where(own, dm, 0.0).astype(BF16))
                wide = probs_low.astype(F32)
                d_scores = (wide * (d_probs - col_sum(wide * d_probs))).astype(BF16)
                d_keys += dot_nn(d_scores, jnp.where(own, q, 0.0).astype(BF16))
                d_query.append(dot_nn(k_flip[h * head : (h + 1) * head, :], d_scores))
            dq_ref[0] = jnp.concatenate(d_query, axis=0).T.astype(BF16)
            dk_ref[0] = d_keys.astype(BF16)
            dv_ref[0] = d_values.astype(BF16)

    def held_pair(i, p, n):
        return jnp.where(i < n[0], p, pairs - 1)

    def at_pair(rows, shift=0):
        return pl.BlockSpec(
            (1, rows, LANES), lambda i, p, n: (held(i, n), 0, held_pair(i, p, n) + shift)
        )

    own = at_pair(tok_rows)
    keys = at_pair(key_rows)
    return run(
        "attention_back",
        body,
        (slots, pairs),
        live,
        (probs, q, kv, kv, d_mixed),
        [
            pl.BlockSpec(
                (1, per_tile, key_rows, tok_rows),
                lambda i, p, n: (held(i, n), held_pair(i, p, n), 0, 0),
            ),
            own,
            keys,
            at_pair(key_rows, pairs),
            own,
        ],
        [
            (q.shape, BF16, own),
            ((slots, key_rows, width), BF16, keys),
            ((slots, key_rows, width), BF16, keys),
        ],
        flops=8 * slots * HEADS * tok_rows * key_rows * LANES,
    )


def qkv_back(live, normed, d_q, d_k, d_v, w_qkv):
    slots, key_rows, width = normed.shape
    tok_rows = d_q.shape[1]

    def body(n, x_ref, dq_ref, dk_ref, dv_ref, w_ref, dn_ref, gw_ref, x_flip, acc):
        at = pl.program_id(0)

        @pl.when(at == 0)
        def _():
            acc[...] = jnp.zeros(acc.shape, F32)

        @pl.when(at < n[0])
        def _():
            x_flip[...] = flip(x_ref[0])
            dn_ref[0] = dot_nt(dk_ref[0], w_ref[:, width : 2 * width])
            dn_ref[0] += dot_nt(dv_ref[0], w_ref[:, 2 * width :])
            dn_ref[0, 0:tok_rows, :] += dot_nt(dq_ref[0], w_ref[:, 0:width])
            acc[:, 0:width] += dot_nn(x_flip[:, 0:tok_rows], dq_ref[0])
            acc[:, width : 2 * width] += dot_nn(x_flip[...], dk_ref[0])
            acc[:, 2 * width :] += dot_nn(x_flip[...], dv_ref[0])

        @pl.when(at == slots - 1)
        def _():
            gw_ref[...] = acc[...].astype(BF16)

    keys = slot(key_rows, width)
    return run(
        "qkv_back",
        body,
        (slots,),
        live,
        (normed, d_q, d_k, d_v, w_qkv),
        [keys, slot(tok_rows, width), keys, keys, whole(*w_qkv.shape)],
        [(normed.shape, F32, keys), (w_qkv.shape, BF16, result(*w_qkv.shape))],
        [pltpu.VMEM((width, key_rows), BF16), pltpu.VMEM(w_qkv.shape, F32)],
        flops=4 * slots * width * width * (2 * key_rows + tok_rows),
    )


def tokens_back(live, tokens, d_norm, arrived, d_residual, gains):
    slots, tok_rows, width = tokens.shape

    def body(n, x_ref, dn_ref, more_ref, dres_ref, g_ref, out_ref, sums_ref):
        at = pl.program_id(0)

        @pl.when(at == 0)
        def _():
            sums_ref[...] = jnp.zeros(sums_ref.shape, F32)

        @pl.when(at < n[0])
        def _():
            def back(rows):
                value, inverse = unit(x_ref[0, rows, :].astype(F32))
                e = dn_ref[0, rows, :] + more_ref[0, rows, :].astype(F32)
                sums_ref[0:1, :] += col_sum(e * value)
                sums_ref[1:2, :] += col_sum(e)
                grad = dres_ref[0, rows, :] + unit_back(value, inverse, e * g_ref[0:1, :])
                out_ref[0, rows, :] = grad.astype(BF16)

            over_rows(tok_rows, back)

        @pl.when(at >= n[0])
        def _():
            out_ref[...] = jnp.zeros(out_ref.shape, BF16)

    one = slot(tok_rows, width)
    return run(
        "tokens_back",
        body,
        (slots,),
        live,
        (tokens, d_norm, arrived, d_residual, gains),
        [one, one, one, one, whole(*gains.shape)],
        [
            (tokens.shape, BF16, every_slot(tok_rows, width)),
            ((8, width), F32, result(8, width)),
        ],
    )


def stage_rows(frame, top_ref, mid_ref, bottom_ref, lanes):
    rows, cols = mid_ref.shape[1], mid_ref.shape[2]
    inside = slice(EDGE, EDGE + cols)
    frame[0:REACH, inside, :] = top_ref[0, :, :, lanes].astype(F32)
    frame[REACH : REACH + rows, inside, :] = mid_ref[0, :, :, lanes].astype(F32)
    frame[REACH + rows :, inside, :] = bottom_ref[0, :, :, lanes].astype(F32)


def depthwise_rows(frame, rows, cols, tap, flipped, emit):
    totals = {}
    for y in range(rows + 2 * REACH):
        for left in range(KS):
            shifted = frame[y, EDGE - REACH + left : EDGE - REACH + left + cols, :]
            for top in range(KS):
                out = y - top
                if 0 <= out < rows:
                    at = (KS - 1 - top) * KS + KS - 1 - left if flipped else top * KS + left
                    term = shifted * tap(at)
                    totals[out] = totals[out] + term if out in totals else term
        if y >= 2 * REACH:
            emit(y - 2 * REACH, totals.pop(y - 2 * REACH))


def conv_front(live, top, high, bottom, kernel, gains, shifts):
    slots, rows, cols, channels = high.shape
    cells = rows * cols

    def body(
        n, top_ref, mid_ref, bottom_ref, k_ref, g_ref, b_ref,
        spatial_ref, flip_ref, unit_ref, inv_ref, frame, middle,
    ):
        @pl.when(pl.program_id(0) < n[0])
        def _():
            frame[...] = jnp.zeros(frame.shape, F32)

            def tile(at, carry):
                lanes = lane_tile(at)
                stage_rows(frame, top_ref, mid_ref, bottom_ref, lanes)
                bias = b_ref[0:1, lanes]

                def emit(y, total):
                    middle[y * cols : (y + 1) * cols, lanes] = total + bias

                depthwise_rows(frame, rows, cols, lambda t: k_ref[t : t + 1, lanes], False, emit)
                return carry

            lax.fori_loop(0, channels // LANES, tile, 0)

            def norm(part):
                value, inverse = unit(middle[part, :])
                inv_ref[0, part, :] = inverse
                unit_ref[0, part, :] = value.astype(BF16)
                spatial_ref[0, part, :] = (value * g_ref[0:1, :] + b_ref[1:2, :]).astype(BF16)

            over_rows(cells, norm)
            flip_ref[0] = flip(spatial_ref[0])

    halo = slot(REACH, cols, channels)
    return run(
        "conv_front",
        body,
        (slots,),
        live,
        (top, high, bottom, kernel, gains, shifts),
        [halo, slot(rows, cols, channels), halo, whole(*kernel.shape)]
        + [whole(*gains.shape), whole(*shifts.shape)],
        [
            ((slots, cells, channels), BF16, slot(cells, channels)),
            ((slots, channels, cells), BF16, slot(channels, cells)),
            ((slots, cells, channels), BF16, slot(cells, channels)),
            ((slots, cells, 1), F32, slot(cells, 1)),
        ],
        [
            pltpu.VMEM((rows + 2 * REACH, cols + 2 * EDGE, LANES), F32),
            pltpu.VMEM((cells, channels), F32),
        ],
        flops=2 * slots * cells * channels * KS * KS * 40,
    )


def conv_mlp(live, spatial, high, w_pw1, w_pw2, gains):
    slots, cells, channels = spatial.shape
    hidden = w_pw1.shape[1]
    block = 512
    steps = hidden // block

    def body(
        n, x_ref, high_ref, w1_ref, w2_ref, g_ref, act_ref, slope_ref, branch_ref, out_ref, acc
    ):
        at, step = pl.program_id(0), pl.program_id(1)

        @pl.when(at < n[0])
        def _():
            act, slope = gelu_pair(dot_nn(x_ref[0], w1_ref[...]))
            act = act.astype(BF16)
            act_ref[0] = act
            slope_ref[0] = slope.astype(BF16)
            part = dot_nn(act, w2_ref[...])

            @pl.when(step == 0)
            def _():
                acc[...] = part

            @pl.when(step > 0)
            def _():
                acc[...] += part

            @pl.when(step == steps - 1)
            def _():
                def close(rows):
                    branch = acc[rows, :]
                    branch_ref[0, rows, :] = branch.astype(BF16)
                    out_ref[0, rows, :] = (
                        high_ref[0, rows, :].astype(F32) + g_ref[1:2, :] * branch
                    ).astype(BF16)

                over_rows(cells, close)

        @pl.when((at >= n[0]) & (step == 0))
        def _():
            out_ref[...] = jnp.zeros(out_ref.shape, BF16)

    def held_step(i, j, n):
        return jnp.where(i < n[0], j, steps - 1)

    one = slot(cells, channels)
    hidden_block = pl.BlockSpec(
        (1, cells, block), lambda i, j, n: (held(i, n), 0, held_step(i, j, n))
    )
    return run(
        "conv_mlp",
        body,
        (slots, steps),
        live,
        (spatial, high, w_pw1, w_pw2, gains),
        [
            one,
            one,
            pl.BlockSpec((channels, block), lambda i, j, n: (0, held_step(i, j, n))),
            pl.BlockSpec((block, channels), lambda i, j, n: (held_step(i, j, n), 0)),
            whole(*gains.shape),
        ],
        [
            ((slots, cells, hidden), BF16, hidden_block),
            ((slots, cells, hidden), BF16, hidden_block),
            (spatial.shape, BF16, one),
            (spatial.shape, BF16, every_slot(cells, channels)),
        ],
        [pltpu.VMEM((cells, channels), F32)],
        flops=4 * slots * cells * channels * hidden,
    )


def pool(live, high_out, bins, side):
    slots, cells, channels = high_out.shape
    tok_rows = bins.shape[0] - 2 * side

    def body(n, x_ref, p_ref, own_ref, before_ref, after_ref):
        @pl.when(pl.program_id(0) < n[0])
        def _():
            part = dot_nn(p_ref[...], x_ref[0])
            before_ref[0] = part[0:side].astype(BF16)
            own_ref[0] = part[side : side + tok_rows]
            after_ref[0] = part[side + tok_rows :].astype(BF16)

    return run(
        "pool",
        body,
        (slots,),
        live,
        (high_out, bins),
        [slot(cells, channels), whole(*bins.shape)],
        [
            ((slots, tok_rows, channels), F32, slot(tok_rows, channels)),
            ((slots, side, channels), BF16, slot(side, channels)),
            ((slots, side, channels), BF16, slot(side, channels)),
        ],
        flops=2 * slots * cells * channels * bins.shape[0],
    )


def adapter(live, own, first, last, low_out, d_merged, w_pool, w_gate):
    slots, tok_rows, channels = own.shape
    side = first.shape[1]
    width = w_pool.shape[1]

    def body(
        n, own_ref, first_ref, last_ref, low_ref, dm_ref, w_ref, gate_ref,
        merged_ref, dpool_ref, gw_ref, ggate_ref, acc,
    ):
        at = pl.program_id(0)

        @pl.when(at == 0)
        def _():
            acc[...] = jnp.zeros(acc.shape, F32)
            ggate_ref[...] = jnp.zeros(ggate_ref.shape, F32)

        @pl.when(at < n[0])
        def _():
            pooled_low = jnp.concatenate(
                [
                    own_ref[0, 0:side] + first_ref[0].astype(F32),
                    own_ref[0, side : tok_rows - side],
                    own_ref[0, tok_rows - side :] + last_ref[0].astype(F32),
                ],
                axis=0,
            ).astype(BF16)
            pooled = pooled_low.astype(F32)
            lifted = dot_nn(pooled_low, w_ref[...])
            logit = jnp.sum(pooled * gate_ref[...], axis=-1, keepdims=True)
            gate = 1.0 / (1.0 + jnp.exp(-logit))
            merged_ref[0] = (low_ref[0] + gate * lifted).astype(BF16)
            d_top = dm_ref[0].astype(F32)
            d_logit = jnp.sum(d_top * lifted, axis=-1, keepdims=True) * gate * (1.0 - gate)
            d_lifted = (gate * d_top).astype(BF16)
            acc[...] += dot_tn(pooled_low, d_lifted)
            ggate_ref[0:1, :] += col_sum(d_logit * pooled)
            dpool_ref[0] = (dot_nt(d_lifted, w_ref[...]) + d_logit * gate_ref[...]).astype(BF16)

        @pl.when(at >= n[0])
        def _():
            merged_ref[...] = jnp.zeros(merged_ref.shape, BF16)

        @pl.when(at == slots - 1)
        def _():
            gw_ref[...] = acc[...].astype(BF16)

    edge = slot(side, channels)
    return run(
        "adapter",
        body,
        (slots,),
        live,
        (own, first, last, low_out, d_merged, w_pool, w_gate),
        [slot(tok_rows, channels), edge, edge, slot(tok_rows, width), slot(tok_rows, width)]
        + [whole(*w_pool.shape), whole(*w_gate.shape)],
        [
            ((slots, tok_rows, width), BF16, every_slot(tok_rows, width)),
            (own.shape, BF16, slot(tok_rows, channels)),
            (w_pool.shape, BF16, result(*w_pool.shape)),
            ((8, channels), F32, result(8, channels)),
        ],
        [pltpu.VMEM(w_pool.shape, F32)],
        flops=6 * slots * tok_rows * channels * width,
    )


def unpool(live, near, spread, d_conv, branch, gains):
    slots, near_rows, channels = near.shape
    cells = d_conv.shape[1]

    def body(n, near_ref, s_ref, dc_ref, branch_ref, g_ref, dpost_ref, dbranch_ref, sums_ref):
        at = pl.program_id(0)

        @pl.when(at == 0)
        def _():
            sums_ref[...] = jnp.zeros(sums_ref.shape, F32)

        @pl.when(at < n[0])
        def _():
            def part(rows):
                d_post = dc_ref[0, rows, :].astype(F32) + dot_nn(s_ref[rows, :], near_ref[0])
                sums_ref[0:1, :] += col_sum(d_post * branch_ref[0, rows, :].astype(F32))
                dpost_ref[0, rows, :] = d_post.astype(BF16)
                dbranch_ref[0, rows, :] = (g_ref[1:2, :] * d_post).astype(BF16)

            over_rows(cells, part)

    one = slot(cells, channels)
    return run(
        "unpool",
        body,
        (slots,),
        live,
        (near, spread, d_conv, branch, gains),
        [slot(near_rows, channels), whole(*spread.shape), one, one, whole(*gains.shape)],
        [
            (d_conv.shape, BF16, one),
            (d_conv.shape, BF16, one),
            ((8, channels), F32, result(8, channels)),
        ],
        flops=2 * slots * cells * channels * near_rows,
    )


def conv_mlp_back(live, spatial_flip, act, slope, d_branch, w_pw1, w_pw2):
    slots, channels, cells = spatial_flip.shape
    hidden = w_pw1.shape[1]
    block = 256
    steps = hidden // block

    def body(
        n, xt_ref, act_ref, slope_ref, db_ref, w1_ref, w2_ref, g1_ref, g2_ref, dsp_ref,
        a1, a2, dsp, sem,
    ):
        step = pl.program_id(0)

        @pl.when(step == 0)
        def _():
            dsp[...] = jnp.zeros(dsp.shape, F32)

        a1[...] = jnp.zeros(a1.shape, F32)
        a2[...] = jnp.zeros(a2.shape, F32)

        def one(at, carry):
            d_hidden = dot_nt(db_ref[at], w2_ref[...])
            d_expand = (slope_ref[at].astype(F32) * d_hidden).astype(BF16)
            a2[...] += dot_tn(act_ref[at], db_ref[at])
            a1[...] += dot_nn(xt_ref[at], d_expand)
            dsp[at] += dot_nt(d_expand, w1_ref[...])
            return carry

        lax.fori_loop(0, n[0], one, 0)
        g1_ref[...] = a1[...].astype(BF16)
        g2_ref[...] = a2[...].astype(BF16)

        @pl.when(step == steps - 1)
        def _():
            out = pltpu.make_async_copy(dsp, dsp_ref, sem)
            out.start()
            out.wait()

    by_col = pl.BlockSpec((channels, block), lambda j, n: (0, j))
    by_row = pl.BlockSpec((block, channels), lambda j, n: (j, 0))
    by_hidden = pl.BlockSpec((slots, cells, block), lambda j, n: (0, 0, j))
    wide = (slots, cells, channels)
    return run(
        "conv_mlp_back",
        body,
        (steps,),
        live,
        (spatial_flip, act, slope, d_branch, w_pw1, w_pw2),
        [whole(*spatial_flip.shape), by_hidden, by_hidden, whole(*wide), by_col, by_row],
        [
            (w_pw1.shape, BF16, by_col),
            (w_pw2.shape, BF16, by_row),
            (wide, F32, pl.BlockSpec(memory_space=pl.ANY)),
        ],
        [
            pltpu.VMEM((channels, block), F32),
            pltpu.VMEM((block, channels), F32),
            pltpu.VMEM(wide, F32),
            pltpu.SemaphoreType.DMA,
        ],
        flops=8 * slots * cells * channels * hidden,
    )


def conv_norm_back(live, d_spatial, unit_values, inverse, gains):
    slots, cells, channels = d_spatial.shape

    def body(n, e_ref, u_ref, inv_ref, g_ref, out_ref, sums_ref):
        at = pl.program_id(0)

        @pl.when(at == 0)
        def _():
            sums_ref[...] = jnp.zeros(sums_ref.shape, F32)

        @pl.when(at < n[0])
        def _():
            def part(rows):
                e = e_ref[0, rows, :]
                value = u_ref[0, rows, :].astype(F32)
                sums_ref[0:1, :] += col_sum(e * value)
                sums_ref[1:2, :] += col_sum(e)
                grad = unit_back(value, inv_ref[0, rows, :], e * g_ref[0:1, :])
                sums_ref[2:3, :] += col_sum(grad)
                out_ref[0, rows, :] = grad.astype(BF16)

            over_rows(cells, part)

    one = slot(cells, channels)
    return run(
        "conv_norm_back",
        body,
        (slots,),
        live,
        (d_spatial, unit_values, inverse, gains),
        [one, one, slot(cells, 1), whole(*gains.shape)],
        [(d_spatial.shape, BF16, one), ((8, channels), F32, result(8, channels))],
    )


def conv_back(live, top, high, bottom, d_top, d_mid, d_bottom, d_post, kernel):
    slots, rows, cols, channels = high.shape

    def body(
        n, top_ref, mid_ref, bottom_ref, dt_ref, dm_ref, db_ref, dpost_ref, k_ref,
        out_ref, gk_ref, frame, d_frame,
    ):
        at = pl.program_id(0)

        @pl.when(at == 0)
        def _():
            gk_ref[...] = jnp.zeros(gk_ref.shape, F32)

        @pl.when(at < n[0])
        def _():
            frame[...] = jnp.zeros(frame.shape, F32)
            d_frame[...] = jnp.zeros(d_frame.shape, F32)

            def tile(tile_at, carry):
                lanes = lane_tile(tile_at)
                stage_rows(frame, top_ref, mid_ref, bottom_ref, lanes)
                stage_rows(d_frame, dt_ref, dm_ref, db_ref, lanes)

                def emit(y, total):
                    grad = total + dpost_ref[0, y, :, lanes].astype(F32)
                    out_ref[0, y, :, lanes] = grad.astype(BF16)

                depthwise_rows(d_frame, rows, cols, lambda t: k_ref[t : t + 1, lanes], True, emit)
                for left in range(KS):
                    totals = [None] * KS
                    grads = {}
                    for y in range(rows + 2 * REACH):
                        begin = EDGE - REACH + left
                        shifted = frame[y, begin : begin + cols, :].reshape(cols // 8, 8, LANES)
                        if y < rows:
                            grads[y] = d_frame[y + REACH, EDGE : EDGE + cols, :].reshape(
                                cols // 8, 8, LANES
                            )
                        for tap_row in range(KS):
                            row = y - tap_row
                            if 0 <= row < rows:
                                term = jnp.sum(shifted * grads[row], axis=0)
                                old = totals[tap_row]
                                totals[tap_row] = term if old is None else old + term
                        grads.pop(y - KS + 1, None)
                    for tap_row in range(KS):
                        tap = tap_row * KS + left
                        gk_ref[tap : tap + 1, lanes] += col_sum(totals[tap_row])
                return carry

            lax.fori_loop(0, channels // LANES, tile, 0)

        @pl.when(at >= n[0])
        def _():
            out_ref[...] = jnp.zeros(out_ref.shape, BF16)

    halo = slot(REACH, cols, channels)
    one = slot(rows, cols, channels)
    frame_shape = (rows + 2 * REACH, cols + 2 * EDGE, LANES)
    return run(
        "conv_back",
        body,
        (slots,),
        live,
        (top, high, bottom, d_top, d_mid, d_bottom, d_post, kernel),
        [halo, one, halo, halo, one, halo, one, whole(*kernel.shape)],
        [
            (high.shape, BF16, every_slot(rows, cols, channels)),
            ((64, channels), F32, result(64, channels)),
        ],
        [pltpu.VMEM(frame_shape, F32), pltpu.VMEM(frame_shape, F32)],
        flops=4 * slots * rows * cols * channels * KS * KS * 40,
    )


def from_both_sides(head, tail):
    count = lax.axis_size("strip")
    before = lax.ppermute(tail, "strip", [(i, i + 1) for i in range(count - 1)])
    after = lax.ppermute(head, "strip", [(i + 1, i) for i in range(count - 1)])
    return before, after


def bin_weights(edges, cell_count):
    cells = jnp.arange(cell_count, dtype=jnp.int32)
    inside = (cells[None, :] >= edges[:-1, None]) & (cells[None, :] < edges[1:, None])
    widths = (edges[1:] - edges[:-1]).astype(F32)
    return inside.astype(F32) / widths[:, None]


def strip_bins(edges, first_bin, bin_count, first_cell, cell_count):
    padded = jnp.concatenate([edges[:1], edges, edges[-1:]])
    window = lax.dynamic_slice_in_dim(padded, first_bin + 1, bin_count + 1)
    cells = first_cell + jnp.arange(cell_count, dtype=jnp.int32)
    inside = (cells[None, :] >= window[:-1, None]) & (cells[None, :] < window[1:, None])
    widths = jnp.maximum(window[1:] - window[:-1], 1).astype(F32)
    return inside.astype(F32) / widths[:, None]


def bit_of(axis, bit):
    return (lax.axis_index(axis) >> bit) & 1


def swap_halves(cells, axis, bit, own):
    size = lax.axis_size(axis)
    keep = lax.dynamic_index_in_dim(cells, own, 1, keepdims=False)
    send = lax.dynamic_index_in_dim(cells, 1 - own, 1, keepdims=False)
    got = lax.ppermute(send, axis, [(i, i ^ (1 << bit)) for i in range(size)])
    return (keep.astype(F32) + got.astype(F32)).astype(BF16)


def bits(axis):
    return int(math.log2(lax.axis_size(axis)))


def halve_dp(cells, base, bit):
    if cells.shape[0] % 2:
        cells = jnp.pad(cells, [(0, 1)] + [(0, 0)] * (cells.ndim - 1))
    own = (bit_of("dp", bit) - base) & 1
    cells = cells.reshape((cells.shape[0] // 2, 2) + cells.shape[1:])
    return swap_halves(cells, "dp", bit, own), (base + own) >> 1


def halve_strip(cells):
    for bit in range(bits("strip")):
        m, count = cells.shape[:2]
        cells = cells.reshape((m * count // 2, 2) + cells.shape[2:])
        cells = swap_halves(cells, "strip", bit, bit_of("strip", bit))
        cells = cells.reshape((m, count // 2) + cells.shape[1:])
    return cells


def shared_sum(matrix, offset, chunk, strip_first):
    strips = lax.axis_size("strip")
    rows, cols = matrix.shape
    chunk_rows = chunk // cols
    base = offset // (chunk * strips)
    front = (offset - base * chunk * strips) // cols
    groups = -(-(front + rows) // (chunk_rows * strips))
    back = groups * chunk_rows * strips - front - rows
    cells = jnp.pad(matrix, ((front, back), (0, 0))).reshape(groups, strips, chunk_rows, cols)
    cells, base = halve_dp(cells, base, 0)
    if strip_first:
        cells = halve_strip(cells)
        cells, base = halve_dp(cells, base, 1)
    else:
        cells, base = halve_dp(cells, base, 1)
        cells = halve_strip(cells)
    return cells.reshape(cells.shape[0], chunk), base


def owned_chunk(matrices, extras):
    data_count = lax.axis_size("dp")
    strips = lax.axis_size("strip")
    devices = data_count * strips
    total = sum(m.size for m in matrices)
    chunk = total // devices
    extra = extras.shape[0] // devices
    span = data_count // 4
    placed = None
    offset = 0
    for order, matrix in enumerate(matrices):
        part, base = shared_sum(matrix, offset, chunk, order % 2 == 0)
        canvas = jnp.zeros((span + part.shape[0], chunk), BF16)
        canvas = lax.dynamic_update_slice(canvas, part, (base, 0))[:span]
        placed = canvas if placed is None else placed + canvas
        offset += matrix.size
    for bit in range(2, bits("dp")):
        placed = placed.reshape(placed.shape[0] // 2, 2, chunk)
        placed = swap_halves(placed, "dp", bit, bit_of("dp", bit))
    mine = placed.reshape(chunk).astype(F32)
    index = lax.axis_index("dp") * strips + lax.axis_index("strip")
    pieces = [mine]
    left = extras.shape[0]
    padded = jnp.pad(extras, (0, chunk))
    for hop in range(1, -(-left // chunk) + 1):
        size = min(left, chunk)
        left -= size
        following = lax.ppermute(
            mine[:size].astype(BF16),
            ("dp", "strip"),
            [(i + hop, i) for i in range(devices - hop)],
        ).astype(F32)
        past = index + hop - devices
        own_extras = lax.dynamic_slice(padded, (jnp.maximum(past, 0) * chunk,), (size,))
        pieces.append(jnp.where(past >= 0, own_extras, following))
    return lax.dynamic_slice(jnp.concatenate(pieces), (index * extra,), (chunk + extra,))


def per_device(
    low_tokens,
    high_map,
    counts,
    row_edges,
    col_edges,
    w_qkv,
    w_attn_out,
    w_fc1,
    w_fc2,
    vit_gains,
    vit_shifts,
    w_pw1,
    w_pw2,
    w_pool,
    dw_kernel,
    conv_gains,
    conv_shifts,
    w_gate,
    d_merged,
    d_conv,
):
    slots, tok_rows, width = low_tokens.shape
    rows, cols, channels = high_map.shape[1:]
    cells = rows * cols
    strips = lax.axis_size("strip")
    strip = lax.axis_index("strip")
    live = counts[:1]

    col_bins = bin_weights(col_edges, cols)
    side = col_bins.shape[0]
    own_bins = tok_rows // side
    near_bins = strip_bins(row_edges, strip * own_bins - 1, own_bins + 2, strip * rows, rows)
    bins = (near_bins[:, None, :, None] * col_bins[None, :, None, :]).astype(BF16)
    bins = bins.reshape((own_bins + 2) * side, cells)

    def shifted(value, by):
        return lax.ppermute(value, "strip", [(i, (i + by) % strips) for i in range(strips)])

    tok_all = jnp.concatenate(
        [low_tokens] + [shifted(low_tokens, by) for by in range(1, strips)], axis=1
    )
    top, bottom = from_both_sides(high_map[:, :REACH], high_map[:, -REACH:])

    spatial, spatial_flip, conv_unit, conv_inverse = conv_front(
        live, top, high_map, bottom, dw_kernel, conv_gains, conv_shifts
    )
    act, slope, branch, high_out = conv_mlp(
        live, spatial, high_map.reshape(slots, cells, channels), w_pw1, w_pw2, conv_gains
    )
    own, before_part, after_part = pool(live, high_out, bins, side)
    first, last = from_both_sides(before_part, after_part)

    normed, q, kv, probs, mixed, residual, inner, inner_flip = vit_front(
        live, tok_all, w_qkv, w_attn_out, vit_gains, vit_shifts, tok_rows
    )
    low_out, d_inner, grad_fc1, grad_fc2 = vit_mlp(
        live, inner, inner_flip, d_merged, residual, w_fc1, w_fc2
    )
    merged, d_pooled, grad_pool, gate_sums = adapter(
        live, own, first, last, low_out, d_merged, w_pool, w_gate.reshape(1, channels)
    )
    near_before, near_after = from_both_sides(d_pooled[:, :side], d_pooled[:, -side:])
    d_post, d_branch, scale_sums = unpool(
        live,
        jnp.concatenate([near_before, d_pooled, near_after], axis=1),
        bins.T,
        d_conv.reshape(slots, cells, channels),
        branch,
        conv_gains,
    )
    grad_pw1, grad_pw2, d_spatial = conv_mlp_back(
        live, spatial_flip, act, slope, d_branch, w_pw1, w_pw2
    )
    d_conv_in, norm_sums = conv_norm_back(live, d_spatial, conv_unit, conv_inverse, conv_gains)
    d_conv_in = d_conv_in.reshape(high_map.shape)
    d_before, d_after = from_both_sides(d_conv_in[:, :REACH], d_conv_in[:, -REACH:])

    d_residual, d_mixed, grad_out, inner_sums = vit_back(
        live, residual, d_inner, d_merged, mixed, w_attn_out, vit_gains
    )
    d_q, d_k, d_v = attention_back(live, probs, q, kv, d_mixed)
    d_normed, grad_qkv = qkv_back(live, normed, d_q, d_k, d_v, w_qkv)
    arrived = jnp.zeros(low_tokens.shape, BF16)
    for by in range(1, strips):
        part = d_normed[:, by * tok_rows : (by + 1) * tok_rows].astype(BF16)
        arrived = arrived + shifted(part, -by) if by > 1 else shifted(part, -by)
    grad_tokens, token_sums = tokens_back(
        live, low_tokens, d_normed, arrived, d_residual, vit_gains
    )
    grad_map, kernel_sums = conv_back(
        live,
        top,
        high_map,
        bottom,
        d_before,
        d_conv_in,
        d_after,
        d_post.reshape(high_map.shape),
        dw_kernel,
    )

    vit_extras = jnp.concatenate([token_sums[0], inner_sums[0], token_sums[1], inner_sums[1]])
    conv_extras = jnp.concatenate(
        [
            kernel_sums[: KS * KS].reshape(-1),
            norm_sums[0],
            scale_sums[0],
            norm_sums[2],
            norm_sums[1],
            gate_sums[0],
        ]
    )
    extras = lax.psum(jnp.concatenate([vit_extras, conv_extras]), ("dp", "strip"))
    vit_grads = owned_chunk(
        [grad_qkv, grad_out, grad_fc1, grad_fc2], extras[: vit_extras.shape[0]]
    )
    conv_grads = owned_chunk([grad_pw1, grad_pw2, grad_pool], extras[vit_extras.shape[0] :])
    return (
        merged,
        high_out.reshape(high_map.shape),
        grad_tokens,
        grad_map,
        vit_grads,
        conv_grads,
    )


def solution(mesh):
    images = P("dp", "strip", None)
    maps = P("dp", "strip", None, None)
    flat = P(("dp", "strip"))
    in_specs = (images, maps, P("dp")) + (P(),) * 15 + (images, maps)
    out_specs = (images, maps, images, maps, flat, flat)
    return jax.shard_map(
        per_device, mesh=mesh, in_specs=in_specs, out_specs=out_specs, check_vma=False
    )
```

```python
import math

import jax
import jax.numpy as jnp
from jax import lax
from jax.experimental import pallas as pl
from jax.experimental.pallas import tpu as pltpu
from jax.sharding import PartitionSpec as P

HEADS = 16
KS = 7
REACH = KS // 2
EPSILON = 1e-05
LANES = 128
EDGE = 8
BLOCK = 256
HALF_CHUNKS = 16
F32 = jnp.float32
BF16 = jnp.bfloat16
VMEM_BYTES = 60 * 1024 * 1024


def dot_nn(a, b):
    return jnp.dot(a, b, preferred_element_type=F32)


def dot_nt(a, b):
    return lax.dot_general(a, b, (((1,), (1,)), ((), ())), preferred_element_type=F32)


def dot_tn(a, b):
    return lax.dot_general(a, b, (((0,), (0,)), ((), ())), preferred_element_type=F32)


def flip(value):
    return value.astype(F32).T.astype(BF16)


def row_step(rows):
    for step in (128, 96, 64, 48, 32, 16):
        if rows % step == 0:
            return step
    return rows


def over_rows(rows, body):
    step = row_step(rows)

    def one(at, carry):
        body(pl.ds(pl.multiple_of(at * step, step), step))
        return carry

    if step == rows:
        body(pl.ds(0, rows))
    else:
        lax.fori_loop(0, rows // step, one, 0)


def lane_tile(at):
    return pl.ds(pl.multiple_of(at * LANES, LANES), LANES)


def unit(values):
    center = values - jnp.mean(values, axis=-1, keepdims=True)
    inverse = lax.rsqrt(jnp.mean(center * center, axis=-1, keepdims=True) + EPSILON)
    return center * inverse, inverse


def unit_back(unit_values, inverse, grad):
    return (
        grad
        - jnp.mean(grad, axis=-1, keepdims=True)
        - unit_values * jnp.mean(grad * unit_values, axis=-1, keepdims=True)
    ) * inverse


def gelu_pair(x):
    scale = math.sqrt(2.0 / math.pi)
    square = x * x
    bend = jnp.tanh(x * (scale + (scale * 0.044715) * square))
    half = 0.5 + 0.5 * bend
    slope = half + (0.5 * x) * (1.0 - bend * bend) * (scale + (3.0 * scale * 0.044715) * square)
    return x * half, slope


def col_sum(values):
    return jnp.sum(values, axis=0, keepdims=True)


def held(at, live):
    return jnp.maximum(jnp.minimum(at, live[0] - 1), 0)


def slot(*shape):
    return pl.BlockSpec(
        (1,) + shape, lambda *g: (held(g[0], g[-1]),) + (0,) * len(shape)
    )


def every_slot(*shape):
    return pl.BlockSpec((1,) + shape, lambda *g: (g[0],) + (0,) * len(shape))


def whole(*shape):
    return pl.BlockSpec(shape, lambda *g: (0,) * len(shape), pipeline_mode=pl.Buffered(1))


def result(*shape):
    return pl.BlockSpec(shape, lambda *g: (0,) * len(shape))


def run(name, body, grid, live, args, in_specs, outs, scratch=(), flops=0, after=(), alias=()):
    out_shape = [jax.ShapeDtypeStruct(shape, dtype) for shape, dtype, _ in outs]
    moved = sum(a.size * a.dtype.itemsize for a in args)
    moved += sum(math.prod(s) * jnp.dtype(d).itemsize for s, d, _ in outs)
    count = 1 + len(args)

    def without_order(*refs):
        body(*refs[:count], *refs[count + len(after) :])

    return pl.pallas_call(
        without_order,
        grid_spec=pltpu.PrefetchScalarGridSpec(
            num_scalar_prefetch=1,
            grid=grid,
            in_specs=list(in_specs) + [pl.BlockSpec(memory_space=pl.ANY)] * len(after),
            out_specs=[spec for _, _, spec in outs],
            scratch_shapes=list(scratch),
        ),
        out_shape=out_shape,
        input_output_aliases={1 + given: out for given, out in alias},
        compiler_params=pltpu.CompilerParams(
            dimension_semantics=("arbitrary",) * len(grid), vmem_limit_bytes=VMEM_BYTES
        ),
        cost_estimate=pl.CostEstimate(
            flops=int(flops), bytes_accessed=int(moved), transcendentals=0
        ),
        name=name,
    )(live, *args, *after)


class Flat:
    def __init__(self, shapes, devices):
        self.shapes = shapes
        self.chunk = sum(r * c for r, c in shapes) // devices
        self.units = self.chunk // BLOCK
        self.pieces = []
        self.even = sum(r * c for r, c in shapes) % (devices * BLOCK * 3 * 16) == 0
        offset = 0
        for rows, cols in shapes:
            self.even &= self.chunk % cols == 0 and offset % cols == 0 and cols % BLOCK == 0
            found = []
            if self.even:
                height, begin = self.chunk // cols, offset // cols
                for k in range(devices):
                    low = max(k * height, begin)
                    high = min((k + 1) * height, begin + rows)
                    if low < high:
                        start = (low - k * height) * (cols // BLOCK)
                        found.append((k, low - begin, high - low, start))
                        self.even &= (high - low) % 8 == 0 and start % 16 == 0
            self.pieces.append(found)
            offset += rows * cols

    def within(self, matrix, first, count):
        out = []
        for k, row, height, start in self.pieces[matrix]:
            low, high = max(row, first), min(row + height, first + count)
            if low < high:
                out.append((k, low, high - low, start + low - row, height))
        return out


def side_of(chunk):
    z1, z0, y = (chunk >> 4) & 1, (chunk >> 3) & 1, (chunk >> 2) & 1
    return (chunk >> 1) & 1, z1 * 8 + (z0 ^ z1) * 4 + y * 2 + (chunk & 1)


def copy_out(own_core, keep_ref, send_ref, copies, sems, action):
    for at, (chunk, source, place, rows) in enumerate(copies):
        core, index = side_of(chunk)
        for held_here, ref in ((True, keep_ref), (False, send_ref)):

            @pl.when((own_core == core) == held_here)
            def _(ref=ref, at=at, source=source, place=place, rows=rows, index=index):
                target = ref.at[index, pl.ds(place, rows), :]
                getattr(pltpu.make_async_copy(source, target, sems.at[at]), action)()


def copy_all(own_core, keep_ref, send_ref, stage, flat, matrix, sems):
    copies = []
    for k, row, rows, start in flat.pieces[matrix]:
        for c in range(stage.shape[1] // BLOCK):
            copies.append((k, block_of(stage, row, rows, c), start + c * rows, rows))
    copy_out(own_core, keep_ref, send_ref, copies, sems, "start")
    copy_out(own_core, keep_ref, send_ref, copies, sems, "wait")


def copy_semaphores(flat, matrix):
    return pltpu.SemaphoreType.DMA((len(flat.pieces[matrix]) * flat.shapes[matrix][1] // BLOCK,))


def halves(flat):
    shape = (HALF_CHUNKS, flat.units, BLOCK)
    spec = pl.BlockSpec(memory_space=pl.ANY)
    return [(shape, BF16, spec), (shape, BF16, spec)]


def block_of(ref, first, rows, block):
    return ref.at[pl.ds(first, rows), pl.ds(block * BLOCK, BLOCK)]


def vit_front(live, tok_all, w_qkv, w_out, gains, shifts, tok_rows, after):
    slots, key_rows, width = tok_all.shape
    head = width // HEADS
    pairs = width // LANES
    per_tile = LANES // head

    def body(
        n, x_ref, wq_ref, wo_ref, g_ref, b_ref,
        normed_ref, q_ref, kv_ref, probs_ref, mixed_ref, res_ref, inner_ref, flip_ref,
    ):
        @pl.when(pl.program_id(0) < n[0])
        def _():
            def first_norm(rows):
                value, _ = unit(x_ref[0, rows, :].astype(F32))
                normed_ref[0, rows, :] = (value * g_ref[0:1, :] + b_ref[0:1, :]).astype(BF16)

            over_rows(key_rows, first_norm)
            q_ref[0] = dot_nn(normed_ref[0, 0:tok_rows, :], wq_ref[:, 0:width]).astype(BF16)
            for part in range(4):
                cols = slice(part * width // 2, (part + 1) * width // 2)
                w_cols = slice(width + cols.start, width + cols.stop)
                kv_ref[0, :, cols] = dot_nn(normed_ref[0], wq_ref[:, w_cols]).astype(BF16)

            lane = lax.broadcasted_iota(jnp.int32, (1, LANES), 1) // head

            def heads(pair, carry):
                q = q_ref[0, :, lane_tile(pair)] * jnp.asarray(1.0 / math.sqrt(head), BF16)
                k = kv_ref[0, :, lane_tile(pair)].astype(F32)
                v_flip = flip(kv_ref[0, :, lane_tile(pairs + pair)])
                mixed = []
                for h in range(per_tile):
                    scores = dot_nt(jnp.where(lane == h, k, 0.0).astype(BF16), q)
                    top = jnp.max(scores, axis=0, keepdims=True)
                    raised = jnp.exp(scores - top)
                    probs = (raised * (1.0 / col_sum(raised))).astype(BF16)
                    probs_ref[0, pair * per_tile + h] = probs
                    mixed.append(dot_nn(v_flip[h * head : (h + 1) * head, :], probs))
                mixed_ref[0, :, lane_tile(pair)] = jnp.concatenate(mixed, axis=0).T.astype(BF16)
                return carry

            lax.fori_loop(0, pairs, heads, 0)
            res_ref[0] = dot_nn(mixed_ref[0], wo_ref[...])

            def second_norm(rows):
                res = res_ref[0, rows, :] + x_ref[0, rows, :].astype(F32)
                res_ref[0, rows, :] = res
                value, _ = unit(res)
                inner_ref[0, rows, :] = (value * g_ref[1:2, :] + b_ref[1:2, :]).astype(BF16)

            over_rows(tok_rows, second_norm)
            flip_ref[0] = flip(inner_ref[0])

    macs = slots * (key_rows * width * 2 * width + tok_rows * width * 2 * width)
    macs += slots * 2 * HEADS * tok_rows * key_rows * LANES
    return run(
        "vit_front",
        body,
        (slots,),
        live,
        (tok_all, w_qkv, w_out, gains, shifts),
        [slot(key_rows, width), whole(*w_qkv.shape), whole(*w_out.shape)]
        + [whole(*gains.shape), whole(*shifts.shape)],
        [
            ((slots, key_rows, width), BF16, slot(key_rows, width)),
            ((slots, tok_rows, width), BF16, slot(tok_rows, width)),
            ((slots, key_rows, 2 * width), BF16, slot(key_rows, 2 * width)),
            ((slots, HEADS, key_rows, tok_rows), BF16, slot(HEADS, key_rows, tok_rows)),
            ((slots, tok_rows, width), BF16, slot(tok_rows, width)),
            ((slots, tok_rows, width), F32, slot(tok_rows, width)),
            ((slots, tok_rows, width), BF16, slot(tok_rows, width)),
            ((slots, width, tok_rows), BF16, slot(width, tok_rows)),
        ],
        flops=2 * macs,
        after=after,
    )


def vit_mlp(live, inner, inner_flip, d_mlp, residual, lift, w_fc1, w_fc2, flat, after):
    slots, tok_rows, width = inner.shape
    hidden = w_fc1.shape[1]
    block = 512
    steps = hidden // block
    blocks = width // BLOCK

    def body(
        n, x_ref, xt_ref, dm_ref, res_ref, lift_ref, w1_ref, w2_ref,
        merged_ref, din_ref, out1_ref, out2_ref, low, a1, a2, *rest,
    ):
        step = pl.program_id(0)

        @pl.when(step == 0)
        def _():
            low[...] = res_ref[...]
            din_ref[...] = jnp.zeros(din_ref.shape, F32)

        a1[...] = jnp.zeros(a1.shape, F32)
        a2[...] = jnp.zeros(a2.shape, F32)

        def one(at, carry):
            act, slope = gelu_pair(dot_nn(x_ref[at], w1_ref[...]))
            act = act.astype(BF16)
            low[at] += dot_nn(act, w2_ref[...])
            d_fc = (slope * dot_nt(dm_ref[at], w2_ref[...])).astype(BF16)
            a1[...] += dot_nn(xt_ref[at], d_fc)
            a2[...] += dot_tn(act, dm_ref[at])
            din_ref[at] += dot_nt(d_fc, w1_ref[...])
            return carry

        lax.fori_loop(0, n[0], one, 0)

        @pl.when(step == steps - 1)
        def _():
            def close(at, carry):
                merged_ref[at] = (low[at] + lift_ref[at]).astype(BF16)
                return carry

            def blank(at, carry):
                merged_ref[at] = jnp.zeros(merged_ref.shape[1:], BF16)
                return carry

            lax.fori_loop(0, n[0], close, 0)
            lax.fori_loop(n[0], slots, blank, 0)

        if flat is None:
            out1_ref[...] = a1[...].astype(BF16)
            out2_ref[...] = a2[...].astype(BF16)
            return
        stage1, stage2, sems1, sems2 = rest

        def first_copies(at):
            out = []
            for c in range(block // BLOCK):
                for k, row, rows, start, height in flat.within(2, 0, width):
                    place = start + (at * (block // BLOCK) + c) * height
                    out.append((k, block_of(stage1, row, rows, c), pl.multiple_of(place, 16), rows))
            return out

        def second_copies(at):
            out = []
            for k, row, rows, start, height in flat.within(3, at * block, block):
                for c in range(blocks):
                    source = block_of(stage2, row - at * block, rows, c)
                    out.append((k, source, start + c * height, rows))
            return out

        def each(at, now, action):
            copy_out(n[1], out1_ref, out2_ref, first_copies(now), sems1, action)
            for static in range(steps):

                @pl.when(now == static)
                def _(static=static):
                    copy_out(n[1], out1_ref, out2_ref, second_copies(static), sems2, action)

        @pl.when(step > 0)
        def _():
            each(step, step - 1, "wait")

        stage1[...] = a1[...].astype(BF16)
        stage2[...] = a2[...].astype(BF16)
        each(step, step, "start")

        @pl.when(step == steps - 1)
        def _():
            each(step, step, "wait")

    wide = (slots, tok_rows, width)
    by_col = pl.BlockSpec((width, block), lambda j, n: (0, j))
    by_row = pl.BlockSpec((block, width), lambda j, n: (j, 0))
    scratch = [
        pltpu.VMEM(wide, F32),
        pltpu.VMEM((width, block), F32),
        pltpu.VMEM((block, width), F32),
    ]
    if flat is None:
        grads = [(w_fc1.shape, BF16, by_col), (w_fc2.shape, BF16, by_row)]
    else:
        grads = halves(flat)
        most = max(len(flat.within(3, at * block, block)) for at in range(steps))
        scratch += [
            pltpu.VMEM((width, block), BF16),
            pltpu.VMEM((block, width), BF16),
            pltpu.SemaphoreType.DMA((block // BLOCK * len(flat.pieces[2]),)),
            pltpu.SemaphoreType.DMA((most * blocks,)),
        ]
    return run(
        "vit_mlp",
        body,
        (steps,),
        live,
        (inner, inner_flip, d_mlp, residual, lift, w_fc1, w_fc2),
        [whole(*wide), whole(*inner_flip.shape)] + [whole(*wide)] * 3 + [by_col, by_row],
        [(wide, BF16, result(*wide)), (wide, F32, result(*wide))] + grads,
        scratch,
        flops=12 * slots * tok_rows * width * hidden,
        after=after,
    )


def vit_back(live, residual, d_inner, d_merged, mixed, w_out, gains, flat, kept, after):
    slots, tok_rows, width = residual.shape

    def body(n, res_ref, din_ref, dm_ref, mix_ref, wo_ref, g_ref, *rest):
        if flat is None:
            dres_ref, dmix_ref, sums_ref, gout_ref, low, acc = rest
        else:
            _, _, dres_ref, dmix_ref, sums_ref, keep_ref, send_ref, low, acc, stage, sems = rest
        at = pl.program_id(0)

        @pl.when(at == 0)
        def _():
            acc[...] = jnp.zeros(acc.shape, F32)
            sums_ref[...] = jnp.zeros(sums_ref.shape, F32)

        @pl.when(at < n[0])
        def _():
            def back(rows):
                value, inverse = unit(res_ref[0, rows, :])
                e = din_ref[0, rows, :]
                sums_ref[0:1, :] += col_sum(e * value)
                sums_ref[1:2, :] += col_sum(e)
                d_res = dm_ref[0, rows, :].astype(F32) + unit_back(value, inverse, e * g_ref[1:2, :])
                dres_ref[0, rows, :] = d_res
                low[rows, :] = d_res.astype(BF16)

            over_rows(tok_rows, back)
            dmix_ref[0] = dot_nt(low[...], wo_ref[...]).astype(BF16)
            acc[...] += dot_tn(mix_ref[0], low[...])

        @pl.when(at == slots - 1)
        def _():
            if flat is None:
                gout_ref[...] = acc[...].astype(BF16)
            else:
                stage[...] = acc[...].astype(BF16)
                copy_all(n[1], keep_ref, send_ref, stage, flat, 1, sems)

    wide = (slots, tok_rows, width)
    one = slot(tok_rows, width)
    args = (residual, d_inner, d_merged, mixed, w_out, gains)
    specs = [one, one, one, one, whole(*w_out.shape), whole(*gains.shape)]
    scratch = [pltpu.VMEM((tok_rows, width), BF16), pltpu.VMEM(w_out.shape, F32)]
    grads, alias = [(w_out.shape, BF16, result(*w_out.shape))], ()
    if flat is not None:
        args, specs, grads = args + kept, specs + [pl.BlockSpec(memory_space=pl.ANY)] * 2, halves(flat)
        scratch += [pltpu.VMEM(w_out.shape, BF16), copy_semaphores(flat, 1)]
        alias = ((6, 3), (7, 4))
    return run(
        "vit_back",
        body,
        (slots,),
        live,
        args,
        specs,
        [(wide, F32, one), (wide, BF16, one), ((8, width), F32, result(8, width))] + grads,
        scratch,
        flops=4 * slots * tok_rows * width * width,
        after=after,
        alias=alias,
    )


def attention_back(live, probs, q, kv, d_mixed):
    slots, _, key_rows, tok_rows = probs.shape
    width = q.shape[2]
    head = width // HEADS
    pairs = width // LANES
    per_tile = LANES // head
    scale = 1.0 / math.sqrt(head)

    def body(n, p_ref, q_ref, k_ref, v_ref, dm_ref, dq_ref, dk_ref, dv_ref):
        @pl.when(pl.program_id(0) < n[0])
        def _():
            lane = lax.broadcasted_iota(jnp.int32, (1, LANES), 1) // head
            q = q_ref[0].astype(F32) * scale
            v = v_ref[0].astype(F32)
            dm = dm_ref[0].astype(F32)
            dm_low = dm_ref[0]
            k_flip = flip(k_ref[0].astype(F32) * scale)
            d_keys = jnp.zeros((key_rows, LANES), F32)
            d_values = jnp.zeros((key_rows, LANES), F32)
            d_query = []
            for h in range(per_tile):
                own = lane == h
                probs_low = p_ref[0, h]
                d_probs = dot_nt(jnp.where(own, v, 0.0).astype(BF16), dm_low)
                d_values += dot_nn(probs_low, jnp.where(own, dm, 0.0).astype(BF16))
                wide = probs_low.astype(F32)
                d_scores = (wide * (d_probs - col_sum(wide * d_probs))).astype(BF16)
                d_keys += dot_nn(d_scores, jnp.where(own, q, 0.0).astype(BF16))
                d_query.append(dot_nn(k_flip[h * head : (h + 1) * head, :], d_scores))
            dq_ref[0] = jnp.concatenate(d_query, axis=0).T.astype(BF16)
            dk_ref[0] = d_keys.astype(BF16)
            dv_ref[0] = d_values.astype(BF16)

    def held_pair(i, p, n):
        return jnp.where(i < n[0], p, pairs - 1)

    def at_pair(rows, shift=0):
        return pl.BlockSpec(
            (1, rows, LANES), lambda i, p, n: (held(i, n), 0, held_pair(i, p, n) + shift)
        )

    own = at_pair(tok_rows)
    keys = at_pair(key_rows)
    return run(
        "attention_back",
        body,
        (slots, pairs),
        live,
        (probs, q, kv, kv, d_mixed),
        [
            pl.BlockSpec(
                (1, per_tile, key_rows, tok_rows),
                lambda i, p, n: (held(i, n), held_pair(i, p, n), 0, 0),
            ),
            own,
            keys,
            at_pair(key_rows, pairs),
            own,
        ],
        [
            (q.shape, BF16, own),
            ((slots, key_rows, width), BF16, keys),
            ((slots, key_rows, width), BF16, keys),
        ],
        flops=8 * slots * HEADS * tok_rows * key_rows * LANES,
    )


def qkv_back(live, normed, d_q, d_k, d_v, w_qkv, flat, kept):
    slots, key_rows, width = normed.shape
    tok_rows = d_q.shape[1]

    def body(n, x_ref, dq_ref, dk_ref, dv_ref, w_ref, *rest):
        if flat is None:
            dn_ref, gw_ref, x_flip, acc = rest
        else:
            _, _, dn_ref, keep_ref, send_ref, x_flip, acc, stage, sems = rest
        at = pl.program_id(0)

        @pl.when(at == 0)
        def _():
            acc[...] = jnp.zeros(acc.shape, F32)

        @pl.when(at < n[0])
        def _():
            x_flip[...] = flip(x_ref[0])
            dn_ref[0] = dot_nt(dk_ref[0], w_ref[:, width : 2 * width])
            dn_ref[0] += dot_nt(dv_ref[0], w_ref[:, 2 * width :])
            dn_ref[0, 0:tok_rows, :] += dot_nt(dq_ref[0], w_ref[:, 0:width])
            acc[:, 0:width] += dot_nn(x_flip[:, 0:tok_rows], dq_ref[0])
            acc[:, width : 2 * width] += dot_nn(x_flip[...], dk_ref[0])
            acc[:, 2 * width :] += dot_nn(x_flip[...], dv_ref[0])

        @pl.when(at == slots - 1)
        def _():
            if flat is None:
                gw_ref[...] = acc[...].astype(BF16)
            else:
                stage[...] = acc[...].astype(BF16)
                copy_all(n[1], keep_ref, send_ref, stage, flat, 0, sems)

    keys = slot(key_rows, width)
    args = (normed, d_q, d_k, d_v, w_qkv)
    specs = [keys, slot(tok_rows, width), keys, keys, whole(*w_qkv.shape)]
    scratch = [pltpu.VMEM((width, key_rows), BF16), pltpu.VMEM(w_qkv.shape, F32)]
    grads, alias = [(w_qkv.shape, BF16, result(*w_qkv.shape))], ()
    if flat is not None:
        args, specs, grads = args + kept, specs + [pl.BlockSpec(memory_space=pl.ANY)] * 2, halves(flat)
        scratch += [pltpu.VMEM(w_qkv.shape, BF16), copy_semaphores(flat, 0)]
        alias = ((5, 1), (6, 2))
    return run(
        "qkv_back",
        body,
        (slots,),
        live,
        args,
        specs,
        [(normed.shape, F32, keys)] + grads,
        scratch,
        flops=4 * slots * width * width * (2 * key_rows + tok_rows),
        alias=alias,
    )


def tokens_back(live, tokens, d_norm, arrived, d_residual, gains, after):
    slots, tok_rows, width = tokens.shape

    def body(n, x_ref, dn_ref, more_ref, dres_ref, g_ref, out_ref, sums_ref):
        at = pl.program_id(0)

        @pl.when(at == 0)
        def _():
            sums_ref[...] = jnp.zeros(sums_ref.shape, F32)

        @pl.when(at < n[0])
        def _():
            def back(rows):
                value, inverse = unit(x_ref[0, rows, :].astype(F32))
                e = dn_ref[0, rows, :] + more_ref[0, rows, :].astype(F32)
                sums_ref[0:1, :] += col_sum(e * value)
                sums_ref[1:2, :] += col_sum(e)
                grad = dres_ref[0, rows, :] + unit_back(value, inverse, e * g_ref[0:1, :])
                out_ref[0, rows, :] = grad.astype(BF16)

            over_rows(tok_rows, back)

        @pl.when(at >= n[0])
        def _():
            out_ref[...] = jnp.zeros(out_ref.shape, BF16)

    one = slot(tok_rows, width)
    return run(
        "tokens_back",
        body,
        (slots,),
        live,
        (tokens, d_norm, arrived, d_residual, gains),
        [one, one, one, one, whole(*gains.shape)],
        [
            (tokens.shape, BF16, every_slot(tok_rows, width)),
            ((8, width), F32, result(8, width)),
        ],
        after=after,
    )


def stage_rows(frame, top_ref, mid_ref, bottom_ref, lanes):
    rows, cols = mid_ref.shape[1], mid_ref.shape[2]
    inside = slice(EDGE, EDGE + cols)
    frame[0:REACH, inside, :] = top_ref[0, :, :, lanes].astype(F32)
    frame[REACH : REACH + rows, inside, :] = mid_ref[0, :, :, lanes].astype(F32)
    frame[REACH + rows :, inside, :] = bottom_ref[0, :, :, lanes].astype(F32)


def depthwise_rows(frame, rows, cols, tap, flipped, emit):
    totals = {}
    for y in range(rows + 2 * REACH):
        for left in range(KS):
            shifted = frame[y, EDGE - REACH + left : EDGE - REACH + left + cols, :]
            for top in range(KS):
                out = y - top
                if 0 <= out < rows:
                    at = (KS - 1 - top) * KS + KS - 1 - left if flipped else top * KS + left
                    term = shifted * tap(at)
                    totals[out] = totals[out] + term if out in totals else term
        if y >= 2 * REACH:
            emit(y - 2 * REACH, totals.pop(y - 2 * REACH))


def conv_front(live, top, high, bottom, kernel, gains, shifts):
    slots, rows, cols, channels = high.shape
    cells = rows * cols

    def body(
        n, top_ref, mid_ref, bottom_ref, k_ref, g_ref, b_ref,
        spatial_ref, flip_ref, unit_ref, inv_ref, frame, middle,
    ):
        @pl.when(pl.program_id(0) < n[0])
        def _():
            frame[...] = jnp.zeros(frame.shape, F32)

            def tile(at, carry):
                lanes = lane_tile(at)
                stage_rows(frame, top_ref, mid_ref, bottom_ref, lanes)
                bias = b_ref[0:1, lanes]

                def emit(y, total):
                    middle[y * cols : (y + 1) * cols, lanes] = total + bias

                depthwise_rows(frame, rows, cols, lambda t: k_ref[t : t + 1, lanes], False, emit)
                return carry

            lax.fori_loop(0, channels // LANES, tile, 0)

            def norm(part):
                value, inverse = unit(middle[part, :])
                inv_ref[0, part, :] = inverse
                unit_ref[0, part, :] = value.astype(BF16)
                spatial_ref[0, part, :] = (value * g_ref[0:1, :] + b_ref[1:2, :]).astype(BF16)

            over_rows(cells, norm)
            flip_ref[0] = flip(spatial_ref[0])

    halo = slot(REACH, cols, channels)
    return run(
        "conv_front",
        body,
        (slots,),
        live,
        (top, high, bottom, kernel, gains, shifts),
        [halo, slot(rows, cols, channels), halo, whole(*kernel.shape)]
        + [whole(*gains.shape), whole(*shifts.shape)],
        [
            ((slots, cells, channels), BF16, slot(cells, channels)),
            ((slots, channels, cells), BF16, slot(channels, cells)),
            ((slots, cells, channels), BF16, slot(cells, channels)),
            ((slots, cells, 1), F32, slot(cells, 1)),
        ],
        [
            pltpu.VMEM((rows + 2 * REACH, cols + 2 * EDGE, LANES), F32),
            pltpu.VMEM((cells, channels), F32),
        ],
        flops=2 * slots * cells * channels * KS * KS * 40,
    )


def conv_mlp(live, spatial, high, w_pw1, w_pw2, gains):
    slots, cells, channels = spatial.shape
    hidden = w_pw1.shape[1]
    block = 512
    steps = hidden // block

    def body(
        n, x_ref, high_ref, w1_ref, w2_ref, g_ref, act_ref, slope_ref, branch_ref, out_ref, acc
    ):
        at, step = pl.program_id(0), pl.program_id(1)

        @pl.when(at < n[0])
        def _():
            act, slope = gelu_pair(dot_nn(x_ref[0], w1_ref[...]))
            act = act.astype(BF16)
            act_ref[0] = act
            slope_ref[0] = slope.astype(BF16)
            part = dot_nn(act, w2_ref[...])

            @pl.when(step == 0)
            def _():
                acc[...] = part

            @pl.when(step > 0)
            def _():
                acc[...] += part

            @pl.when(step == steps - 1)
            def _():
                def close(rows):
                    branch = acc[rows, :]
                    branch_ref[0, rows, :] = branch.astype(BF16)
                    out_ref[0, rows, :] = (
                        high_ref[0, rows, :].astype(F32) + g_ref[1:2, :] * branch
                    ).astype(BF16)

                over_rows(cells, close)

        @pl.when((at >= n[0]) & (step == 0))
        def _():
            out_ref[...] = jnp.zeros(out_ref.shape, BF16)

    def held_step(i, j, n):
        return jnp.where(i < n[0], j, steps - 1)

    one = slot(cells, channels)
    hidden_block = pl.BlockSpec(
        (1, cells, block), lambda i, j, n: (held(i, n), 0, held_step(i, j, n))
    )
    return run(
        "conv_mlp",
        body,
        (slots, steps),
        live,
        (spatial, high, w_pw1, w_pw2, gains),
        [
            one,
            one,
            pl.BlockSpec((channels, block), lambda i, j, n: (0, held_step(i, j, n))),
            pl.BlockSpec((block, channels), lambda i, j, n: (held_step(i, j, n), 0)),
            whole(*gains.shape),
        ],
        [
            ((slots, cells, hidden), BF16, hidden_block),
            ((slots, cells, hidden), BF16, hidden_block),
            (spatial.shape, BF16, one),
            (spatial.shape, BF16, every_slot(cells, channels)),
        ],
        [pltpu.VMEM((cells, channels), F32)],
        flops=4 * slots * cells * channels * hidden,
    )


def pool(live, high_out, bins, side):
    slots, cells, channels = high_out.shape
    tok_rows = bins.shape[0] - 2 * side

    def body(n, x_ref, p_ref, own_ref, before_ref, after_ref):
        @pl.when(pl.program_id(0) < n[0])
        def _():
            part = dot_nn(p_ref[...], x_ref[0])
            before_ref[0] = part[0:side].astype(BF16)
            own_ref[0] = part[side : side + tok_rows]
            after_ref[0] = part[side + tok_rows :].astype(BF16)

    return run(
        "pool",
        body,
        (slots,),
        live,
        (high_out, bins),
        [slot(cells, channels), whole(*bins.shape)],
        [
            ((slots, tok_rows, channels), F32, slot(tok_rows, channels)),
            ((slots, side, channels), BF16, slot(side, channels)),
            ((slots, side, channels), BF16, slot(side, channels)),
        ],
        flops=2 * slots * cells * channels * bins.shape[0],
    )


def adapter(live, own, first, last, d_merged, w_pool, w_gate, after):
    slots, tok_rows, channels = own.shape
    side = first.shape[1]
    width = w_pool.shape[1]

    def body(
        n, own_ref, first_ref, last_ref, dm_ref, w_ref, gate_ref,
        lift_ref, dpool_ref, gw_ref, ggate_ref, acc,
    ):
        at = pl.program_id(0)

        @pl.when(at == 0)
        def _():
            acc[...] = jnp.zeros(acc.shape, F32)
            ggate_ref[...] = jnp.zeros(ggate_ref.shape, F32)

        @pl.when(at < n[0])
        def _():
            pooled_low = jnp.concatenate(
                [
                    own_ref[0, 0:side] + first_ref[0].astype(F32),
                    own_ref[0, side : tok_rows - side],
                    own_ref[0, tok_rows - side :] + last_ref[0].astype(F32),
                ],
                axis=0,
            ).astype(BF16)
            pooled = pooled_low.astype(F32)
            lifted = dot_nn(pooled_low, w_ref[...])
            logit = jnp.sum(pooled * gate_ref[...], axis=-1, keepdims=True)
            gate = 1.0 / (1.0 + jnp.exp(-logit))
            lift_ref[0] = gate * lifted
            d_top = dm_ref[0].astype(F32)
            d_logit = jnp.sum(d_top * lifted, axis=-1, keepdims=True) * gate * (1.0 - gate)
            d_lifted = (gate * d_top).astype(BF16)
            acc[...] += dot_tn(pooled_low, d_lifted)
            ggate_ref[0:1, :] += col_sum(d_logit * pooled)
            dpool_ref[0] = (dot_nt(d_lifted, w_ref[...]) + d_logit * gate_ref[...]).astype(BF16)

        @pl.when(at == slots - 1)
        def _():
            gw_ref[...] = acc[...].astype(BF16)

    edge = slot(side, channels)
    return run(
        "adapter",
        body,
        (slots,),
        live,
        (own, first, last, d_merged, w_pool, w_gate),
        [slot(tok_rows, channels), edge, edge, slot(tok_rows, width)]
        + [whole(*w_pool.shape), whole(*w_gate.shape)],
        [
            ((slots, tok_rows, width), F32, slot(tok_rows, width)),
            (own.shape, BF16, slot(tok_rows, channels)),
            (w_pool.shape, BF16, result(*w_pool.shape)),
            ((8, channels), F32, result(8, channels)),
        ],
        [pltpu.VMEM(w_pool.shape, F32)],
        flops=6 * slots * tok_rows * channels * width,
        after=after,
    )


def unpool(live, near, spread, d_conv, branch, gains):
    slots, near_rows, channels = near.shape
    cells = d_conv.shape[1]

    def body(n, near_ref, s_ref, dc_ref, branch_ref, g_ref, dpost_ref, dbranch_ref, sums_ref):
        at = pl.program_id(0)

        @pl.when(at == 0)
        def _():
            sums_ref[...] = jnp.zeros(sums_ref.shape, F32)

        @pl.when(at < n[0])
        def _():
            def part(rows):
                d_post = dc_ref[0, rows, :].astype(F32) + dot_nn(s_ref[rows, :], near_ref[0])
                sums_ref[0:1, :] += col_sum(d_post * branch_ref[0, rows, :].astype(F32))
                dpost_ref[0, rows, :] = d_post.astype(BF16)
                dbranch_ref[0, rows, :] = (g_ref[1:2, :] * d_post).astype(BF16)

            over_rows(cells, part)

    one = slot(cells, channels)
    return run(
        "unpool",
        body,
        (slots,),
        live,
        (near, spread, d_conv, branch, gains),
        [slot(near_rows, channels), whole(*spread.shape), one, one, whole(*gains.shape)],
        [
            (d_conv.shape, BF16, one),
            (d_conv.shape, BF16, one),
            ((8, channels), F32, result(8, channels)),
        ],
        flops=2 * slots * cells * channels * near_rows,
    )


def conv_mlp_back(live, spatial_flip, act, slope, d_branch, w_pw1, w_pw2, grad_pool, flat):
    slots, channels, cells = spatial_flip.shape
    hidden = w_pw1.shape[1]
    block = BLOCK
    steps = hidden // block
    blocks = channels // BLOCK

    def body(
        n, xt_ref, act_ref, slope_ref, db_ref, w1_ref, w2_ref, pool_ref,
        dsp_ref, out1_ref, out2_ref, a1, a2, dsp, sem, *rest,
    ):
        step = pl.program_id(0)
        odd = lax.rem(step, 2)

        @pl.when(step == 0)
        def _():
            dsp[...] = jnp.zeros(dsp.shape, F32)

        a1[odd] = jnp.zeros(a1.shape[1:], F32)
        a2[...] = jnp.zeros(a2.shape, F32)

        def one(at, carry):
            d_hidden = dot_nt(db_ref[at], w2_ref[...])
            d_expand = (slope_ref[at].astype(F32) * d_hidden).astype(BF16)
            a2[...] += dot_tn(act_ref[at], db_ref[at])
            a1[odd] += dot_nn(xt_ref[at], d_expand)
            dsp[at] += dot_nt(d_expand, w1_ref[...])
            return carry

        lax.fori_loop(0, n[0], one, 0)

        @pl.when(step == steps - 1)
        def _():
            out = pltpu.make_async_copy(dsp, dsp_ref, sem)
            out.start()
            out.wait()

        if flat is None:
            out1_ref[...] = a1[odd].astype(BF16)
            out2_ref[...] = a2[...].astype(BF16)
            return
        stage1, stage2, sems1, sems2, sems3 = rest

        def first_copies(at):
            out = []
            for index, (k, _, rows, start) in enumerate(flat.pieces[0]):
                place = pl.multiple_of(start + at * 2 * rows, 16)
                out.append((k, stage1.at[index, pl.ds(0, 2 * rows), :], place, 2 * rows))
            return out

        def second_copies(at):
            out = []
            for k, row, rows, start, height in flat.within(1, at * block, block):
                for c in range(blocks):
                    source = block_of(stage2, row - at * block, rows, c)
                    out.append((k, source, start + c * height, rows))
            return out

        def pool_copies():
            out = []
            for k, row, rows, start in flat.pieces[2]:
                for c in range(flat.shapes[2][1] // BLOCK):
                    out.append((k, block_of(pool_ref, row, rows, c), start + c * rows, rows))
            return out

        def firsts(now, action):
            copy_out(n[1], out1_ref, out2_ref, first_copies(now), sems1, action)

        def seconds(now, action):
            for static in range(steps):

                @pl.when(now == static)
                def _(static=static):
                    copy_out(n[1], out1_ref, out2_ref, second_copies(static), sems2, action)

        @pl.when(step == 0)
        def _():
            copy_out(n[1], out1_ref, out2_ref, pool_copies(), sems3, "start")

        @pl.when(step > 0)
        def _():
            seconds(step - 1, "wait")

        stage2[...] = a2[...].astype(BF16)
        seconds(step, "start")

        @pl.when(odd == 1)
        def _():
            pair = step // 2

            @pl.when(pair > 0)
            def _():
                firsts(pair - 1, "wait")

            for index, (_, row, rows, _) in enumerate(flat.pieces[0]):
                both = jnp.concatenate([a1[0, row : row + rows], a1[1, row : row + rows]], axis=0)
                stage1[index, 0 : 2 * rows, :] = both.astype(BF16)
            firsts(pair, "start")

        @pl.when(step == steps - 1)
        def _():
            seconds(step, "wait")
            firsts(step // 2, "wait")
            copy_out(n[1], out1_ref, out2_ref, pool_copies(), sems3, "wait")

    by_col = pl.BlockSpec((channels, block), lambda j, n: (0, j))
    by_row = pl.BlockSpec((block, channels), lambda j, n: (j, 0))
    by_hidden = pl.BlockSpec((slots, cells, block), lambda j, n: (0, 0, j))
    anywhere = pl.BlockSpec(memory_space=pl.ANY)
    wide = (slots, cells, channels)
    scratch = [
        pltpu.VMEM((2, channels, block), F32),
        pltpu.VMEM((block, channels), F32),
        pltpu.VMEM(wide, F32),
        pltpu.SemaphoreType.DMA,
    ]
    if flat is None:
        grads = [(w_pw1.shape, BF16, by_col), (w_pw2.shape, BF16, by_row)]
    else:
        grads = halves(flat)
        most = max(len(flat.within(1, at * block, block)) for at in range(steps))
        tall = max(rows for _, _, rows, _ in flat.pieces[0])
        scratch += [
            pltpu.VMEM((len(flat.pieces[0]), 2 * tall, BLOCK), BF16),
            pltpu.VMEM((block, channels), BF16),
            pltpu.SemaphoreType.DMA((len(flat.pieces[0]),)),
            pltpu.SemaphoreType.DMA((most * blocks,)),
            copy_semaphores(flat, 2),
        ]
    return run(
        "conv_mlp_back",
        body,
        (steps,),
        live,
        (spatial_flip, act, slope, d_branch, w_pw1, w_pw2, grad_pool),
        [whole(*spatial_flip.shape), by_hidden, by_hidden, whole(*wide), by_col, by_row, anywhere],
        [(wide, F32, anywhere)] + grads,
        scratch,
        flops=8 * slots * cells * channels * hidden,
    )


def conv_norm_back(live, d_spatial, unit_values, inverse, gains):
    slots, cells, channels = d_spatial.shape

    def body(n, e_ref, u_ref, inv_ref, g_ref, out_ref, sums_ref):
        at = pl.program_id(0)

        @pl.when(at == 0)
        def _():
            sums_ref[...] = jnp.zeros(sums_ref.shape, F32)

        @pl.when(at < n[0])
        def _():
            def part(rows):
                e = e_ref[0, rows, :]
                value = u_ref[0, rows, :].astype(F32)
                sums_ref[0:1, :] += col_sum(e * value)
                sums_ref[1:2, :] += col_sum(e)
                grad = unit_back(value, inv_ref[0, rows, :], e * g_ref[0:1, :])
                sums_ref[2:3, :] += col_sum(grad)
                out_ref[0, rows, :] = grad.astype(BF16)

            over_rows(cells, part)

    one = slot(cells, channels)
    return run(
        "conv_norm_back",
        body,
        (slots,),
        live,
        (d_spatial, unit_values, inverse, gains),
        [one, one, slot(cells, 1), whole(*gains.shape)],
        [(d_spatial.shape, BF16, one), ((8, channels), F32, result(8, channels))],
    )


def conv_back(live, top, high, bottom, d_top, d_mid, d_bottom, d_post, kernel, after):
    slots, rows, cols, channels = high.shape

    def body(
        n, top_ref, mid_ref, bottom_ref, dt_ref, dm_ref, db_ref, dpost_ref, k_ref,
        out_ref, gk_ref, frame, d_frame,
    ):
        at = pl.program_id(0)

        @pl.when(at == 0)
        def _():
            gk_ref[...] = jnp.zeros(gk_ref.shape, F32)

        @pl.when(at < n[0])
        def _():
            frame[...] = jnp.zeros(frame.shape, F32)
            d_frame[...] = jnp.zeros(d_frame.shape, F32)

            def tile(tile_at, carry):
                lanes = lane_tile(tile_at)
                stage_rows(frame, top_ref, mid_ref, bottom_ref, lanes)
                stage_rows(d_frame, dt_ref, dm_ref, db_ref, lanes)

                def emit(y, total):
                    grad = total + dpost_ref[0, y, :, lanes].astype(F32)
                    out_ref[0, y, :, lanes] = grad.astype(BF16)

                depthwise_rows(d_frame, rows, cols, lambda t: k_ref[t : t + 1, lanes], True, emit)
                for left in range(KS):
                    totals = [None] * KS
                    grads = {}
                    for y in range(rows + 2 * REACH):
                        begin = EDGE - REACH + left
                        shifted = frame[y, begin : begin + cols, :].reshape(cols // 8, 8, LANES)
                        if y < rows:
                            grads[y] = d_frame[y + REACH, EDGE : EDGE + cols, :].reshape(
                                cols // 8, 8, LANES
                            )
                        for tap_row in range(KS):
                            row = y - tap_row
                            if 0 <= row < rows:
                                term = jnp.sum(shifted * grads[row], axis=0)
                                old = totals[tap_row]
                                totals[tap_row] = term if old is None else old + term
                        grads.pop(y - KS + 1, None)
                    for tap_row in range(KS):
                        tap = tap_row * KS + left
                        gk_ref[tap : tap + 1, lanes] += col_sum(totals[tap_row])
                return carry

            lax.fori_loop(0, channels // LANES, tile, 0)

        @pl.when(at >= n[0])
        def _():
            out_ref[...] = jnp.zeros(out_ref.shape, BF16)

    halo = slot(REACH, cols, channels)
    one = slot(rows, cols, channels)
    frame_shape = (rows + 2 * REACH, cols + 2 * EDGE, LANES)
    return run(
        "conv_back",
        body,
        (slots,),
        live,
        (top, high, bottom, d_top, d_mid, d_bottom, d_post, kernel),
        [halo, one, halo, halo, one, halo, one, whole(*kernel.shape)],
        [
            (high.shape, BF16, every_slot(rows, cols, channels)),
            ((64, channels), F32, result(64, channels)),
        ],
        [pltpu.VMEM(frame_shape, F32), pltpu.VMEM(frame_shape, F32)],
        flops=4 * slots * rows * cols * channels * KS * KS * 40,
        after=after,
    )


def from_both_sides(head, tail):
    count = lax.axis_size("strip")
    before = lax.ppermute(tail, "strip", [(i, i + 1) for i in range(count - 1)])
    after = lax.ppermute(head, "strip", [(i + 1, i) for i in range(count - 1)])
    return before, after


def bin_weights(edges, cell_count):
    cells = jnp.arange(cell_count, dtype=jnp.int32)
    inside = (cells[None, :] >= edges[:-1, None]) & (cells[None, :] < edges[1:, None])
    widths = (edges[1:] - edges[:-1]).astype(F32)
    return inside.astype(F32) / widths[:, None]


def strip_bins(edges, first_bin, bin_count, first_cell, cell_count):
    padded = jnp.concatenate([edges[:1], edges, edges[-1:]])
    window = lax.dynamic_slice_in_dim(padded, first_bin + 1, bin_count + 1)
    cells = first_cell + jnp.arange(cell_count, dtype=jnp.int32)
    inside = (cells[None, :] >= window[:-1, None]) & (cells[None, :] < window[1:, None])
    widths = jnp.maximum(window[1:] - window[:-1], 1).astype(F32)
    return inside.astype(F32) / widths[:, None]


def bit_of(axis, bit):
    return (lax.axis_index(axis) >> bit) & 1


def swap_halves(cells, axis, bit, own):
    size = lax.axis_size(axis)
    keep = lax.dynamic_index_in_dim(cells, own, 1, keepdims=False)
    send = lax.dynamic_index_in_dim(cells, 1 - own, 1, keepdims=False)
    got = lax.ppermute(send, axis, [(i, i ^ (1 << bit)) for i in range(size)])
    return (keep.astype(F32) + got.astype(F32)).astype(BF16)


def bits(axis):
    return int(math.log2(lax.axis_size(axis)))


def halve_dp(cells, base, bit):
    if cells.shape[0] % 2:
        cells = jnp.pad(cells, [(0, 1)] + [(0, 0)] * (cells.ndim - 1))
    own = (bit_of("dp", bit) - base) & 1
    cells = cells.reshape((cells.shape[0] // 2, 2) + cells.shape[1:])
    return swap_halves(cells, "dp", bit, own), (base + own) >> 1


def halve_strip(cells):
    for bit in range(bits("strip")):
        m, count = cells.shape[:2]
        cells = cells.reshape((m * count // 2, 2) + cells.shape[2:])
        cells = swap_halves(cells, "strip", bit, bit_of("strip", bit))
        cells = cells.reshape((m, count // 2) + cells.shape[1:])
    return cells


def shared_sum(matrix, offset, chunk, strip_first):
    strips = lax.axis_size("strip")
    rows, cols = matrix.shape
    chunk_rows = chunk // cols
    base = offset // (chunk * strips)
    front = (offset - base * chunk * strips) // cols
    groups = -(-(front + rows) // (chunk_rows * strips))
    back = groups * chunk_rows * strips - front - rows
    cells = jnp.pad(matrix, ((front, back), (0, 0))).reshape(groups, strips, chunk_rows, cols)
    cells, base = halve_dp(cells, base, 0)
    if strip_first:
        cells = halve_strip(cells)
        cells, base = halve_dp(cells, base, 1)
    else:
        cells, base = halve_dp(cells, base, 1)
        cells = halve_strip(cells)
    return cells.reshape(cells.shape[0], chunk), base


def owned_chunk(matrices, extras):
    data_count = lax.axis_size("dp")
    strips = lax.axis_size("strip")
    devices = data_count * strips
    chunk = sum(m.size for m in matrices) // devices
    span = data_count // 4
    placed = None
    offset = 0
    for order, matrix in enumerate(matrices):
        part, base = shared_sum(matrix, offset, chunk, order % 2 == 0)
        canvas = jnp.zeros((span + part.shape[0], chunk), BF16)
        canvas = lax.dynamic_update_slice(canvas, part, (base, 0))[:span]
        placed = canvas if placed is None else placed + canvas
        offset += matrix.size
    for bit in range(2, bits("dp")):
        placed = placed.reshape(placed.shape[0] // 2, 2, chunk)
        placed = swap_halves(placed, "dp", bit, bit_of("dp", bit))
    return share_of(placed.reshape(chunk).astype(F32), chunk, extras)


STEPS = {
    "core": ("dp", 1, lambda dp, strip: dp & 1),
    "x": ("strip", 1, lambda dp, strip: strip & 1),
    "y": ("dp", 2, lambda dp, strip: (dp >> 1) & 1),
    "z": ("dp", 4, lambda dp, strip: ((dp >> 2) ^ (dp >> 3)) & 1),
    "far": ("dp", 12, lambda dp, strip: (dp >> 3) & 1),
}
ORDERS = (("x", "y", "z", "far"), ("y", "z", "x", "far"), ("z", "x", "y", "far"))


def across(step, value):
    axis, flip_bits, _ = STEPS[step]
    return lax.ppermute(value, axis, [(i, i ^ flip_bits) for i in range(lax.axis_size(axis))])


def split_sum(flat, kept, arrived, level, after):
    parts = len(ORDERS)
    rows = flat.units // parts
    count = HALF_CHUNKS >> (level + 1)
    own = [STEPS[order[level]][2](lax.axis_index("dp"), lax.axis_index("strip")) for order in ORDERS]
    bits = jnp.stack(own).astype(jnp.int32)
    specs, args = [], []
    for part, order in enumerate(ORDERS):
        left = [name for name in ("far", "z", "y", "x") if name not in order[:level]]
        low = len(left) - 1 - left.index(order[level])

        for flipped in (0, 1):

            def place(i, bit, part=part, low=low, flipped=flipped):
                mine = bit[part] ^ flipped
                index = ((i >> low) << (low + 1)) | (mine << low) | (i & ((1 << low) - 1))
                return index, part if level == 0 else 0, 0

            for source in (kept, arrived):
                args.append(source[0 if level == 0 else part])
                specs.append(pl.BlockSpec((1, rows, BLOCK), place))

    def body(_, *refs):
        ins, outs = refs[: 4 * parts], refs[4 * parts :]
        for at in range(2 * parts):
            total = ins[2 * at][...].astype(F32) + ins[2 * at + 1][...].astype(F32)
            outs[at][...] = total.astype(BF16)

    out = pl.BlockSpec((1, rows, BLOCK), lambda i, bit: (i, 0, 0))
    done = run(
        "split_sum",
        body,
        (count,),
        bits,
        tuple(args),
        specs,
        [((count, rows, BLOCK), BF16, out)] * (2 * parts),
        after=after,
    )
    return done[0::2], done[1::2]


def sent(sends, level):
    return [across(order[level], value) for order, value in zip(ORDERS, sends)]


def last_sum(kept, arrived):
    parts = [(k.astype(F32) + a.astype(F32))[0] for k, a in zip(kept, arrived)]
    return jnp.concatenate(parts, axis=0)


def row_major(flat, units):
    devices = lax.axis_size("dp") * lax.axis_size("strip")
    index = lax.axis_index("dp") * lax.axis_size("strip") + lax.axis_index("strip")
    kinds, kind_of = [], []
    for k in range(devices):
        kind = []
        for matrix, pieces in enumerate(flat.pieces):
            for chunk, _, rows, start in pieces:
                if chunk == k:
                    kind.append((start, rows, flat.shapes[matrix][1] // BLOCK))
        kind = tuple(kind)
        if kind not in kinds:
            kinds.append(kind)
        kind_of.append(kinds.index(kind))

    def ordered(kind):
        def branch(value):
            out = []
            for start, rows, blocks in kind:
                piece = value[start : start + rows * blocks].reshape(blocks, rows, BLOCK)
                out.append(piece.transpose(1, 0, 2).reshape(-1))
            return jnp.concatenate(out)

        return branch

    which = jnp.asarray(kind_of, jnp.int32)[index]
    return lax.switch(which, [ordered(kind) for kind in kinds], units)


def share_of(mine, chunk, extras):
    data_count = lax.axis_size("dp")
    strips = lax.axis_size("strip")
    devices = data_count * strips
    extra = extras.shape[0] // devices
    index = lax.axis_index("dp") * strips + lax.axis_index("strip")
    pieces = [mine]
    left = extras.shape[0]
    padded = jnp.pad(extras, (0, chunk))
    for hop in range(1, -(-left // chunk) + 1):
        size = min(left, chunk)
        left -= size
        following = lax.ppermute(
            mine[:size].astype(BF16),
            ("dp", "strip"),
            [(i + hop, i) for i in range(devices - hop)],
        ).astype(F32)
        past = index + hop - devices
        own_extras = lax.dynamic_slice(padded, (jnp.maximum(past, 0) * chunk,), (size,))
        pieces.append(jnp.where(past >= 0, own_extras, following))
    return lax.dynamic_slice(jnp.concatenate(pieces), (index * extra,), (chunk + extra,))


def per_device(
    low_tokens,
    high_map,
    counts,
    row_edges,
    col_edges,
    w_qkv,
    w_attn_out,
    w_fc1,
    w_fc2,
    vit_gains,
    vit_shifts,
    w_pw1,
    w_pw2,
    w_pool,
    dw_kernel,
    conv_gains,
    conv_shifts,
    w_gate,
    d_merged,
    d_conv,
):
    slots, tok_rows, width = low_tokens.shape
    rows, cols, channels = high_map.shape[1:]
    cells = rows * cols
    strips = lax.axis_size("strip")
    strip = lax.axis_index("strip")
    live = jnp.stack([counts[0], lax.axis_index("dp") & 1]).astype(jnp.int32)

    col_bins = bin_weights(col_edges, cols)
    side = col_bins.shape[0]
    own_bins = tok_rows // side
    near_bins = strip_bins(row_edges, strip * own_bins - 1, own_bins + 2, strip * rows, rows)
    bins = (near_bins[:, None, :, None] * col_bins[None, :, None, :]).astype(BF16)
    bins = bins.reshape((own_bins + 2) * side, cells)

    def shifted(value, by):
        return lax.ppermute(value, "strip", [(i, (i + by) % strips) for i in range(strips)])

    tok_all = jnp.concatenate(
        [low_tokens] + [shifted(low_tokens, by) for by in range(1, strips)], axis=1
    )
    top, bottom = from_both_sides(high_map[:, :REACH], high_map[:, -REACH:])

    data_count = lax.axis_size("dp")
    devices = data_count * strips
    vit_flat = Flat([w.shape for w in (w_qkv, w_attn_out, w_fc1, w_fc2)], devices)
    conv_flat = Flat([w.shape for w in (w_pw1, w_pw2, w_pool)], devices)
    chunked = devices == 2 * HALF_CHUNKS and strips == 2 and vit_flat.even and conv_flat.even
    if not chunked:
        vit_flat = conv_flat = None

    spatial, spatial_flip, conv_unit, conv_inverse = conv_front(
        live, top, high_map, bottom, dw_kernel, conv_gains, conv_shifts
    )
    act, slope, branch, high_out = conv_mlp(
        live, spatial, high_map.reshape(slots, cells, channels), w_pw1, w_pw2, conv_gains
    )
    own, before_part, after_part = pool(live, high_out, bins, side)
    first, last = from_both_sides(before_part, after_part)
    normed, q, kv, probs, mixed, residual, inner, inner_flip = vit_front(
        live, tok_all, w_qkv, w_attn_out, vit_gains, vit_shifts, tok_rows, (own,)
    )
    lift, d_pooled, grad_pool, gate_sums = adapter(
        live, own, first, last, d_merged, w_pool, w_gate.reshape(1, channels), (inner,)
    )
    near_before, near_after = from_both_sides(d_pooled[:, :side], d_pooled[:, -side:])
    d_post, d_branch, scale_sums = unpool(
        live,
        jnp.concatenate([near_before, d_pooled, near_after], axis=1),
        bins.T,
        d_conv.reshape(slots, cells, channels),
        branch,
        conv_gains,
    )
    d_spatial, *conv_grads = conv_mlp_back(
        live, spatial_flip, act, slope, d_branch, w_pw1, w_pw2, grad_pool, conv_flat
    )
    d_conv_in, norm_sums = conv_norm_back(live, d_spatial, conv_unit, conv_inverse, conv_gains)
    d_conv_in = d_conv_in.reshape(high_map.shape)
    d_before, d_after = from_both_sides(d_conv_in[:, :REACH], d_conv_in[:, -REACH:])

    merged, d_inner, *vit_grads = vit_mlp(
        live, inner, inner_flip, d_merged, residual, lift, w_fc1, w_fc2, vit_flat, (d_conv_in,)
    )
    order = (d_inner,)
    if chunked:
        kept, sends = split_sum(
            conv_flat, conv_grads[:1], [across("core", conv_grads[1])], 0, order
        )
        arrived = sent(sends, 0)
        order = (sends[0],)
    d_residual, d_mixed, inner_sums, *vit_grads_out = vit_back(
        live, residual, d_inner, d_merged, mixed, w_attn_out, vit_gains, vit_flat,
        tuple(vit_grads), order,
    )
    d_q, d_k, d_v = attention_back(live, probs, q, kv, d_mixed)
    d_normed, *vit_grads_qkv = qkv_back(
        live, normed, d_q, d_k, d_v, w_qkv, vit_flat, tuple(vit_grads_out)
    )
    d_other = jnp.zeros(low_tokens.shape, BF16)
    for by in range(1, strips):
        part = d_normed[:, by * tok_rows : (by + 1) * tok_rows].astype(BF16)
        d_other = d_other + shifted(part, -by) if by > 1 else shifted(part, -by)
    order = (d_normed,)
    if chunked:
        kept, sends = split_sum(conv_flat, kept, arrived, 1, order)
        arrived = sent(sends, 1)
        vit_arrived = across("core", vit_grads_qkv[1])
        order = (sends[0],)
    grad_map, kernel_sums = conv_back(
        live,
        top,
        high_map,
        bottom,
        d_before,
        d_conv_in,
        d_after,
        d_post.reshape(high_map.shape),
        dw_kernel,
        order,
    )
    order = (grad_map,)
    if chunked:
        kept, sends = split_sum(conv_flat, kept, arrived, 2, order)
        arrived = sent(sends, 2)
        vit_kept, vit_sends = split_sum(vit_flat, vit_grads_qkv[:1], [vit_arrived], 0, (sends[0],))
        vit_arrived = sent(vit_sends, 0)
        order = (vit_sends[0],)
    grad_tokens, token_sums = tokens_back(
        live, low_tokens, d_normed, d_other, d_residual, vit_gains, order
    )

    vit_extras = jnp.concatenate([token_sums[0], inner_sums[0], token_sums[1], inner_sums[1]])
    conv_extras = jnp.concatenate(
        [
            kernel_sums[: KS * KS].reshape(-1),
            norm_sums[0],
            scale_sums[0],
            norm_sums[2],
            norm_sums[1],
            gate_sums[0],
        ]
    )
    extras = lax.psum(jnp.concatenate([vit_extras, conv_extras]), ("dp", "strip"))
    vit_extras, conv_extras = extras[: vit_extras.shape[0]], extras[vit_extras.shape[0] :]
    if chunked:
        kept, sends = split_sum(conv_flat, kept, arrived, 3, (grad_tokens,))
        arrived = sent(sends, 3)
        vit_kept, vit_sends = split_sum(vit_flat, vit_kept, vit_arrived, 1, (sends[0],))
        vit_arrived = sent(vit_sends, 1)
        conv_mine = row_major(conv_flat, last_sum(kept, arrived))
        conv_out = share_of(conv_mine, conv_flat.chunk, conv_extras)
        for level in (2, 3):
            vit_kept, vit_sends = split_sum(vit_flat, vit_kept, vit_arrived, level, ())
            vit_arrived = sent(vit_sends, level)
        vit_mine = row_major(vit_flat, last_sum(vit_kept, vit_arrived))
        vit_out = share_of(vit_mine, vit_flat.chunk, vit_extras)
    else:
        vit_out = owned_chunk(vit_grads_qkv + vit_grads_out + vit_grads, vit_extras)
        conv_out = owned_chunk(conv_grads + [grad_pool], conv_extras)
    return (
        merged,
        high_out.reshape(high_map.shape),
        grad_tokens,
        grad_map,
        vit_out,
        conv_out,
    )


def solution(mesh):
    images = P("dp", "strip", None)
    maps = P("dp", "strip", None, None)
    flat = P(("dp", "strip"))
    in_specs = (images, maps, P("dp")) + (P(),) * 15 + (images, maps)
    out_specs = (images, maps, images, maps, flat, flat)
    return jax.shard_map(
        per_device, mesh=mesh, in_specs=in_specs, out_specs=out_specs, check_vma=False
    )
```

```python
import math

import jax
import jax.numpy as jnp
from jax import lax
from jax.experimental import pallas as pl
from jax.experimental.pallas import tpu as pltpu
from jax.sharding import PartitionSpec as P

HEADS = 16
KS = 7
REACH = KS // 2
EPSILON = 1e-05
LANES = 128
EDGE = 8
BLOCK = 256
HALF_CHUNKS = 16
F32 = jnp.float32
BF16 = jnp.bfloat16
VMEM_BYTES = 60 * 1024 * 1024


def dot_nn(a, b):
    return jnp.dot(a, b, preferred_element_type=F32)


def dot_nt(a, b):
    return lax.dot_general(a, b, (((1,), (1,)), ((), ())), preferred_element_type=F32)


def dot_tn(a, b):
    return lax.dot_general(a, b, (((0,), (0,)), ((), ())), preferred_element_type=F32)


def flip(value):
    return value.astype(F32).T.astype(BF16)


def row_step(rows):
    for step in (128, 96, 64, 48, 32, 16):
        if rows % step == 0:
            return step
    return rows


def over_rows(rows, body):
    step = row_step(rows)

    def one(at, carry):
        body(pl.ds(pl.multiple_of(at * step, step), step))
        return carry

    if step == rows:
        body(pl.ds(0, rows))
    else:
        lax.fori_loop(0, rows // step, one, 0)


def lane_tile(at):
    return pl.ds(pl.multiple_of(at * LANES, LANES), LANES)


def unit(values):
    center = values - jnp.mean(values, axis=-1, keepdims=True)
    inverse = lax.rsqrt(jnp.mean(center * center, axis=-1, keepdims=True) + EPSILON)
    return center * inverse, inverse


def unit_back(unit_values, inverse, grad):
    return (
        grad
        - jnp.mean(grad, axis=-1, keepdims=True)
        - unit_values * jnp.mean(grad * unit_values, axis=-1, keepdims=True)
    ) * inverse


def gelu_pair(x):
    scale = math.sqrt(2.0 / math.pi)
    square = x * x
    bend = jnp.tanh(x * (scale + (scale * 0.044715) * square))
    half = 0.5 + 0.5 * bend
    slope = half + (0.5 * x) * (1.0 - bend * bend) * (scale + (3.0 * scale * 0.044715) * square)
    return x * half, slope


def col_sum(values):
    return jnp.sum(values, axis=0, keepdims=True)


def held(at, live):
    return jnp.maximum(jnp.minimum(at, live[0] - 1), 0)


def slot(*shape):
    return pl.BlockSpec(
        (1,) + shape, lambda *g: (held(g[0], g[-1]),) + (0,) * len(shape)
    )


def every_slot(*shape):
    return pl.BlockSpec((1,) + shape, lambda *g: (g[0],) + (0,) * len(shape))


def whole(*shape):
    return pl.BlockSpec(shape, lambda *g: (0,) * len(shape), pipeline_mode=pl.Buffered(1))


def result(*shape):
    return pl.BlockSpec(shape, lambda *g: (0,) * len(shape))


def run(name, body, grid, live, args, in_specs, outs, scratch=(), after=(), alias=()):
    out_shape = [jax.ShapeDtypeStruct(shape, dtype) for shape, dtype, _ in outs]
    count = 1 + len(args)

    def without_order(*refs):
        body(*refs[:count], *refs[count + len(after) :])

    return pl.pallas_call(
        without_order,
        grid_spec=pltpu.PrefetchScalarGridSpec(
            num_scalar_prefetch=1,
            grid=grid,
            in_specs=list(in_specs) + [pl.BlockSpec(memory_space=pl.ANY)] * len(after),
            out_specs=[spec for _, _, spec in outs],
            scratch_shapes=list(scratch),
        ),
        out_shape=out_shape,
        input_output_aliases={1 + given: out for given, out in alias},
        compiler_params=pltpu.CompilerParams(
            dimension_semantics=("arbitrary",) * len(grid), vmem_limit_bytes=VMEM_BYTES
        ),
        cost_estimate=pl.CostEstimate(flops=0, bytes_accessed=0, transcendentals=0),
        name=name,
    )(live, *args, *after)


class Flat:
    def __init__(self, shapes, devices):
        self.shapes = shapes
        self.chunk = sum(r * c for r, c in shapes) // devices
        self.units = self.chunk // BLOCK
        self.pieces = []
        self.even = sum(r * c for r, c in shapes) % (devices * BLOCK * 3 * 16) == 0
        offset = 0
        for rows, cols in shapes:
            self.even &= self.chunk % cols == 0 and offset % cols == 0 and cols % BLOCK == 0
            found = []
            if self.even:
                height, begin = self.chunk // cols, offset // cols
                for k in range(devices):
                    low = max(k * height, begin)
                    high = min((k + 1) * height, begin + rows)
                    if low < high:
                        start = (low - k * height) * (cols // BLOCK)
                        found.append((k, low - begin, high - low, start))
                        self.even &= (high - low) % 8 == 0 and start % 16 == 0
            self.pieces.append(found)
            offset += rows * cols

    def within(self, matrix, first, count):
        out = []
        for k, row, height, start in self.pieces[matrix]:
            low, high = max(row, first), min(row + height, first + count)
            if low < high:
                out.append((k, low, high - low, start + low - row, height))
        return out


def side_of(chunk):
    z1, z0, y = (chunk >> 4) & 1, (chunk >> 3) & 1, (chunk >> 2) & 1
    return (chunk >> 1) & 1, z1 * 8 + (z0 ^ z1) * 4 + y * 2 + (chunk & 1)


def copy_out(own_core, keep_ref, send_ref, copies, sems, action):
    for at, (chunk, source, place, rows) in enumerate(copies):
        core, index = side_of(chunk)
        for held_here, ref in ((True, keep_ref), (False, send_ref)):

            @pl.when((own_core == core) == held_here)
            def _(ref=ref, at=at, source=source, place=place, rows=rows, index=index):
                target = ref.at[index, pl.ds(place, rows), :]
                getattr(pltpu.make_async_copy(source, target, sems.at[at]), action)()


def copy_all(own_core, keep_ref, send_ref, stage, flat, matrix, sems):
    copies = []
    for k, row, rows, start in flat.pieces[matrix]:
        for c in range(stage.shape[1] // BLOCK):
            copies.append((k, block_of(stage, row, rows, c), start + c * rows, rows))
    copy_out(own_core, keep_ref, send_ref, copies, sems, "start")
    copy_out(own_core, keep_ref, send_ref, copies, sems, "wait")


def copy_semaphores(flat, matrix):
    return pltpu.SemaphoreType.DMA((len(flat.pieces[matrix]) * flat.shapes[matrix][1] // BLOCK,))


def halves(flat):
    shape = (HALF_CHUNKS, flat.units, BLOCK)
    spec = pl.BlockSpec(memory_space=pl.ANY)
    return [(shape, BF16, spec), (shape, BF16, spec)]


def block_of(ref, first, rows, block):
    return ref.at[pl.ds(first, rows), pl.ds(block * BLOCK, BLOCK)]


def vit_front(live, tok_all, w_qkv, w_out, gains, shifts, tok_rows, after):
    slots, key_rows, width = tok_all.shape
    head = width // HEADS
    pairs = width // LANES
    per_tile = LANES // head

    def body(
        n, x_ref, wq_ref, wo_ref, g_ref, b_ref,
        normed_ref, q_ref, kv_ref, probs_ref, mixed_ref, res_ref, inner_ref, flip_ref,
    ):
        @pl.when(pl.program_id(0) < n[0])
        def _():
            def first_norm(rows):
                value, _ = unit(x_ref[0, rows, :].astype(F32))
                normed_ref[0, rows, :] = (value * g_ref[0:1, :] + b_ref[0:1, :]).astype(BF16)

            over_rows(key_rows, first_norm)
            q_ref[0] = dot_nn(normed_ref[0, 0:tok_rows, :], wq_ref[:, 0:width]).astype(BF16)
            for part in range(4):
                cols = slice(part * width // 2, (part + 1) * width // 2)
                w_cols = slice(width + cols.start, width + cols.stop)
                kv_ref[0, :, cols] = dot_nn(normed_ref[0], wq_ref[:, w_cols]).astype(BF16)

            lane = lax.broadcasted_iota(jnp.int32, (1, LANES), 1) // head

            def heads(pair, carry):
                q = q_ref[0, :, lane_tile(pair)] * jnp.asarray(1.0 / math.sqrt(head), BF16)
                k = kv_ref[0, :, lane_tile(pair)].astype(F32)
                v_flip = flip(kv_ref[0, :, lane_tile(pairs + pair)])
                mixed = []
                for h in range(per_tile):
                    scores = dot_nt(jnp.where(lane == h, k, 0.0).astype(BF16), q)
                    top = jnp.max(scores, axis=0, keepdims=True)
                    raised = jnp.exp(scores - top)
                    probs = (raised * (1.0 / col_sum(raised))).astype(BF16)
                    probs_ref[0, pair * per_tile + h] = probs
                    mixed.append(dot_nn(v_flip[h * head : (h + 1) * head, :], probs))
                mixed_ref[0, :, lane_tile(pair)] = jnp.concatenate(mixed, axis=0).T.astype(BF16)
                return carry

            lax.fori_loop(0, pairs, heads, 0)
            res_ref[0] = dot_nn(mixed_ref[0], wo_ref[...])

            def second_norm(rows):
                res = res_ref[0, rows, :] + x_ref[0, rows, :].astype(F32)
                res_ref[0, rows, :] = res
                value, _ = unit(res)
                inner_ref[0, rows, :] = (value * g_ref[1:2, :] + b_ref[1:2, :]).astype(BF16)

            over_rows(tok_rows, second_norm)
            flip_ref[0] = flip(inner_ref[0])

    return run(
        "vit_front",
        body,
        (slots,),
        live,
        (tok_all, w_qkv, w_out, gains, shifts),
        [slot(key_rows, width), whole(*w_qkv.shape), whole(*w_out.shape)]
        + [whole(*gains.shape), whole(*shifts.shape)],
        [
            ((slots, key_rows, width), BF16, slot(key_rows, width)),
            ((slots, tok_rows, width), BF16, slot(tok_rows, width)),
            ((slots, key_rows, 2 * width), BF16, slot(key_rows, 2 * width)),
            ((slots, HEADS, key_rows, tok_rows), BF16, slot(HEADS, key_rows, tok_rows)),
            ((slots, tok_rows, width), BF16, slot(tok_rows, width)),
            ((slots, tok_rows, width), F32, slot(tok_rows, width)),
            ((slots, tok_rows, width), BF16, slot(tok_rows, width)),
            ((slots, width, tok_rows), BF16, slot(width, tok_rows)),
        ],
        after=after,
    )


def vit_mlp(live, inner, inner_flip, d_mlp, residual, lift, w_fc1, w_fc2, flat, after):
    slots, tok_rows, width = inner.shape
    hidden = w_fc1.shape[1]
    block = 512
    steps = hidden // block
    blocks = width // BLOCK

    def body(
        n, x_ref, xt_ref, dm_ref, res_ref, lift_ref, w1_ref, w2_ref,
        merged_ref, din_ref, out1_ref, out2_ref, low, a1, a2, *rest,
    ):
        step = pl.program_id(0)

        @pl.when(step == 0)
        def _():
            low[...] = res_ref[...]
            din_ref[...] = jnp.zeros(din_ref.shape, F32)

        a1[...] = jnp.zeros(a1.shape, F32)
        a2[...] = jnp.zeros(a2.shape, F32)

        def one(at, carry):
            before = dot_nn(x_ref[at], w1_ref[...])
            d_act = dot_nt(dm_ref[at], w2_ref[...])
            act, slope = gelu_pair(before)
            act = act.astype(BF16)
            d_fc = (slope * d_act).astype(BF16)
            low[at] += dot_nn(act, w2_ref[...])
            a2[...] += dot_tn(act, dm_ref[at])
            a1[...] += dot_nn(xt_ref[at], d_fc)
            din_ref[at] += dot_nt(d_fc, w1_ref[...])
            return carry

        lax.fori_loop(0, n[0], one, 0)

        @pl.when(step == steps - 1)
        def _():
            def close(at, carry):
                merged_ref[at] = (low[at] + lift_ref[at]).astype(BF16)
                return carry

            def blank(at, carry):
                merged_ref[at] = jnp.zeros(merged_ref.shape[1:], BF16)
                return carry

            lax.fori_loop(0, n[0], close, 0)
            lax.fori_loop(n[0], slots, blank, 0)

        if flat is None:
            out1_ref[...] = a1[...].astype(BF16)
            out2_ref[...] = a2[...].astype(BF16)
            return
        stage1, stage2, sems1, sems2 = rest

        def first_copies(at):
            out = []
            for c in range(block // BLOCK):
                for k, row, rows, start, height in flat.within(2, 0, width):
                    place = start + (at * (block // BLOCK) + c) * height
                    out.append((k, block_of(stage1, row, rows, c), pl.multiple_of(place, 16), rows))
            return out

        def second_copies(at):
            out = []
            for k, row, rows, start, height in flat.within(3, at * block, block):
                for c in range(blocks):
                    source = block_of(stage2, row - at * block, rows, c)
                    out.append((k, source, start + c * height, rows))
            return out

        def each(at, now, action):
            copy_out(n[1], out1_ref, out2_ref, first_copies(now), sems1, action)
            for static in range(steps):

                @pl.when(now == static)
                def _(static=static):
                    copy_out(n[1], out1_ref, out2_ref, second_copies(static), sems2, action)

        @pl.when(step > 0)
        def _():
            each(step, step - 1, "wait")

        stage1[...] = a1[...].astype(BF16)
        stage2[...] = a2[...].astype(BF16)
        each(step, step, "start")

        @pl.when(step == steps - 1)
        def _():
            each(step, step, "wait")

    wide = (slots, tok_rows, width)
    by_col = pl.BlockSpec((width, block), lambda j, n: (0, j))
    by_row = pl.BlockSpec((block, width), lambda j, n: (j, 0))
    scratch = [
        pltpu.VMEM(wide, F32),
        pltpu.VMEM((width, block), F32),
        pltpu.VMEM((block, width), F32),
    ]
    if flat is None:
        grads = [(w_fc1.shape, BF16, by_col), (w_fc2.shape, BF16, by_row)]
    else:
        grads = halves(flat)
        most = max(len(flat.within(3, at * block, block)) for at in range(steps))
        scratch += [
            pltpu.VMEM((width, block), BF16),
            pltpu.VMEM((block, width), BF16),
            pltpu.SemaphoreType.DMA((block // BLOCK * len(flat.pieces[2]),)),
            pltpu.SemaphoreType.DMA((most * blocks,)),
        ]
    return run(
        "vit_mlp",
        body,
        (steps,),
        live,
        (inner, inner_flip, d_mlp, residual, lift, w_fc1, w_fc2),
        [whole(*wide), whole(*inner_flip.shape)] + [whole(*wide)] * 3 + [by_col, by_row],
        [(wide, BF16, result(*wide)), (wide, F32, result(*wide))] + grads,
        scratch,
        after=after,
    )


def vit_back(live, residual, d_inner, d_merged, mixed, w_out, gains, flat, kept, after):
    slots, tok_rows, width = residual.shape

    def body(n, res_ref, din_ref, dm_ref, mix_ref, wo_ref, g_ref, *rest):
        if flat is None:
            dres_ref, dmix_ref, sums_ref, gout_ref, low, acc = rest
        else:
            _, _, dres_ref, dmix_ref, sums_ref, keep_ref, send_ref, low, acc, stage, sems = rest
        at = pl.program_id(0)

        @pl.when(at == 0)
        def _():
            acc[...] = jnp.zeros(acc.shape, F32)
            sums_ref[...] = jnp.zeros(sums_ref.shape, F32)

        @pl.when(at < n[0])
        def _():
            def back(rows):
                value, inverse = unit(res_ref[0, rows, :])
                e = din_ref[0, rows, :]
                sums_ref[0:1, :] += col_sum(e * value)
                sums_ref[1:2, :] += col_sum(e)
                d_res = dm_ref[0, rows, :].astype(F32) + unit_back(value, inverse, e * g_ref[1:2, :])
                dres_ref[0, rows, :] = d_res
                low[rows, :] = d_res.astype(BF16)

            over_rows(tok_rows, back)
            dmix_ref[0] = dot_nt(low[...], wo_ref[...]).astype(BF16)
            acc[...] += dot_tn(mix_ref[0], low[...])

        @pl.when(at == slots - 1)
        def _():
            if flat is None:
                gout_ref[...] = acc[...].astype(BF16)
            else:
                stage[...] = acc[...].astype(BF16)
                copy_all(n[1], keep_ref, send_ref, stage, flat, 1, sems)

    wide = (slots, tok_rows, width)
    one = slot(tok_rows, width)
    args = (residual, d_inner, d_merged, mixed, w_out, gains)
    specs = [one, one, one, one, whole(*w_out.shape), whole(*gains.shape)]
    scratch = [pltpu.VMEM((tok_rows, width), BF16), pltpu.VMEM(w_out.shape, F32)]
    grads, alias = [(w_out.shape, BF16, result(*w_out.shape))], ()
    if flat is not None:
        args, specs, grads = args + kept, specs + [pl.BlockSpec(memory_space=pl.ANY)] * 2, halves(flat)
        scratch += [pltpu.VMEM(w_out.shape, BF16), copy_semaphores(flat, 1)]
        alias = ((6, 3), (7, 4))
    return run(
        "vit_back",
        body,
        (slots,),
        live,
        args,
        specs,
        [(wide, F32, one), (wide, BF16, one), ((8, width), F32, result(8, width))] + grads,
        scratch,
        after=after,
        alias=alias,
    )


def attention_back(live, probs, q, kv, d_mixed):
    slots, _, key_rows, tok_rows = probs.shape
    width = q.shape[2]
    head = width // HEADS
    pairs = width // LANES
    per_tile = LANES // head
    scale = 1.0 / math.sqrt(head)

    def body(n, p_ref, q_ref, k_ref, v_ref, dm_ref, dq_ref, dk_ref, dv_ref):
        @pl.when(pl.program_id(0) < n[0])
        def _():
            lane = lax.broadcasted_iota(jnp.int32, (1, LANES), 1) // head
            q = q_ref[0].astype(F32) * scale
            v = v_ref[0].astype(F32)
            dm = dm_ref[0].astype(F32)
            dm_low = dm_ref[0]
            k_flip = flip(k_ref[0].astype(F32) * scale)
            d_keys = jnp.zeros((key_rows, LANES), F32)
            d_values = jnp.zeros((key_rows, LANES), F32)
            d_query = []
            for h in range(per_tile):
                own = lane == h
                probs_low = p_ref[0, h]
                d_probs = dot_nt(jnp.where(own, v, 0.0).astype(BF16), dm_low)
                d_values += dot_nn(probs_low, jnp.where(own, dm, 0.0).astype(BF16))
                wide = probs_low.astype(F32)
                d_scores = (wide * (d_probs - col_sum(wide * d_probs))).astype(BF16)
                d_keys += dot_nn(d_scores, jnp.where(own, q, 0.0).astype(BF16))
                d_query.append(dot_nn(k_flip[h * head : (h + 1) * head, :], d_scores))
            dq_ref[0] = jnp.concatenate(d_query, axis=0).T.astype(BF16)
            dk_ref[0] = d_keys.astype(BF16)
            dv_ref[0] = d_values.astype(BF16)

    def held_pair(i, p, n):
        return jnp.where(i < n[0], p, pairs - 1)

    def at_pair(rows, shift=0):
        return pl.BlockSpec(
            (1, rows, LANES), lambda i, p, n: (held(i, n), 0, held_pair(i, p, n) + shift)
        )

    own = at_pair(tok_rows)
    keys = at_pair(key_rows)
    return run(
        "attention_back",
        body,
        (slots, pairs),
        live,
        (probs, q, kv, kv, d_mixed),
        [
            pl.BlockSpec(
                (1, per_tile, key_rows, tok_rows),
                lambda i, p, n: (held(i, n), held_pair(i, p, n), 0, 0),
            ),
            own,
            keys,
            at_pair(key_rows, pairs),
            own,
        ],
        [
            (q.shape, BF16, own),
            ((slots, key_rows, width), BF16, keys),
            ((slots, key_rows, width), BF16, keys),
        ],
    )


def qkv_back(live, normed, d_q, d_k, d_v, w_qkv, flat, kept, after):
    slots, key_rows, width = normed.shape
    tok_rows = d_q.shape[1]

    def body(n, x_ref, dq_ref, dk_ref, dv_ref, w_ref, *rest):
        if flat is None:
            dn_ref, gw_ref, x_flip, acc = rest
        else:
            _, _, dn_ref, keep_ref, send_ref, x_flip, acc, stage, sems = rest
        at = pl.program_id(0)

        @pl.when(at == 0)
        def _():
            acc[...] = jnp.zeros(acc.shape, F32)

        @pl.when(at < n[0])
        def _():
            x_flip[...] = flip(x_ref[0])
            dn_ref[0] = dot_nt(dk_ref[0], w_ref[:, width : 2 * width])
            dn_ref[0] += dot_nt(dv_ref[0], w_ref[:, 2 * width :])
            dn_ref[0, 0:tok_rows, :] += dot_nt(dq_ref[0], w_ref[:, 0:width])
            acc[:, 0:width] += dot_nn(x_flip[:, 0:tok_rows], dq_ref[0])
            acc[:, width : 2 * width] += dot_nn(x_flip[...], dk_ref[0])
            acc[:, 2 * width :] += dot_nn(x_flip[...], dv_ref[0])

        @pl.when(at == slots - 1)
        def _():
            if flat is None:
                gw_ref[...] = acc[...].astype(BF16)
            else:
                stage[...] = acc[...].astype(BF16)
                copy_all(n[1], keep_ref, send_ref, stage, flat, 0, sems)

    keys = slot(key_rows, width)
    args = (normed, d_q, d_k, d_v, w_qkv)
    specs = [keys, slot(tok_rows, width), keys, keys, whole(*w_qkv.shape)]
    scratch = [pltpu.VMEM((width, key_rows), BF16), pltpu.VMEM(w_qkv.shape, F32)]
    grads, alias = [(w_qkv.shape, BF16, result(*w_qkv.shape))], ()
    if flat is not None:
        args, specs, grads = args + kept, specs + [pl.BlockSpec(memory_space=pl.ANY)] * 2, halves(flat)
        scratch += [pltpu.VMEM(w_qkv.shape, BF16), copy_semaphores(flat, 0)]
        alias = ((5, 1), (6, 2))
    return run(
        "qkv_back",
        body,
        (slots,),
        live,
        args,
        specs,
        [(normed.shape, F32, keys)] + grads,
        scratch,
        after=after,
        alias=alias,
    )


def tokens_back(live, tokens, d_norm, arrived, d_residual, gains, after):
    slots, tok_rows, width = tokens.shape

    def body(n, x_ref, dn_ref, more_ref, dres_ref, g_ref, out_ref, sums_ref):
        at = pl.program_id(0)

        @pl.when(at == 0)
        def _():
            sums_ref[...] = jnp.zeros(sums_ref.shape, F32)

        @pl.when(at < n[0])
        def _():
            def back(rows):
                value, inverse = unit(x_ref[0, rows, :].astype(F32))
                e = dn_ref[0, rows, :] + more_ref[0, rows, :].astype(F32)
                sums_ref[0:1, :] += col_sum(e * value)
                sums_ref[1:2, :] += col_sum(e)
                grad = dres_ref[0, rows, :] + unit_back(value, inverse, e * g_ref[0:1, :])
                out_ref[0, rows, :] = grad.astype(BF16)

            over_rows(tok_rows, back)

        @pl.when(at >= n[0])
        def _():
            out_ref[...] = jnp.zeros(out_ref.shape, BF16)

    one = slot(tok_rows, width)
    return run(
        "tokens_back",
        body,
        (slots,),
        live,
        (tokens, d_norm, arrived, d_residual, gains),
        [one, one, one, one, whole(*gains.shape)],
        [
            (tokens.shape, BF16, every_slot(tok_rows, width)),
            ((8, width), F32, result(8, width)),
        ],
        after=after,
    )


def stage_rows(frame, top_ref, mid_ref, bottom_ref, lanes):
    rows, cols = mid_ref.shape[1], mid_ref.shape[2]
    inside = slice(EDGE, EDGE + cols)
    frame[0:REACH, inside, :] = top_ref[0, :, :, lanes].astype(F32)
    frame[REACH : REACH + rows, inside, :] = mid_ref[0, :, :, lanes].astype(F32)
    frame[REACH + rows :, inside, :] = bottom_ref[0, :, :, lanes].astype(F32)


def depthwise_rows(frame, rows, cols, tap, flipped, emit):
    totals = {}
    for y in range(rows + 2 * REACH):
        for left in range(KS):
            shifted = frame[y, EDGE - REACH + left : EDGE - REACH + left + cols, :]
            for top in range(KS):
                out = y - top
                if 0 <= out < rows:
                    at = (KS - 1 - top) * KS + KS - 1 - left if flipped else top * KS + left
                    term = shifted * tap(at)
                    totals[out] = totals[out] + term if out in totals else term
        if y >= 2 * REACH:
            emit(y - 2 * REACH, totals.pop(y - 2 * REACH))


def conv_front(live, top, high, bottom, kernel, gains, shifts):
    slots, rows, cols, channels = high.shape
    cells = rows * cols

    def body(
        n, top_ref, mid_ref, bottom_ref, k_ref, g_ref, b_ref,
        spatial_ref, flip_ref, unit_ref, inv_ref, frame, middle,
    ):
        @pl.when(pl.program_id(0) < n[0])
        def _():
            frame[...] = jnp.zeros(frame.shape, F32)

            def tile(at, carry):
                lanes = lane_tile(at)
                stage_rows(frame, top_ref, mid_ref, bottom_ref, lanes)
                bias = b_ref[0:1, lanes]

                def emit(y, total):
                    middle[y * cols : (y + 1) * cols, lanes] = total + bias

                depthwise_rows(frame, rows, cols, lambda t: k_ref[t : t + 1, lanes], False, emit)
                return carry

            lax.fori_loop(0, channels // LANES, tile, 0)

            def norm(part):
                value, inverse = unit(middle[part, :])
                inv_ref[0, part, :] = inverse
                unit_ref[0, part, :] = value.astype(BF16)
                spatial_ref[0, part, :] = (value * g_ref[0:1, :] + b_ref[1:2, :]).astype(BF16)

            over_rows(cells, norm)
            flip_ref[0] = flip(spatial_ref[0])

    halo = slot(REACH, cols, channels)
    return run(
        "conv_front",
        body,
        (slots,),
        live,
        (top, high, bottom, kernel, gains, shifts),
        [halo, slot(rows, cols, channels), halo, whole(*kernel.shape)]
        + [whole(*gains.shape), whole(*shifts.shape)],
        [
            ((slots, cells, channels), BF16, slot(cells, channels)),
            ((slots, channels, cells), BF16, slot(channels, cells)),
            ((slots, cells, channels), BF16, slot(cells, channels)),
            ((slots, cells, 1), F32, slot(cells, 1)),
        ],
        [
            pltpu.VMEM((rows + 2 * REACH, cols + 2 * EDGE, LANES), F32),
            pltpu.VMEM((cells, channels), F32),
        ],
    )


def conv_mlp(live, spatial, high, w_pw1, w_pw2, gains):
    slots, cells, channels = spatial.shape
    hidden = w_pw1.shape[1]
    block = 1024
    steps = hidden // block

    def body(
        n, x_ref, high_ref, w1_ref, w2_ref, g_ref, act_ref, slope_ref, branch_ref, out_ref, acc
    ):
        at, step = pl.program_id(0), pl.program_id(1)

        @pl.when((at < n[0]) & (step == 0))
        def _():
            acc[...] = jnp.zeros(acc.shape, F32)

        @pl.when(at < n[0])
        def _():
            parts = [slice(0, cells // 2), slice(cells // 2, cells)]
            hidden_parts = [dot_nn(x_ref[0, rows, :], w1_ref[...]) for rows in parts]
            for rows, value in zip(parts, hidden_parts):
                act, slope = gelu_pair(value)
                act = act.astype(BF16)
                act_ref[0, rows, :] = act
                slope_ref[0, rows, :] = slope.astype(BF16)
                acc[rows, :] += dot_nn(act, w2_ref[...])

            @pl.when(step == steps - 1)
            def _():
                def close(rows):
                    branch = acc[rows, :]
                    branch_ref[0, rows, :] = branch.astype(BF16)
                    out_ref[0, rows, :] = (
                        high_ref[0, rows, :].astype(F32) + g_ref[1:2, :] * branch
                    ).astype(BF16)

                over_rows(cells, close)

        @pl.when((at >= n[0]) & (step == 0))
        def _():
            out_ref[...] = jnp.zeros(out_ref.shape, BF16)

    def held_step(i, j, n):
        return jnp.where(i < n[0], j, steps - 1)

    one = slot(cells, channels)
    hidden_block = pl.BlockSpec(
        (1, cells, block), lambda i, j, n: (held(i, n), 0, held_step(i, j, n))
    )
    return run(
        "conv_mlp",
        body,
        (slots, steps),
        live,
        (spatial, high, w_pw1, w_pw2, gains),
        [
            one,
            one,
            pl.BlockSpec((channels, block), lambda i, j, n: (0, held_step(i, j, n))),
            pl.BlockSpec((block, channels), lambda i, j, n: (held_step(i, j, n), 0)),
            whole(*gains.shape),
        ],
        [
            ((slots, cells, hidden), BF16, hidden_block),
            ((slots, cells, hidden), BF16, hidden_block),
            (spatial.shape, BF16, one),
            (spatial.shape, BF16, every_slot(cells, channels)),
        ],
        [pltpu.VMEM((cells, channels), F32)],
    )


def pool(live, high_out, bins, side):
    slots, cells, channels = high_out.shape
    tok_rows = bins.shape[0] - 2 * side

    def body(n, x_ref, p_ref, own_ref, before_ref, after_ref):
        @pl.when(pl.program_id(0) < n[0])
        def _():
            part = dot_nn(p_ref[...], x_ref[0])
            before_ref[0] = part[0:side].astype(BF16)
            own_ref[0] = part[side : side + tok_rows]
            after_ref[0] = part[side + tok_rows :].astype(BF16)

    return run(
        "pool",
        body,
        (slots,),
        live,
        (high_out, bins),
        [slot(cells, channels), whole(*bins.shape)],
        [
            ((slots, tok_rows, channels), F32, slot(tok_rows, channels)),
            ((slots, side, channels), BF16, slot(side, channels)),
            ((slots, side, channels), BF16, slot(side, channels)),
        ],
    )


def adapter(live, own, first, last, d_merged, w_pool, w_gate, after):
    slots, tok_rows, channels = own.shape
    side = first.shape[1]
    width = w_pool.shape[1]

    def body(
        n, own_ref, first_ref, last_ref, dm_ref, w_ref, gate_ref,
        lift_ref, dpool_ref, gw_ref, ggate_ref, acc,
    ):
        at = pl.program_id(0)

        @pl.when(at == 0)
        def _():
            acc[...] = jnp.zeros(acc.shape, F32)
            ggate_ref[...] = jnp.zeros(ggate_ref.shape, F32)

        @pl.when(at < n[0])
        def _():
            pooled_low = jnp.concatenate(
                [
                    own_ref[0, 0:side] + first_ref[0].astype(F32),
                    own_ref[0, side : tok_rows - side],
                    own_ref[0, tok_rows - side :] + last_ref[0].astype(F32),
                ],
                axis=0,
            ).astype(BF16)
            pooled = pooled_low.astype(F32)
            lifted = dot_nn(pooled_low, w_ref[...])
            logit = jnp.sum(pooled * gate_ref[...], axis=-1, keepdims=True)
            gate = 1.0 / (1.0 + jnp.exp(-logit))
            lift_ref[0] = gate * lifted
            d_top = dm_ref[0].astype(F32)
            d_logit = jnp.sum(d_top * lifted, axis=-1, keepdims=True) * gate * (1.0 - gate)
            d_lifted = (gate * d_top).astype(BF16)
            acc[...] += dot_tn(pooled_low, d_lifted)
            ggate_ref[0:1, :] += col_sum(d_logit * pooled)
            dpool_ref[0] = (dot_nt(d_lifted, w_ref[...]) + d_logit * gate_ref[...]).astype(BF16)

        @pl.when(at == slots - 1)
        def _():
            gw_ref[...] = acc[...].astype(BF16)

    edge = slot(side, channels)
    return run(
        "adapter",
        body,
        (slots,),
        live,
        (own, first, last, d_merged, w_pool, w_gate),
        [slot(tok_rows, channels), edge, edge, slot(tok_rows, width)]
        + [whole(*w_pool.shape), whole(*w_gate.shape)],
        [
            ((slots, tok_rows, width), F32, slot(tok_rows, width)),
            (own.shape, BF16, slot(tok_rows, channels)),
            (w_pool.shape, BF16, result(*w_pool.shape)),
            ((8, channels), F32, result(8, channels)),
        ],
        [pltpu.VMEM(w_pool.shape, F32)],
        after=after,
    )


def unpool(live, near, spread, d_conv, branch, gains):
    slots, near_rows, channels = near.shape
    cells = d_conv.shape[1]

    def body(n, near_ref, s_ref, dc_ref, branch_ref, g_ref, dpost_ref, dbranch_ref, sums_ref):
        at = pl.program_id(0)

        @pl.when(at == 0)
        def _():
            sums_ref[...] = jnp.zeros(sums_ref.shape, F32)

        @pl.when(at < n[0])
        def _():
            def part(rows):
                d_post = dc_ref[0, rows, :].astype(F32) + dot_nn(s_ref[rows, :], near_ref[0])
                sums_ref[0:1, :] += col_sum(d_post * branch_ref[0, rows, :].astype(F32))
                dpost_ref[0, rows, :] = d_post.astype(BF16)
                dbranch_ref[0, rows, :] = (g_ref[1:2, :] * d_post).astype(BF16)

            over_rows(cells, part)

    one = slot(cells, channels)
    return run(
        "unpool",
        body,
        (slots,),
        live,
        (near, spread, d_conv, branch, gains),
        [slot(near_rows, channels), whole(*spread.shape), one, one, whole(*gains.shape)],
        [
            (d_conv.shape, BF16, one),
            (d_conv.shape, BF16, one),
            ((8, channels), F32, result(8, channels)),
        ],
    )


def conv_mlp_back(live, spatial_flip, act, slope, d_branch, w_pw1, w_pw2, grad_pool, flat):
    slots, channels, cells = spatial_flip.shape
    hidden = w_pw1.shape[1]
    block = 2 * BLOCK
    steps = hidden // block
    blocks = channels // BLOCK

    def body(
        n, xt_ref, act_ref, slope_ref, db_ref, w1_ref, w2_ref, pool_ref,
        dsp_ref, out1_ref, out2_ref, a1, a2, dsp, sem, *rest,
    ):
        step = pl.program_id(0)

        @pl.when(step == 0)
        def _():
            dsp[...] = jnp.zeros(dsp.shape, F32)

        a1[...] = jnp.zeros(a1.shape, F32)
        a2[...] = jnp.zeros(a2.shape, F32)

        def one(at, carry):
            d_hidden = dot_nt(db_ref[at], w2_ref[...])
            d_expand = (slope_ref[at].astype(F32) * d_hidden).astype(BF16)
            a2[...] += dot_tn(act_ref[at], db_ref[at])
            a1[...] += dot_nn(xt_ref[at], d_expand)
            dsp[at] += dot_nt(d_expand, w1_ref[...])
            return carry

        lax.fori_loop(0, n[0], one, 0)

        @pl.when(step == steps - 1)
        def _():
            out = pltpu.make_async_copy(dsp, dsp_ref, sem)
            out.start()
            out.wait()

        if flat is None:
            out1_ref[...] = a1[...].astype(BF16)
            out2_ref[...] = a2[...].astype(BF16)
            return
        stage1, stage2, sems1, sems2, sems3 = rest

        def first_copies(at):
            out = []
            for index, (k, _, rows, start) in enumerate(flat.pieces[0]):
                place = pl.multiple_of(start + at * 2 * rows, 16)
                out.append((k, stage1.at[index, pl.ds(0, 2 * rows), :], place, 2 * rows))
            return out

        def second_copies(at):
            out = []
            for k, row, rows, start, height in flat.within(1, at * block, block):
                for c in range(blocks):
                    source = block_of(stage2, row - at * block, rows, c)
                    out.append((k, source, start + c * height, rows))
            return out

        def pool_copies():
            out = []
            for k, row, rows, start in flat.pieces[2]:
                for c in range(flat.shapes[2][1] // BLOCK):
                    out.append((k, block_of(pool_ref, row, rows, c), start + c * rows, rows))
            return out

        def firsts(now, action):
            copy_out(n[1], out1_ref, out2_ref, first_copies(now), sems1, action)

        def seconds(now, action):
            for static in range(steps):

                @pl.when(now == static)
                def _(static=static):
                    copy_out(n[1], out1_ref, out2_ref, second_copies(static), sems2, action)

        @pl.when(step == 0)
        def _():
            copy_out(n[1], out1_ref, out2_ref, pool_copies(), sems3, "start")

        @pl.when(step > 0)
        def _():
            seconds(step - 1, "wait")
            firsts(step - 1, "wait")

        stage2[...] = a2[...].astype(BF16)
        seconds(step, "start")
        for index, (_, row, rows, _) in enumerate(flat.pieces[0]):
            part = a1[row : row + rows, :]
            both = jnp.concatenate([part[:, 0:BLOCK], part[:, BLOCK:]], axis=0)
            stage1[index, 0 : 2 * rows, :] = both.astype(BF16)
        firsts(step, "start")

        @pl.when(step == steps - 1)
        def _():
            seconds(step, "wait")
            firsts(step, "wait")
            copy_out(n[1], out1_ref, out2_ref, pool_copies(), sems3, "wait")

    by_col = pl.BlockSpec((channels, block), lambda j, n: (0, j))
    by_row = pl.BlockSpec((block, channels), lambda j, n: (j, 0))
    by_hidden = pl.BlockSpec((slots, cells, block), lambda j, n: (0, 0, j))
    anywhere = pl.BlockSpec(memory_space=pl.ANY)
    wide = (slots, cells, channels)
    scratch = [
        pltpu.VMEM((channels, block), F32),
        pltpu.VMEM((block, channels), F32),
        pltpu.VMEM(wide, F32),
        pltpu.SemaphoreType.DMA,
    ]
    if flat is None:
        grads = [(w_pw1.shape, BF16, by_col), (w_pw2.shape, BF16, by_row)]
    else:
        grads = halves(flat)
        most = max(len(flat.within(1, at * block, block)) for at in range(steps))
        tall = max(rows for _, _, rows, _ in flat.pieces[0])
        scratch += [
            pltpu.VMEM((len(flat.pieces[0]), 2 * tall, BLOCK), BF16),
            pltpu.VMEM((block, channels), BF16),
            pltpu.SemaphoreType.DMA((len(flat.pieces[0]),)),
            pltpu.SemaphoreType.DMA((most * blocks,)),
            copy_semaphores(flat, 2),
        ]
    return run(
        "conv_mlp_back",
        body,
        (steps,),
        live,
        (spatial_flip, act, slope, d_branch, w_pw1, w_pw2, grad_pool),
        [whole(*spatial_flip.shape), by_hidden, by_hidden, whole(*wide), by_col, by_row, anywhere],
        [(wide, F32, anywhere)] + grads,
        scratch,
    )


def conv_norm_back(live, d_spatial, unit_values, inverse, gains):
    slots, cells, channels = d_spatial.shape

    def body(n, e_ref, u_ref, inv_ref, g_ref, out_ref, sums_ref):
        at = pl.program_id(0)

        @pl.when(at == 0)
        def _():
            sums_ref[...] = jnp.zeros(sums_ref.shape, F32)

        @pl.when(at < n[0])
        def _():
            def part(rows):
                e = e_ref[0, rows, :]
                value = u_ref[0, rows, :].astype(F32)
                sums_ref[0:1, :] += col_sum(e * value)
                sums_ref[1:2, :] += col_sum(e)
                grad = unit_back(value, inv_ref[0, rows, :], e * g_ref[0:1, :])
                sums_ref[2:3, :] += col_sum(grad)
                out_ref[0, rows, :] = grad.astype(BF16)

            over_rows(cells, part)

    one = slot(cells, channels)
    return run(
        "conv_norm_back",
        body,
        (slots,),
        live,
        (d_spatial, unit_values, inverse, gains),
        [one, one, slot(cells, 1), whole(*gains.shape)],
        [(d_spatial.shape, BF16, one), ((8, channels), F32, result(8, channels))],
    )


def conv_back(live, top, high, bottom, d_top, d_mid, d_bottom, d_post, kernel, after):
    slots, rows, cols, channels = high.shape

    def body(
        n, top_ref, mid_ref, bottom_ref, dt_ref, dm_ref, db_ref, dpost_ref, k_ref,
        out_ref, gk_ref, frame, d_frame,
    ):
        at = pl.program_id(0)

        @pl.when(at == 0)
        def _():
            gk_ref[...] = jnp.zeros(gk_ref.shape, F32)

        @pl.when(at < n[0])
        def _():
            frame[...] = jnp.zeros(frame.shape, F32)
            d_frame[...] = jnp.zeros(d_frame.shape, F32)

            def tile(tile_at, carry):
                lanes = lane_tile(tile_at)
                stage_rows(frame, top_ref, mid_ref, bottom_ref, lanes)
                stage_rows(d_frame, dt_ref, dm_ref, db_ref, lanes)

                def emit(y, total):
                    grad = total + dpost_ref[0, y, :, lanes].astype(F32)
                    out_ref[0, y, :, lanes] = grad.astype(BF16)

                depthwise_rows(d_frame, rows, cols, lambda t: k_ref[t : t + 1, lanes], True, emit)
                for left in range(KS):
                    totals = [None] * KS
                    grads = {}
                    for y in range(rows + 2 * REACH):
                        begin = EDGE - REACH + left
                        shifted = frame[y, begin : begin + cols, :].reshape(cols // 8, 8, LANES)
                        if y < rows:
                            grads[y] = d_frame[y + REACH, EDGE : EDGE + cols, :].reshape(
                                cols // 8, 8, LANES
                            )
                        for tap_row in range(KS):
                            row = y - tap_row
                            if 0 <= row < rows:
                                term = jnp.sum(shifted * grads[row], axis=0)
                                old = totals[tap_row]
                                totals[tap_row] = term if old is None else old + term
                        grads.pop(y - KS + 1, None)
                    for tap_row in range(KS):
                        tap = tap_row * KS + left
                        gk_ref[tap : tap + 1, lanes] += col_sum(totals[tap_row])
                return carry

            lax.fori_loop(0, channels // LANES, tile, 0)

        @pl.when(at >= n[0])
        def _():
            out_ref[...] = jnp.zeros(out_ref.shape, BF16)

    halo = slot(REACH, cols, channels)
    one = slot(rows, cols, channels)
    frame_shape = (rows + 2 * REACH, cols + 2 * EDGE, LANES)
    return run(
        "conv_back",
        body,
        (slots,),
        live,
        (top, high, bottom, d_top, d_mid, d_bottom, d_post, kernel),
        [halo, one, halo, halo, one, halo, one, whole(*kernel.shape)],
        [
            (high.shape, BF16, every_slot(rows, cols, channels)),
            ((64, channels), F32, result(64, channels)),
        ],
        [pltpu.VMEM(frame_shape, F32), pltpu.VMEM(frame_shape, F32)],
        after=after,
    )


def from_both_sides(head, tail):
    count = lax.axis_size("strip")
    before = lax.ppermute(tail, "strip", [(i, i + 1) for i in range(count - 1)])
    after = lax.ppermute(head, "strip", [(i + 1, i) for i in range(count - 1)])
    return before, after


def bin_weights(edges, cell_count):
    cells = jnp.arange(cell_count, dtype=jnp.int32)
    inside = (cells[None, :] >= edges[:-1, None]) & (cells[None, :] < edges[1:, None])
    widths = (edges[1:] - edges[:-1]).astype(F32)
    return inside.astype(F32) / widths[:, None]


def strip_bins(edges, first_bin, bin_count, first_cell, cell_count):
    padded = jnp.concatenate([edges[:1], edges, edges[-1:]])
    window = lax.dynamic_slice_in_dim(padded, first_bin + 1, bin_count + 1)
    cells = first_cell + jnp.arange(cell_count, dtype=jnp.int32)
    inside = (cells[None, :] >= window[:-1, None]) & (cells[None, :] < window[1:, None])
    widths = jnp.maximum(window[1:] - window[:-1], 1).astype(F32)
    return inside.astype(F32) / widths[:, None]


def bit_of(axis, bit):
    return (lax.axis_index(axis) >> bit) & 1


def swap_halves(cells, axis, bit, own):
    size = lax.axis_size(axis)
    keep = lax.dynamic_index_in_dim(cells, own, 1, keepdims=False)
    send = lax.dynamic_index_in_dim(cells, 1 - own, 1, keepdims=False)
    got = lax.ppermute(send, axis, [(i, i ^ (1 << bit)) for i in range(size)])
    return (keep.astype(F32) + got.astype(F32)).astype(BF16)


def sum_everywhere(values):
    for axis in ("dp", "strip"):
        size = lax.axis_size(axis)
        step = 1
        while step < size:
            values = values + lax.ppermute(values, axis, [(i, i ^ step) for i in range(size)])
            step *= 2
    return values


def bits(axis):
    return int(math.log2(lax.axis_size(axis)))


def halve_dp(cells, base, bit):
    if cells.shape[0] % 2:
        cells = jnp.pad(cells, [(0, 1)] + [(0, 0)] * (cells.ndim - 1))
    own = (bit_of("dp", bit) - base) & 1
    cells = cells.reshape((cells.shape[0] // 2, 2) + cells.shape[1:])
    return swap_halves(cells, "dp", bit, own), (base + own) >> 1


def halve_strip(cells):
    for bit in range(bits("strip")):
        m, count = cells.shape[:2]
        cells = cells.reshape((m * count // 2, 2) + cells.shape[2:])
        cells = swap_halves(cells, "strip", bit, bit_of("strip", bit))
        cells = cells.reshape((m, count // 2) + cells.shape[1:])
    return cells


def shared_sum(matrix, offset, chunk, strip_first):
    strips = lax.axis_size("strip")
    rows, cols = matrix.shape
    chunk_rows = chunk // cols
    base = offset // (chunk * strips)
    front = (offset - base * chunk * strips) // cols
    groups = -(-(front + rows) // (chunk_rows * strips))
    back = groups * chunk_rows * strips - front - rows
    cells = jnp.pad(matrix, ((front, back), (0, 0))).reshape(groups, strips, chunk_rows, cols)
    cells, base = halve_dp(cells, base, 0)
    if strip_first:
        cells = halve_strip(cells)
        cells, base = halve_dp(cells, base, 1)
    else:
        cells, base = halve_dp(cells, base, 1)
        cells = halve_strip(cells)
    return cells.reshape(cells.shape[0], chunk), base


def owned_chunk(matrices, extras):
    data_count = lax.axis_size("dp")
    strips = lax.axis_size("strip")
    devices = data_count * strips
    chunk = sum(m.size for m in matrices) // devices
    span = data_count // 4
    placed = None
    offset = 0
    for order, matrix in enumerate(matrices):
        part, base = shared_sum(matrix, offset, chunk, order % 2 == 0)
        canvas = jnp.zeros((span + part.shape[0], chunk), BF16)
        canvas = lax.dynamic_update_slice(canvas, part, (base, 0))[:span]
        placed = canvas if placed is None else placed + canvas
        offset += matrix.size
    for bit in range(2, bits("dp")):
        placed = placed.reshape(placed.shape[0] // 2, 2, chunk)
        placed = swap_halves(placed, "dp", bit, bit_of("dp", bit))
    return share_of(placed.reshape(chunk).astype(F32), chunk, extras)


STEPS = {
    "core": ("dp", 1, lambda dp, strip: dp & 1),
    "x": ("strip", 1, lambda dp, strip: strip & 1),
    "y": ("dp", 2, lambda dp, strip: (dp >> 1) & 1),
    "z": ("dp", 4, lambda dp, strip: ((dp >> 2) ^ (dp >> 3)) & 1),
    "far": ("dp", 12, lambda dp, strip: (dp >> 3) & 1),
}
ORDERS = (("x", "y", "z", "far"), ("y", "z", "x", "far"), ("z", "x", "y", "far"))


def across(step, value):
    axis, flip_bits, _ = STEPS[step]
    return lax.ppermute(value, axis, [(i, i ^ flip_bits) for i in range(lax.axis_size(axis))])


def split_sum(flat, kept, arrived, level, after):
    parts = len(ORDERS)
    rows = flat.units // parts
    count = HALF_CHUNKS >> (level + 1)
    own = [STEPS[order[level]][2](lax.axis_index("dp"), lax.axis_index("strip")) for order in ORDERS]
    bits = jnp.stack(own).astype(jnp.int32)
    specs, args = [], []
    for part, order in enumerate(ORDERS):
        left = [name for name in ("far", "z", "y", "x") if name not in order[:level]]
        low = len(left) - 1 - left.index(order[level])

        for flipped in (0, 1):

            def place(i, bit, part=part, low=low, flipped=flipped):
                mine = bit[part] ^ flipped
                index = ((i >> low) << (low + 1)) | (mine << low) | (i & ((1 << low) - 1))
                return index, part if level == 0 else 0, 0

            for source in (kept, arrived):
                args.append(source[0 if level == 0 else part])
                specs.append(pl.BlockSpec((1, rows, BLOCK), place))

    def body(_, *refs):
        ins, outs = refs[: 4 * parts], refs[4 * parts :]
        for at in range(2 * parts):
            total = ins[2 * at][...].astype(F32) + ins[2 * at + 1][...].astype(F32)
            outs[at][...] = total.astype(BF16)

    out = pl.BlockSpec((1, rows, BLOCK), lambda i, bit: (i, 0, 0))
    done = run(
        "split_sum",
        body,
        (count,),
        bits,
        tuple(args),
        specs,
        [((count, rows, BLOCK), BF16, out)] * (2 * parts),
        after=after,
    )
    return done[0::2], done[1::2]


def sent(sends, level):
    return [across(order[level], value) for order, value in zip(ORDERS, sends)]


def last_sum(kept, arrived):
    parts = [(k.astype(F32) + a.astype(F32))[0] for k, a in zip(kept, arrived)]
    return jnp.concatenate(parts, axis=0)


def row_major(flat, units):
    devices = lax.axis_size("dp") * lax.axis_size("strip")
    index = lax.axis_index("dp") * lax.axis_size("strip") + lax.axis_index("strip")
    kinds, kind_of = [], []
    for k in range(devices):
        kind = []
        for matrix, pieces in enumerate(flat.pieces):
            for chunk, _, rows, start in pieces:
                if chunk == k:
                    kind.append((start, rows, flat.shapes[matrix][1] // BLOCK))
        kind = tuple(kind)
        if kind not in kinds:
            kinds.append(kind)
        kind_of.append(kinds.index(kind))

    def ordered(kind):
        def branch(value):
            out = []
            for start, rows, blocks in kind:
                piece = value[start : start + rows * blocks].reshape(blocks, rows, BLOCK)
                out.append(piece.transpose(1, 0, 2).reshape(-1))
            return jnp.concatenate(out)

        return branch

    which = jnp.asarray(kind_of, jnp.int32)[index]
    return lax.switch(which, [ordered(kind) for kind in kinds], units)


def share_of(mine, chunk, extras):
    data_count = lax.axis_size("dp")
    strips = lax.axis_size("strip")
    devices = data_count * strips
    extra = extras.shape[0] // devices
    index = lax.axis_index("dp") * strips + lax.axis_index("strip")
    pieces = [mine]
    left = extras.shape[0]
    padded = jnp.pad(extras, (0, chunk))
    for hop in range(1, -(-left // chunk) + 1):
        size = min(left, chunk)
        left -= size
        following = lax.ppermute(
            mine[:size].astype(BF16),
            ("dp", "strip"),
            [(i + hop, i) for i in range(devices - hop)],
        ).astype(F32)
        past = index + hop - devices
        own_extras = lax.dynamic_slice(padded, (jnp.maximum(past, 0) * chunk,), (size,))
        pieces.append(jnp.where(past >= 0, own_extras, following))
    return lax.dynamic_slice(jnp.concatenate(pieces), (index * extra,), (chunk + extra,))


def per_device(
    low_tokens,
    high_map,
    counts,
    row_edges,
    col_edges,
    w_qkv,
    w_attn_out,
    w_fc1,
    w_fc2,
    vit_gains,
    vit_shifts,
    w_pw1,
    w_pw2,
    w_pool,
    dw_kernel,
    conv_gains,
    conv_shifts,
    w_gate,
    d_merged,
    d_conv,
):
    slots, tok_rows, width = low_tokens.shape
    rows, cols, channels = high_map.shape[1:]
    cells = rows * cols
    strips = lax.axis_size("strip")
    strip = lax.axis_index("strip")
    live = jnp.stack([counts[0], lax.axis_index("dp") & 1]).astype(jnp.int32)

    col_bins = bin_weights(col_edges, cols)
    side = col_bins.shape[0]
    own_bins = tok_rows // side
    near_bins = strip_bins(row_edges, strip * own_bins - 1, own_bins + 2, strip * rows, rows)
    bins = (near_bins[:, None, :, None] * col_bins[None, :, None, :]).astype(BF16)
    bins = bins.reshape((own_bins + 2) * side, cells)

    def shifted(value, by):
        return lax.ppermute(value, "strip", [(i, (i + by) % strips) for i in range(strips)])

    tok_all = jnp.concatenate(
        [low_tokens] + [shifted(low_tokens, by) for by in range(1, strips)], axis=1
    )
    top, bottom = from_both_sides(high_map[:, :REACH], high_map[:, -REACH:])

    data_count = lax.axis_size("dp")
    devices = data_count * strips
    vit_flat = Flat([w.shape for w in (w_qkv, w_attn_out, w_fc1, w_fc2)], devices)
    conv_flat = Flat([w.shape for w in (w_pw1, w_pw2, w_pool)], devices)
    chunked = devices == 2 * HALF_CHUNKS and strips == 2 and vit_flat.even and conv_flat.even
    if not chunked:
        vit_flat = conv_flat = None

    spatial, spatial_flip, conv_unit, conv_inverse = conv_front(
        live, top, high_map, bottom, dw_kernel, conv_gains, conv_shifts
    )
    act, slope, branch, high_out = conv_mlp(
        live, spatial, high_map.reshape(slots, cells, channels), w_pw1, w_pw2, conv_gains
    )
    own, before_part, after_part = pool(live, high_out, bins, side)
    first, last = from_both_sides(before_part, after_part)
    normed, q, kv, probs, mixed, residual, inner, inner_flip = vit_front(
        live, tok_all, w_qkv, w_attn_out, vit_gains, vit_shifts, tok_rows, (own,)
    )
    lift, d_pooled, grad_pool, gate_sums = adapter(
        live, own, first, last, d_merged, w_pool, w_gate.reshape(1, channels), (inner,)
    )
    near_before, near_after = from_both_sides(d_pooled[:, :side], d_pooled[:, -side:])
    d_post, d_branch, scale_sums = unpool(
        live,
        jnp.concatenate([near_before, d_pooled, near_after], axis=1),
        bins.T,
        d_conv.reshape(slots, cells, channels),
        branch,
        conv_gains,
    )
    d_spatial, *conv_grads = conv_mlp_back(
        live, spatial_flip, act, slope, d_branch, w_pw1, w_pw2, grad_pool, conv_flat
    )
    d_conv_in, norm_sums = conv_norm_back(live, d_spatial, conv_unit, conv_inverse, conv_gains)
    d_conv_in = d_conv_in.reshape(high_map.shape)
    d_before, d_after = from_both_sides(d_conv_in[:, :REACH], d_conv_in[:, -REACH:])

    merged, d_inner, *vit_grads = vit_mlp(
        live, inner, inner_flip, d_merged, residual, lift, w_fc1, w_fc2, vit_flat, (d_conv_in,)
    )
    order = (d_inner,)
    if chunked:
        kept, sends = split_sum(
            conv_flat, conv_grads[:1], [across("core", conv_grads[1])], 0, order
        )
        arrived = sent(sends, 0)
        order = (sends[0],)
    d_residual, d_mixed, inner_sums, *vit_grads_out = vit_back(
        live, residual, d_inner, d_merged, mixed, w_attn_out, vit_gains, vit_flat,
        tuple(vit_grads), order,
    )
    d_q, d_k, d_v = attention_back(live, probs, q, kv, d_mixed)
    order = (d_q,)
    if chunked:
        kept, sends = split_sum(conv_flat, kept, arrived, 1, order)
        arrived = sent(sends, 1)
        order = (sends[0],)
    d_normed, *vit_grads_qkv = qkv_back(
        live, normed, d_q, d_k, d_v, w_qkv, vit_flat, tuple(vit_grads_out), order
    )
    d_other = jnp.zeros(low_tokens.shape, BF16)
    for by in range(1, strips):
        part = d_normed[:, by * tok_rows : (by + 1) * tok_rows].astype(BF16)
        d_other = d_other + shifted(part, -by) if by > 1 else shifted(part, -by)
    order = (d_normed,)
    if chunked:
        vit_arrived = across("core", vit_grads_qkv[1])
    grad_map, kernel_sums = conv_back(
        live,
        top,
        high_map,
        bottom,
        d_before,
        d_conv_in,
        d_after,
        d_post.reshape(high_map.shape),
        dw_kernel,
        order,
    )
    order = (grad_map,)
    if chunked:
        kept, sends = split_sum(conv_flat, kept, arrived, 2, order)
        arrived = sent(sends, 2)
        vit_kept, vit_sends = split_sum(vit_flat, vit_grads_qkv[:1], [vit_arrived], 0, (sends[0],))
        vit_arrived = sent(vit_sends, 0)
        order = (vit_sends[0],)
    grad_tokens, token_sums = tokens_back(
        live, low_tokens, d_normed, d_other, d_residual, vit_gains, order
    )

    vit_extras = jnp.concatenate([token_sums[0], inner_sums[0], token_sums[1], inner_sums[1]])
    conv_extras = jnp.concatenate(
        [
            kernel_sums[: KS * KS].reshape(-1),
            norm_sums[0],
            scale_sums[0],
            norm_sums[2],
            norm_sums[1],
            gate_sums[0],
        ]
    )
    extras = sum_everywhere(jnp.concatenate([vit_extras, conv_extras]))
    vit_extras, conv_extras = extras[: vit_extras.shape[0]], extras[vit_extras.shape[0] :]
    if chunked:
        kept, sends = split_sum(conv_flat, kept, arrived, 3, (grad_tokens,))
        arrived = sent(sends, 3)
        vit_kept, vit_sends = split_sum(vit_flat, vit_kept, vit_arrived, 1, (sends[0],))
        vit_arrived = sent(vit_sends, 1)
        conv_mine = row_major(conv_flat, last_sum(kept, arrived))
        conv_out = share_of(conv_mine, conv_flat.chunk, conv_extras)
        for level in (2, 3):
            vit_kept, vit_sends = split_sum(vit_flat, vit_kept, vit_arrived, level, ())
            vit_arrived = sent(vit_sends, level)
        vit_mine = row_major(vit_flat, last_sum(vit_kept, vit_arrived))
        vit_out = share_of(vit_mine, vit_flat.chunk, vit_extras)
    else:
        vit_out = owned_chunk(vit_grads_qkv + vit_grads_out + vit_grads, vit_extras)
        conv_out = owned_chunk(conv_grads + [grad_pool], conv_extras)
    return (
        merged,
        high_out.reshape(high_map.shape),
        grad_tokens,
        grad_map,
        vit_out,
        conv_out,
    )


def solution(mesh):
    images = P("dp", "strip", None)
    maps = P("dp", "strip", None, None)
    flat = P(("dp", "strip"))
    in_specs = (images, maps, P("dp")) + (P(),) * 15 + (images, maps)
    out_specs = (images, maps, images, maps, flat, flat)
    return jax.shard_map(
        per_device, mesh=mesh, in_specs=in_specs, out_specs=out_specs, check_vma=False
    )
```

```python
import math

import jax
import jax.numpy as jnp
from jax import lax
from jax.experimental import pallas as pl
from jax.experimental.pallas import tpu as pltpu
from jax.sharding import PartitionSpec as P

HEADS = 16
KS = 7
REACH = KS // 2
EPSILON = 1e-05
LANES = 128
EDGE = 8
BLOCK = 256
BUNDLE = 8
F32 = jnp.float32
BF16 = jnp.bfloat16
VMEM_BYTES = 60 * 1024 * 1024


def dot_nn(a, b):
    return jnp.dot(a, b, preferred_element_type=F32)


def dot_nt(a, b):
    return lax.dot_general(a, b, (((1,), (1,)), ((), ())), preferred_element_type=F32)


def dot_tn(a, b):
    return lax.dot_general(a, b, (((0,), (0,)), ((), ())), preferred_element_type=F32)


def flip(value):
    return value.astype(F32).T.astype(BF16)


def row_step(rows):
    for step in (128, 96, 64, 48, 32, 16):
        if rows % step == 0:
            return step
    return rows


def over_rows(rows, body):
    step = row_step(rows)

    def one(at, carry):
        body(pl.ds(pl.multiple_of(at * step, step), step))
        return carry

    if step == rows:
        body(pl.ds(0, rows))
    else:
        lax.fori_loop(0, rows // step, one, 0)


def lane_tile(at):
    return pl.ds(pl.multiple_of(at * LANES, LANES), LANES)


def unit(values):
    center = values - jnp.mean(values, axis=-1, keepdims=True)
    inverse = lax.rsqrt(jnp.mean(center * center, axis=-1, keepdims=True) + EPSILON)
    return center * inverse, inverse


def unit_back(unit_values, inverse, grad):
    return (
        grad
        - jnp.mean(grad, axis=-1, keepdims=True)
        - unit_values * jnp.mean(grad * unit_values, axis=-1, keepdims=True)
    ) * inverse


def gelu_pair(x):
    scale = math.sqrt(2.0 / math.pi)
    square = x * x
    bend = jnp.tanh(x * (scale + (scale * 0.044715) * square))
    half = 0.5 + 0.5 * bend
    slope = half + (0.5 * x) * (1.0 - bend * bend) * (scale + (3.0 * scale * 0.044715) * square)
    return x * half, slope


def col_sum(values):
    return jnp.sum(values, axis=0, keepdims=True)


def held(at, live):
    return jnp.maximum(jnp.minimum(at, live[0] - 1), 0)


def slot(*shape):
    return pl.BlockSpec(
        (1,) + shape, lambda *g: (held(g[0], g[-1]),) + (0,) * len(shape)
    )


def every_slot(*shape):
    return pl.BlockSpec((1,) + shape, lambda *g: (g[0],) + (0,) * len(shape))


def whole(*shape):
    return pl.BlockSpec(shape, lambda *g: (0,) * len(shape), pipeline_mode=pl.Buffered(1))


def result(*shape):
    return pl.BlockSpec(shape, lambda *g: (0,) * len(shape))


def run(name, body, grid, live, args, in_specs, outs, scratch=(), after=(), alias=()):
    out_shape = [jax.ShapeDtypeStruct(shape, dtype) for shape, dtype, _ in outs]
    count = 1 + len(args)

    def without_order(*refs):
        body(*refs[:count], *refs[count + len(after) :])

    return pl.pallas_call(
        without_order,
        grid_spec=pltpu.PrefetchScalarGridSpec(
            num_scalar_prefetch=1,
            grid=grid,
            in_specs=list(in_specs) + [pl.BlockSpec(memory_space=pl.ANY)] * len(after),
            out_specs=[spec for _, _, spec in outs],
            scratch_shapes=list(scratch),
        ),
        out_shape=out_shape,
        input_output_aliases={1 + given: out for given, out in alias},
        compiler_params=pltpu.CompilerParams(
            dimension_semantics=("arbitrary",) * len(grid), vmem_limit_bytes=VMEM_BYTES
        ),
        cost_estimate=pl.CostEstimate(flops=0, bytes_accessed=0, transcendentals=0),
        name=name,
    )(live, *args, *after)


class Flat:
    def __init__(self, shapes, devices):
        self.shapes = shapes
        self.chunk = sum(r * c for r, c in shapes) // devices
        self.units = self.chunk // BLOCK
        self.pieces = []
        self.even = sum(r * c for r, c in shapes) % (devices * BLOCK * 3 * 16) == 0
        offset = 0
        for rows, cols in shapes:
            self.even &= self.chunk % cols == 0 and offset % cols == 0 and cols % BLOCK == 0
            found = []
            if self.even:
                height, begin = self.chunk // cols, offset // cols
                for k in range(devices):
                    low = max(k * height, begin)
                    high = min((k + 1) * height, begin + rows)
                    if low < high:
                        start = (low - k * height) * (cols // BLOCK)
                        found.append((k, low - begin, high - low, start))
                        self.even &= (high - low) % 8 == 0 and start % 16 == 0
                self.even &= bool(self.pieces) or found[-1][0] < 2 * BUNDLE
            self.pieces.append(found)
            offset += rows * cols

    def within(self, matrix, first, count):
        out = []
        for k, row, height, start in self.pieces[matrix]:
            low, high = max(row, first), min(row + height, first + count)
            if low < high:
                out.append((k, low, high - low, start + low - row, height))
        return out


def side_of(chunk):
    z1, z0, y = (chunk >> 4) & 1, (chunk >> 3) & 1, (chunk >> 2) & 1
    return z1, (chunk >> 1) & 1, (z0 ^ z1) * 4 + y * 2 + (chunk & 1)


def copy_out(own_core, refs, copies, sems, action):
    for at, (chunk, source, place, rows) in enumerate(copies):
        upper, core, index = side_of(chunk)
        for held_here, ref in ((True, refs[2 * upper]), (False, refs[2 * upper + 1])):

            @pl.when((own_core == core) == held_here)
            def _(ref=ref, at=at, source=source, place=place, rows=rows, index=index):
                target = ref.at[index, pl.ds(place, rows), :]
                getattr(pltpu.make_async_copy(source, target, sems.at[at]), action)()


def copy_all(own_core, refs, stage, flat, matrix, sems):
    copies = []
    for k, row, rows, start in flat.pieces[matrix]:
        for c in range(stage.shape[1] // BLOCK):
            copies.append((k, block_of(stage, row, rows, c), start + c * rows, rows))
    copy_out(own_core, refs, copies, sems, "start")
    copy_out(own_core, refs, copies, sems, "wait")


def copy_semaphores(flat, matrix):
    return pltpu.SemaphoreType.DMA((len(flat.pieces[matrix]) * flat.shapes[matrix][1] // BLOCK,))


def bundles(flat, count):
    shape = (BUNDLE, flat.units, BLOCK)
    return [(shape, BF16, pl.BlockSpec(memory_space=pl.ANY))] * count


def block_of(ref, first, rows, block):
    return ref.at[pl.ds(first, rows), pl.ds(block * BLOCK, BLOCK)]


def vit_front(live, tok_all, w_qkv, w_out, gains, shifts, tok_rows, after):
    slots, key_rows, width = tok_all.shape
    head = width // HEADS
    pairs = width // LANES
    per_tile = LANES // head

    def body(
        n, x_ref, wq_ref, wo_ref, g_ref, b_ref,
        normed_ref, q_ref, kv_ref, probs_ref, mixed_ref, res_ref, inner_ref, flip_ref,
    ):
        @pl.when(pl.program_id(0) < n[0])
        def _():
            def first_norm(rows):
                value, _ = unit(x_ref[0, rows, :].astype(F32))
                normed_ref[0, rows, :] = (value * g_ref[0:1, :] + b_ref[0:1, :]).astype(BF16)

            over_rows(key_rows, first_norm)
            q_ref[0] = dot_nn(normed_ref[0, 0:tok_rows, :], wq_ref[:, 0:width]).astype(BF16)
            for part in range(4):
                cols = slice(part * width // 2, (part + 1) * width // 2)
                w_cols = slice(width + cols.start, width + cols.stop)
                kv_ref[0, :, cols] = dot_nn(normed_ref[0], wq_ref[:, w_cols]).astype(BF16)

            lane = lax.broadcasted_iota(jnp.int32, (1, LANES), 1) // head

            def heads(pair, carry):
                q = q_ref[0, :, lane_tile(pair)] * jnp.asarray(1.0 / math.sqrt(head), BF16)
                k = kv_ref[0, :, lane_tile(pair)].astype(F32)
                v_flip = flip(kv_ref[0, :, lane_tile(pairs + pair)])
                mixed = []
                for h in range(per_tile):
                    scores = dot_nt(jnp.where(lane == h, k, 0.0).astype(BF16), q)
                    top = jnp.max(scores, axis=0, keepdims=True)
                    raised = jnp.exp(scores - top)
                    probs = (raised * (1.0 / col_sum(raised))).astype(BF16)
                    probs_ref[0, pair * per_tile + h] = probs
                    mixed.append(dot_nn(v_flip[h * head : (h + 1) * head, :], probs))
                mixed_ref[0, :, lane_tile(pair)] = jnp.concatenate(mixed, axis=0).T.astype(BF16)
                return carry

            lax.fori_loop(0, pairs, heads, 0)
            res_ref[0] = dot_nn(mixed_ref[0], wo_ref[...])

            def second_norm(rows):
                res = res_ref[0, rows, :] + x_ref[0, rows, :].astype(F32)
                res_ref[0, rows, :] = res
                value, _ = unit(res)
                inner_ref[0, rows, :] = (value * g_ref[1:2, :] + b_ref[1:2, :]).astype(BF16)

            over_rows(tok_rows, second_norm)
            flip_ref[0] = flip(inner_ref[0])

    return run(
        "vit_front",
        body,
        (slots,),
        live,
        (tok_all, w_qkv, w_out, gains, shifts),
        [slot(key_rows, width), whole(*w_qkv.shape), whole(*w_out.shape)]
        + [whole(*gains.shape), whole(*shifts.shape)],
        [
            ((slots, key_rows, width), BF16, slot(key_rows, width)),
            ((slots, tok_rows, width), BF16, slot(tok_rows, width)),
            ((slots, key_rows, 2 * width), BF16, slot(key_rows, 2 * width)),
            ((slots, HEADS, key_rows, tok_rows), BF16, slot(HEADS, key_rows, tok_rows)),
            ((slots, tok_rows, width), BF16, slot(tok_rows, width)),
            ((slots, tok_rows, width), F32, slot(tok_rows, width)),
            ((slots, tok_rows, width), BF16, slot(tok_rows, width)),
            ((slots, width, tok_rows), BF16, slot(width, tok_rows)),
        ],
        after=after,
    )


def vit_mlp(live, inner, inner_flip, d_mlp, residual, lift, w_fc1, w_fc2, flat, after):
    slots, tok_rows, width = inner.shape
    hidden = w_fc1.shape[1]
    block = 512
    steps = hidden // block
    blocks = width // BLOCK

    def body(
        n, x_ref, xt_ref, dm_ref, res_ref, lift_ref, w1_ref, w2_ref,
        merged_ref, din_ref, *rest,
    ):
        if flat is None:
            out1_ref, out2_ref, low, a1, a2 = rest
        else:
            refs, (low, a1, a2, stage1, stage2, sems1, sems2) = rest[:4], rest[4:]
        step = pl.program_id(0)

        @pl.when(step == 0)
        def _():
            low[...] = res_ref[...]
            din_ref[...] = jnp.zeros(din_ref.shape, F32)

        a1[...] = jnp.zeros(a1.shape, F32)
        a2[...] = jnp.zeros(a2.shape, F32)

        def one(at, carry):
            before = dot_nn(x_ref[at], w1_ref[...])
            d_act = dot_nt(dm_ref[at], w2_ref[...])
            act, slope = gelu_pair(before)
            act = act.astype(BF16)
            d_fc = (slope * d_act).astype(BF16)
            low[at] += dot_nn(act, w2_ref[...])
            a2[...] += dot_tn(act, dm_ref[at])
            a1[...] += dot_nn(xt_ref[at], d_fc)
            din_ref[at] += dot_nt(d_fc, w1_ref[...])
            return carry

        lax.fori_loop(0, n[0], one, 0)

        @pl.when(step == steps - 1)
        def _():
            def close(at, carry):
                merged_ref[at] = (low[at] + lift_ref[at]).astype(BF16)
                return carry

            def blank(at, carry):
                merged_ref[at] = jnp.zeros(merged_ref.shape[1:], BF16)
                return carry

            lax.fori_loop(0, n[0], close, 0)
            lax.fori_loop(n[0], slots, blank, 0)

        if flat is None:
            out1_ref[...] = a1[...].astype(BF16)
            out2_ref[...] = a2[...].astype(BF16)
            return

        def first_copies(at):
            out = []
            for c in range(block // BLOCK):
                for k, row, rows, start, height in flat.within(2, 0, width):
                    place = start + (at * (block // BLOCK) + c) * height
                    out.append((k, block_of(stage1, row, rows, c), pl.multiple_of(place, 16), rows))
            return out

        def second_copies(at):
            out = []
            for k, row, rows, start, height in flat.within(3, at * block, block):
                for c in range(blocks):
                    source = block_of(stage2, row - at * block, rows, c)
                    out.append((k, source, start + c * height, rows))
            return out

        def each(at, now, action):
            copy_out(n[1], refs, first_copies(now), sems1, action)
            for static in range(steps):

                @pl.when(now == static)
                def _(static=static):
                    copy_out(n[1], refs, second_copies(static), sems2, action)

        @pl.when(step > 0)
        def _():
            each(step, step - 1, "wait")

        stage1[...] = a1[...].astype(BF16)
        stage2[...] = a2[...].astype(BF16)
        each(step, step, "start")

        @pl.when(step == steps - 1)
        def _():
            each(step, step, "wait")

    wide = (slots, tok_rows, width)
    by_col = pl.BlockSpec((width, block), lambda j, n: (0, j))
    by_row = pl.BlockSpec((block, width), lambda j, n: (j, 0))
    scratch = [
        pltpu.VMEM(wide, F32),
        pltpu.VMEM((width, block), F32),
        pltpu.VMEM((block, width), F32),
    ]
    if flat is None:
        grads = [(w_fc1.shape, BF16, by_col), (w_fc2.shape, BF16, by_row)]
    else:
        grads = bundles(flat, 4)
        most = max(len(flat.within(3, at * block, block)) for at in range(steps))
        scratch += [
            pltpu.VMEM((width, block), BF16),
            pltpu.VMEM((block, width), BF16),
            pltpu.SemaphoreType.DMA((block // BLOCK * len(flat.pieces[2]),)),
            pltpu.SemaphoreType.DMA((most * blocks,)),
        ]
    return run(
        "vit_mlp",
        body,
        (steps,),
        live,
        (inner, inner_flip, d_mlp, residual, lift, w_fc1, w_fc2),
        [whole(*wide), whole(*inner_flip.shape)] + [whole(*wide)] * 3 + [by_col, by_row],
        [(wide, BF16, result(*wide)), (wide, F32, result(*wide))] + grads,
        scratch,
        after=after,
    )


def vit_back(live, residual, d_inner, d_merged, mixed, w_out, gains, flat, kept, after):
    slots, tok_rows, width = residual.shape

    def body(n, res_ref, din_ref, dm_ref, mix_ref, wo_ref, g_ref, *rest):
        if flat is None:
            dres_ref, dmix_ref, sums_ref, gout_ref, low, acc = rest
        else:
            _, _, dres_ref, dmix_ref, sums_ref, keep_ref, send_ref, low, acc, stage, sems = rest
        at = pl.program_id(0)

        @pl.when(at == 0)
        def _():
            acc[...] = jnp.zeros(acc.shape, F32)
            sums_ref[...] = jnp.zeros(sums_ref.shape, F32)

        @pl.when(at < n[0])
        def _():
            def back(rows):
                value, inverse = unit(res_ref[0, rows, :])
                e = din_ref[0, rows, :]
                sums_ref[0:1, :] += col_sum(e * value)
                sums_ref[1:2, :] += col_sum(e)
                d_res = dm_ref[0, rows, :].astype(F32) + unit_back(value, inverse, e * g_ref[1:2, :])
                dres_ref[0, rows, :] = d_res
                low[rows, :] = d_res.astype(BF16)

            over_rows(tok_rows, back)
            dmix_ref[0] = dot_nt(low[...], wo_ref[...]).astype(BF16)
            acc[...] += dot_tn(mix_ref[0], low[...])

        @pl.when(at == slots - 1)
        def _():
            if flat is None:
                gout_ref[...] = acc[...].astype(BF16)
            else:
                stage[...] = acc[...].astype(BF16)
                copy_all(n[1], (keep_ref, send_ref), stage, flat, 1, sems)

    wide = (slots, tok_rows, width)
    one = slot(tok_rows, width)
    args = (residual, d_inner, d_merged, mixed, w_out, gains)
    specs = [one, one, one, one, whole(*w_out.shape), whole(*gains.shape)]
    scratch = [pltpu.VMEM((tok_rows, width), BF16), pltpu.VMEM(w_out.shape, F32)]
    grads, alias = [(w_out.shape, BF16, result(*w_out.shape))], ()
    if flat is not None:
        args, specs, grads = args + kept, specs + [pl.BlockSpec(memory_space=pl.ANY)] * 2, bundles(flat, 2)
        scratch += [pltpu.VMEM(w_out.shape, BF16), copy_semaphores(flat, 1)]
        alias = ((6, 3), (7, 4))
    return run(
        "vit_back",
        body,
        (slots,),
        live,
        args,
        specs,
        [(wide, F32, one), (wide, BF16, one), ((8, width), F32, result(8, width))] + grads,
        scratch,
        after=after,
        alias=alias,
    )


def attention_back(live, probs, q, kv, d_mixed, after):
    slots, _, key_rows, tok_rows = probs.shape
    width = q.shape[2]
    head = width // HEADS
    pairs = width // LANES
    per_tile = LANES // head
    scale = 1.0 / math.sqrt(head)

    def body(n, p_ref, q_ref, k_ref, v_ref, dm_ref, dq_ref, dk_ref, dv_ref):
        @pl.when(pl.program_id(0) < n[0])
        def _():
            lane = lax.broadcasted_iota(jnp.int32, (1, LANES), 1) // head
            q = q_ref[0].astype(F32) * scale
            v = v_ref[0].astype(F32)
            dm = dm_ref[0].astype(F32)
            dm_low = dm_ref[0]
            k_flip = flip(k_ref[0].astype(F32) * scale)
            d_keys = jnp.zeros((key_rows, LANES), F32)
            d_values = jnp.zeros((key_rows, LANES), F32)
            d_query = []
            for h in range(per_tile):
                own = lane == h
                probs_low = p_ref[0, h]
                d_probs = dot_nt(jnp.where(own, v, 0.0).astype(BF16), dm_low)
                d_values += dot_nn(probs_low, jnp.where(own, dm, 0.0).astype(BF16))
                wide = probs_low.astype(F32)
                d_scores = (wide * (d_probs - col_sum(wide * d_probs))).astype(BF16)
                d_keys += dot_nn(d_scores, jnp.where(own, q, 0.0).astype(BF16))
                d_query.append(dot_nn(k_flip[h * head : (h + 1) * head, :], d_scores))
            dq_ref[0] = jnp.concatenate(d_query, axis=0).T.astype(BF16)
            dk_ref[0] = d_keys.astype(BF16)
            dv_ref[0] = d_values.astype(BF16)

    def held_pair(i, p, n):
        return jnp.where(i < n[0], p, pairs - 1)

    def at_pair(rows, shift=0):
        return pl.BlockSpec(
            (1, rows, LANES), lambda i, p, n: (held(i, n), 0, held_pair(i, p, n) + shift)
        )

    own = at_pair(tok_rows)
    keys = at_pair(key_rows)
    return run(
        "attention_back",
        body,
        (slots, pairs),
        live,
        (probs, q, kv, kv, d_mixed),
        [
            pl.BlockSpec(
                (1, per_tile, key_rows, tok_rows),
                lambda i, p, n: (held(i, n), held_pair(i, p, n), 0, 0),
            ),
            own,
            keys,
            at_pair(key_rows, pairs),
            own,
        ],
        [
            (q.shape, BF16, own),
            ((slots, key_rows, width), BF16, keys),
            ((slots, key_rows, width), BF16, keys),
        ],
        after=after,
    )


def qkv_back(live, normed, d_q, d_k, d_v, w_qkv, flat, kept, after):
    slots, key_rows, width = normed.shape
    tok_rows = d_q.shape[1]

    def body(n, x_ref, dq_ref, dk_ref, dv_ref, w_ref, *rest):
        if flat is None:
            dn_ref, gw_ref, x_flip, acc = rest
        else:
            _, _, dn_ref, keep_ref, send_ref, x_flip, acc, stage, sems = rest
        at = pl.program_id(0)

        @pl.when(at == 0)
        def _():
            acc[...] = jnp.zeros(acc.shape, F32)

        @pl.when(at < n[0])
        def _():
            x_flip[...] = flip(x_ref[0])
            dn_ref[0] = dot_nt(dk_ref[0], w_ref[:, width : 2 * width])
            dn_ref[0] += dot_nt(dv_ref[0], w_ref[:, 2 * width :])
            dn_ref[0, 0:tok_rows, :] += dot_nt(dq_ref[0], w_ref[:, 0:width])
            acc[:, 0:width] += dot_nn(x_flip[:, 0:tok_rows], dq_ref[0])
            acc[:, width : 2 * width] += dot_nn(x_flip[...], dk_ref[0])
            acc[:, 2 * width :] += dot_nn(x_flip[...], dv_ref[0])

        @pl.when(at == slots - 1)
        def _():
            if flat is None:
                gw_ref[...] = acc[...].astype(BF16)
            else:
                stage[...] = acc[...].astype(BF16)
                copy_all(n[1], (keep_ref, send_ref), stage, flat, 0, sems)

    keys = slot(key_rows, width)
    args = (normed, d_q, d_k, d_v, w_qkv)
    specs = [keys, slot(tok_rows, width), keys, keys, whole(*w_qkv.shape)]
    scratch = [pltpu.VMEM((width, key_rows), BF16), pltpu.VMEM(w_qkv.shape, F32)]
    grads, alias = [(w_qkv.shape, BF16, result(*w_qkv.shape))], ()
    if flat is not None:
        args, specs, grads = args + kept, specs + [pl.BlockSpec(memory_space=pl.ANY)] * 2, bundles(flat, 2)
        scratch += [pltpu.VMEM(w_qkv.shape, BF16), copy_semaphores(flat, 0)]
        alias = ((5, 1), (6, 2))
    return run(
        "qkv_back",
        body,
        (slots,),
        live,
        args,
        specs,
        [(normed.shape, F32, keys)] + grads,
        scratch,
        after=after,
        alias=alias,
    )


def tokens_back(live, tokens, d_norm, arrived, d_residual, gains, after):
    slots, tok_rows, width = tokens.shape

    def body(n, x_ref, dn_ref, more_ref, dres_ref, g_ref, out_ref, sums_ref):
        at = pl.program_id(0)

        @pl.when(at == 0)
        def _():
            sums_ref[...] = jnp.zeros(sums_ref.shape, F32)

        @pl.when(at < n[0])
        def _():
            def back(rows):
                value, inverse = unit(x_ref[0, rows, :].astype(F32))
                e = dn_ref[0, rows, :] + more_ref[0, rows, :].astype(F32)
                sums_ref[0:1, :] += col_sum(e * value)
                sums_ref[1:2, :] += col_sum(e)
                grad = dres_ref[0, rows, :] + unit_back(value, inverse, e * g_ref[0:1, :])
                out_ref[0, rows, :] = grad.astype(BF16)

            over_rows(tok_rows, back)

        @pl.when(at >= n[0])
        def _():
            out_ref[...] = jnp.zeros(out_ref.shape, BF16)

    one = slot(tok_rows, width)
    return run(
        "tokens_back",
        body,
        (slots,),
        live,
        (tokens, d_norm, arrived, d_residual, gains),
        [one, one, one, one, whole(*gains.shape)],
        [
            (tokens.shape, BF16, every_slot(tok_rows, width)),
            ((8, width), F32, result(8, width)),
        ],
        after=after,
    )


def stage_rows(frame, top_ref, mid_ref, bottom_ref, lanes):
    rows, cols = mid_ref.shape[1], mid_ref.shape[2]
    inside = slice(EDGE, EDGE + cols)
    frame[0:REACH, inside, :] = top_ref[0, :, :, lanes].astype(F32)
    frame[REACH : REACH + rows, inside, :] = mid_ref[0, :, :, lanes].astype(F32)
    frame[REACH + rows :, inside, :] = bottom_ref[0, :, :, lanes].astype(F32)


def depthwise_rows(frame, rows, cols, tap, flipped, emit):
    totals = {}
    for y in range(rows + 2 * REACH):
        for left in range(KS):
            shifted = frame[y, EDGE - REACH + left : EDGE - REACH + left + cols, :]
            for top in range(KS):
                out = y - top
                if 0 <= out < rows:
                    at = (KS - 1 - top) * KS + KS - 1 - left if flipped else top * KS + left
                    term = shifted * tap(at)
                    totals[out] = totals[out] + term if out in totals else term
        if y >= 2 * REACH:
            emit(y - 2 * REACH, totals.pop(y - 2 * REACH))


def conv_front(live, top, high, bottom, kernel, gains, shifts):
    slots, rows, cols, channels = high.shape
    cells = rows * cols

    def body(
        n, top_ref, mid_ref, bottom_ref, k_ref, g_ref, b_ref,
        spatial_ref, flip_ref, unit_ref, inv_ref, frame, middle,
    ):
        @pl.when(pl.program_id(0) < n[0])
        def _():
            frame[...] = jnp.zeros(frame.shape, F32)

            def tile(at, carry):
                lanes = lane_tile(at)
                stage_rows(frame, top_ref, mid_ref, bottom_ref, lanes)
                bias = b_ref[0:1, lanes]

                def emit(y, total):
                    middle[y * cols : (y + 1) * cols, lanes] = total + bias

                depthwise_rows(frame, rows, cols, lambda t: k_ref[t : t + 1, lanes], False, emit)
                return carry

            lax.fori_loop(0, channels // LANES, tile, 0)

            def norm(part):
                value, inverse = unit(middle[part, :])
                inv_ref[0, part, :] = inverse
                unit_ref[0, part, :] = value.astype(BF16)
                spatial_ref[0, part, :] = (value * g_ref[0:1, :] + b_ref[1:2, :]).astype(BF16)

            over_rows(cells, norm)
            flip_ref[0] = flip(spatial_ref[0])

    halo = slot(REACH, cols, channels)
    return run(
        "conv_front",
        body,
        (slots,),
        live,
        (top, high, bottom, kernel, gains, shifts),
        [halo, slot(rows, cols, channels), halo, whole(*kernel.shape)]
        + [whole(*gains.shape), whole(*shifts.shape)],
        [
            ((slots, cells, channels), BF16, slot(cells, channels)),
            ((slots, channels, cells), BF16, slot(channels, cells)),
            ((slots, cells, channels), BF16, slot(cells, channels)),
            ((slots, cells, 1), F32, slot(cells, 1)),
        ],
        [
            pltpu.VMEM((rows + 2 * REACH, cols + 2 * EDGE, LANES), F32),
            pltpu.VMEM((cells, channels), F32),
        ],
    )


def conv_mlp(live, spatial, high, w_pw1, w_pw2, gains):
    slots, cells, channels = spatial.shape
    hidden = w_pw1.shape[1]
    block = 1024
    steps = hidden // block

    def body(
        n, x_ref, high_ref, w1_ref, w2_ref, g_ref, act_ref, slope_ref, branch_ref, out_ref, acc
    ):
        at, step = pl.program_id(0), pl.program_id(1)

        @pl.when((at < n[0]) & (step == 0))
        def _():
            acc[...] = jnp.zeros(acc.shape, F32)

        @pl.when(at < n[0])
        def _():
            parts = [slice(0, cells // 2), slice(cells // 2, cells)]
            hidden_parts = [dot_nn(x_ref[0, rows, :], w1_ref[...]) for rows in parts]
            for rows, value in zip(parts, hidden_parts):
                act, slope = gelu_pair(value)
                act = act.astype(BF16)
                act_ref[0, rows, :] = act
                slope_ref[0, rows, :] = slope.astype(BF16)
                acc[rows, :] += dot_nn(act, w2_ref[...])

            @pl.when(step == steps - 1)
            def _():
                def close(rows):
                    branch = acc[rows, :]
                    branch_ref[0, rows, :] = branch.astype(BF16)
                    out_ref[0, rows, :] = (
                        high_ref[0, rows, :].astype(F32) + g_ref[1:2, :] * branch
                    ).astype(BF16)

                over_rows(cells, close)

        @pl.when((at >= n[0]) & (step == 0))
        def _():
            out_ref[...] = jnp.zeros(out_ref.shape, BF16)

    def held_step(i, j, n):
        return jnp.where(i < n[0], j, steps - 1)

    one = slot(cells, channels)
    hidden_block = pl.BlockSpec(
        (1, cells, block), lambda i, j, n: (held(i, n), 0, held_step(i, j, n))
    )
    return run(
        "conv_mlp",
        body,
        (slots, steps),
        live,
        (spatial, high, w_pw1, w_pw2, gains),
        [
            one,
            one,
            pl.BlockSpec((channels, block), lambda i, j, n: (0, held_step(i, j, n))),
            pl.BlockSpec((block, channels), lambda i, j, n: (held_step(i, j, n), 0)),
            whole(*gains.shape),
        ],
        [
            ((slots, cells, hidden), BF16, hidden_block),
            ((slots, cells, hidden), BF16, hidden_block),
            (spatial.shape, BF16, one),
            (spatial.shape, BF16, every_slot(cells, channels)),
        ],
        [pltpu.VMEM((cells, channels), F32)],
    )


def pool(live, high_out, bins, side):
    slots, cells, channels = high_out.shape
    tok_rows = bins.shape[0] - 2 * side

    def body(n, x_ref, p_ref, own_ref, before_ref, after_ref):
        @pl.when(pl.program_id(0) < n[0])
        def _():
            part = dot_nn(p_ref[...], x_ref[0])
            before_ref[0] = part[0:side].astype(BF16)
            own_ref[0] = part[side : side + tok_rows]
            after_ref[0] = part[side + tok_rows :].astype(BF16)

    return run(
        "pool",
        body,
        (slots,),
        live,
        (high_out, bins),
        [slot(cells, channels), whole(*bins.shape)],
        [
            ((slots, tok_rows, channels), F32, slot(tok_rows, channels)),
            ((slots, side, channels), BF16, slot(side, channels)),
            ((slots, side, channels), BF16, slot(side, channels)),
        ],
    )


def adapter(live, own, first, last, d_merged, w_pool, w_gate, after):
    slots, tok_rows, channels = own.shape
    side = first.shape[1]
    width = w_pool.shape[1]

    def body(
        n, own_ref, first_ref, last_ref, dm_ref, w_ref, gate_ref,
        lift_ref, dpool_ref, gw_ref, ggate_ref, acc,
    ):
        at = pl.program_id(0)

        @pl.when(at == 0)
        def _():
            acc[...] = jnp.zeros(acc.shape, F32)
            ggate_ref[...] = jnp.zeros(ggate_ref.shape, F32)

        @pl.when(at < n[0])
        def _():
            pooled_low = jnp.concatenate(
                [
                    own_ref[0, 0:side] + first_ref[0].astype(F32),
                    own_ref[0, side : tok_rows - side],
                    own_ref[0, tok_rows - side :] + last_ref[0].astype(F32),
                ],
                axis=0,
            ).astype(BF16)
            pooled = pooled_low.astype(F32)
            lifted = dot_nn(pooled_low, w_ref[...])
            logit = jnp.sum(pooled * gate_ref[...], axis=-1, keepdims=True)
            gate = 1.0 / (1.0 + jnp.exp(-logit))
            lift_ref[0] = gate * lifted
            d_top = dm_ref[0].astype(F32)
            d_logit = jnp.sum(d_top * lifted, axis=-1, keepdims=True) * gate * (1.0 - gate)
            d_lifted = (gate * d_top).astype(BF16)
            acc[...] += dot_tn(pooled_low, d_lifted)
            ggate_ref[0:1, :] += col_sum(d_logit * pooled)
            dpool_ref[0] = (dot_nt(d_lifted, w_ref[...]) + d_logit * gate_ref[...]).astype(BF16)

        @pl.when(at == slots - 1)
        def _():
            gw_ref[...] = acc[...].astype(BF16)

    edge = slot(side, channels)
    return run(
        "adapter",
        body,
        (slots,),
        live,
        (own, first, last, d_merged, w_pool, w_gate),
        [slot(tok_rows, channels), edge, edge, slot(tok_rows, width)]
        + [whole(*w_pool.shape), whole(*w_gate.shape)],
        [
            ((slots, tok_rows, width), F32, slot(tok_rows, width)),
            (own.shape, BF16, slot(tok_rows, channels)),
            (w_pool.shape, BF16, result(*w_pool.shape)),
            ((8, channels), F32, result(8, channels)),
        ],
        [pltpu.VMEM(w_pool.shape, F32)],
        after=after,
    )


def unpool(live, near, spread, d_conv, branch, gains):
    slots, near_rows, channels = near.shape
    cells = d_conv.shape[1]

    def body(n, near_ref, s_ref, dc_ref, branch_ref, g_ref, dpost_ref, dbranch_ref, sums_ref):
        at = pl.program_id(0)

        @pl.when(at == 0)
        def _():
            sums_ref[...] = jnp.zeros(sums_ref.shape, F32)

        @pl.when(at < n[0])
        def _():
            def part(rows):
                d_post = dc_ref[0, rows, :].astype(F32) + dot_nn(s_ref[rows, :], near_ref[0])
                sums_ref[0:1, :] += col_sum(d_post * branch_ref[0, rows, :].astype(F32))
                dpost_ref[0, rows, :] = d_post.astype(BF16)
                dbranch_ref[0, rows, :] = (g_ref[1:2, :] * d_post).astype(BF16)

            over_rows(cells, part)

    one = slot(cells, channels)
    return run(
        "unpool",
        body,
        (slots,),
        live,
        (near, spread, d_conv, branch, gains),
        [slot(near_rows, channels), whole(*spread.shape), one, one, whole(*gains.shape)],
        [
            (d_conv.shape, BF16, one),
            (d_conv.shape, BF16, one),
            ((8, channels), F32, result(8, channels)),
        ],
    )


def conv_second_grad(live, act, d_branch, grad_pool, flat):
    slots, cells, hidden = act.shape
    channels = d_branch.shape[2]
    block = 2 * BLOCK
    steps = hidden // block

    def body(n, act_ref, db_ref, pool_ref, *rest):
        step = pl.program_id(0)
        if flat is None:
            out_ref, acc = rest
        else:
            refs, (acc, stage, sems, pool_sems) = rest[:4], rest[4:]
        acc[...] = jnp.zeros(acc.shape, F32)

        def one(at, carry):
            acc[...] += dot_tn(act_ref[at], db_ref[at])
            return carry

        lax.fori_loop(0, n[0], one, 0)
        if flat is None:
            out_ref[...] = acc[...].astype(BF16)
            return

        def copies(at):
            out = []
            for k, row, rows, start, height in flat.within(1, at * block, block):
                for c in range(channels // BLOCK):
                    source = block_of(stage, row - at * block, rows, c)
                    out.append((k, source, start + c * height, rows))
            return out

        def pool_copies():
            out = []
            for k, row, rows, start in flat.pieces[2]:
                for c in range(flat.shapes[2][1] // BLOCK):
                    out.append((k, block_of(pool_ref, row, rows, c), start + c * rows, rows))
            return out

        def each(now, action):
            for static in range(steps):

                @pl.when(now == static)
                def _(static=static):
                    copy_out(n[1], refs, copies(static), sems, action)

        @pl.when(step == 0)
        def _():
            copy_out(n[1], refs, pool_copies(), pool_sems, "start")

        @pl.when(step > 0)
        def _():
            each(step - 1, "wait")

        stage[...] = acc[...].astype(BF16)
        each(step, "start")

        @pl.when(step == steps - 1)
        def _():
            each(step, "wait")
            copy_out(n[1], refs, pool_copies(), pool_sems, "wait")

    by_hidden = pl.BlockSpec((slots, cells, block), lambda j, n: (0, 0, j))
    scratch = [pltpu.VMEM((block, channels), F32)]
    if flat is None:
        by_row = pl.BlockSpec((block, channels), lambda j, n: (j, 0))
        grads = [((hidden, channels), BF16, by_row)]
    else:
        grads = bundles(flat, 4)
        most = max(len(flat.within(1, at * block, block)) for at in range(steps))
        scratch += [
            pltpu.VMEM((block, channels), BF16),
            pltpu.SemaphoreType.DMA((most * channels // BLOCK,)),
            copy_semaphores(flat, 2),
        ]
    return run(
        "conv_second_grad",
        body,
        (steps,),
        live,
        (act, d_branch, grad_pool),
        [by_hidden, whole(*d_branch.shape), pl.BlockSpec(memory_space=pl.ANY)],
        grads,
        scratch,
    )


def conv_mlp_back(live, spatial_flip, slope, d_branch, w_pw1, w_pw2, flat, kept, after):
    slots, channels, cells = spatial_flip.shape
    hidden = w_pw1.shape[1]
    block = 2 * BLOCK
    steps = hidden // block

    def body(n, xt_ref, slope_ref, db_ref, w1_ref, w2_ref, *rest):
        step = pl.program_id(0)
        if flat is None:
            dsp_ref, out_ref, acc, dsp, sem = rest
        else:
            dsp_ref, refs, (acc, dsp, sem, stage, sems) = rest[2], rest[3:5], rest[5:]

        @pl.when(step == 0)
        def _():
            dsp[...] = jnp.zeros(dsp.shape, F32)

        acc[...] = jnp.zeros(acc.shape, F32)

        def one(at, carry):
            d_hidden = dot_nt(db_ref[at], w2_ref[...])
            d_expand = (slope_ref[at].astype(F32) * d_hidden).astype(BF16)
            acc[...] += dot_nn(xt_ref[at], d_expand)
            dsp[at] += dot_nt(d_expand, w1_ref[...])
            return carry

        lax.fori_loop(0, n[0], one, 0)

        @pl.when(step == steps - 1)
        def _():
            out = pltpu.make_async_copy(dsp, dsp_ref, sem)
            out.start()
            out.wait()

        if flat is None:
            out_ref[...] = acc[...].astype(BF16)
            return

        def each(at, action):
            copies = []
            for index, (k, _, rows, start) in enumerate(flat.pieces[0]):
                place = pl.multiple_of(start + at * 2 * rows, 16)
                copies.append((k, stage.at[index, pl.ds(0, 2 * rows), :], place, 2 * rows))
            copy_out(n[1], refs, copies, sems, action)

        @pl.when(step > 0)
        def _():
            each(step - 1, "wait")

        for index, (_, row, rows, _) in enumerate(flat.pieces[0]):
            part = acc[row : row + rows, :]
            both = jnp.concatenate([part[:, 0:BLOCK], part[:, BLOCK:]], axis=0)
            stage[index, 0 : 2 * rows, :] = both.astype(BF16)
        each(step, "start")

        @pl.when(step == steps - 1)
        def _():
            each(step, "wait")

    by_col = pl.BlockSpec((channels, block), lambda j, n: (0, j))
    by_row = pl.BlockSpec((block, channels), lambda j, n: (j, 0))
    by_hidden = pl.BlockSpec((slots, cells, block), lambda j, n: (0, 0, j))
    anywhere = pl.BlockSpec(memory_space=pl.ANY)
    wide = (slots, cells, channels)
    scratch = [
        pltpu.VMEM((channels, block), F32),
        pltpu.VMEM(wide, F32),
        pltpu.SemaphoreType.DMA,
    ]
    args = (spatial_flip, slope, d_branch, w_pw1, w_pw2)
    specs = [whole(*spatial_flip.shape), by_hidden, whole(*wide), by_col, by_row]
    grads, alias = [(w_pw1.shape, BF16, by_col)], ()
    if flat is not None:
        args, specs, grads = args + kept, specs + [anywhere] * 2, bundles(flat, 2)
        alias = ((5, 1), (6, 2))
        tall = max(rows for _, _, rows, _ in flat.pieces[0])
        scratch += [
            pltpu.VMEM((len(flat.pieces[0]), 2 * tall, BLOCK), BF16),
            pltpu.SemaphoreType.DMA((len(flat.pieces[0]),)),
        ]
    return run(
        "conv_mlp_back",
        body,
        (steps,),
        live,
        args,
        specs,
        [(wide, F32, anywhere)] + grads,
        scratch,
        after=after,
        alias=alias,
    )


def conv_norm_back(live, d_spatial, unit_values, inverse, gains, after):
    slots, cells, channels = d_spatial.shape

    def body(n, e_ref, u_ref, inv_ref, g_ref, out_ref, sums_ref):
        at = pl.program_id(0)

        @pl.when(at == 0)
        def _():
            sums_ref[...] = jnp.zeros(sums_ref.shape, F32)

        @pl.when(at < n[0])
        def _():
            def part(rows):
                e = e_ref[0, rows, :]
                value = u_ref[0, rows, :].astype(F32)
                sums_ref[0:1, :] += col_sum(e * value)
                sums_ref[1:2, :] += col_sum(e)
                grad = unit_back(value, inv_ref[0, rows, :], e * g_ref[0:1, :])
                sums_ref[2:3, :] += col_sum(grad)
                out_ref[0, rows, :] = grad.astype(BF16)

            over_rows(cells, part)

    one = slot(cells, channels)
    return run(
        "conv_norm_back",
        body,
        (slots,),
        live,
        (d_spatial, unit_values, inverse, gains),
        [one, one, slot(cells, 1), whole(*gains.shape)],
        [(d_spatial.shape, BF16, one), ((8, channels), F32, result(8, channels))],
        after=after,
    )


def conv_back(live, d_top, d_mid, d_bottom, d_post, kernel, after):
    slots, rows, cols, channels = d_mid.shape

    def body(n, dt_ref, dm_ref, db_ref, dpost_ref, k_ref, out_ref, frame):
        at = pl.program_id(0)

        @pl.when(at < n[0])
        def _():
            frame[...] = jnp.zeros(frame.shape, F32)

            def tile(tile_at, carry):
                lanes = lane_tile(tile_at)
                stage_rows(frame, dt_ref, dm_ref, db_ref, lanes)

                def emit(y, total):
                    grad = total + dpost_ref[0, y, :, lanes].astype(F32)
                    out_ref[0, y, :, lanes] = grad.astype(BF16)

                depthwise_rows(frame, rows, cols, lambda t: k_ref[t : t + 1, lanes], True, emit)
                return carry

            lax.fori_loop(0, channels // LANES, tile, 0)

        @pl.when(at >= n[0])
        def _():
            out_ref[...] = jnp.zeros(out_ref.shape, BF16)

    halo = slot(REACH, cols, channels)
    one = slot(rows, cols, channels)
    return run(
        "conv_back",
        body,
        (slots,),
        live,
        (d_top, d_mid, d_bottom, d_post, kernel),
        [halo, one, halo, one, whole(*kernel.shape)],
        [(d_mid.shape, BF16, every_slot(rows, cols, channels))],
        [pltpu.VMEM((rows + 2 * REACH, cols + 2 * EDGE, LANES), F32)],
        after=after,
    )[0]


def kernel_back(live, top, high, bottom, d_mid, half, after):
    slots, rows, cols, channels = high.shape
    channels = channels // 2

    def body(n, top_ref, mid_ref, bottom_ref, dm_ref, gk_ref, frame, d_rows):
        at = pl.program_id(0)

        @pl.when(at == 0)
        def _():
            gk_ref[...] = jnp.zeros(gk_ref.shape, F32)

        @pl.when(at < n[0])
        def _():
            frame[...] = jnp.zeros(frame.shape, F32)

            def tile(tile_at, carry):
                lanes = lane_tile(tile_at)
                stage_rows(frame, top_ref, mid_ref, bottom_ref, lanes)
                d_rows[...] = dm_ref[0, :, :, lanes].astype(F32)
                for left in range(KS):
                    totals = [None] * KS
                    grads = {}
                    begin = EDGE - REACH + left
                    for y in range(rows + 2 * REACH):
                        shifted = frame[y, begin : begin + cols, :].reshape(cols // 8, 8, LANES)
                        if y < rows:
                            grads[y] = d_rows[y].reshape(cols // 8, 8, LANES)
                        for tap_row in range(KS):
                            row = y - tap_row
                            if 0 <= row < rows:
                                term = jnp.sum(shifted * grads[row], axis=0)
                                old = totals[tap_row]
                                totals[tap_row] = term if old is None else old + term
                        grads.pop(y - KS + 1, None)
                    for tap_row in range(KS):
                        tap = tap_row * KS + left
                        gk_ref[tap : tap + 1, lanes] += col_sum(totals[tap_row])
                return carry

            lax.fori_loop(0, channels // LANES, tile, 0)

    def half_slot(*shape):
        return pl.BlockSpec((1,) + shape, lambda i, n: (held(i, n), 0, 0, half))

    halo = half_slot(REACH, cols, channels)
    one = half_slot(rows, cols, channels)
    return run(
        "kernel_back",
        body,
        (slots,),
        live,
        (top, high, bottom, d_mid),
        [halo, one, halo, one],
        [((64, channels), F32, result(64, channels))],
        [
            pltpu.VMEM((rows + 2 * REACH, cols + 2 * EDGE, LANES), F32),
            pltpu.VMEM((rows, cols, LANES), F32),
        ],
        after=after,
    )[0]


def from_both_sides(head, tail):
    count = lax.axis_size("strip")
    if count == 2:
        upper = lax.axis_index("strip") == 0
        got = lax.ppermute(jnp.where(upper, tail, head), "strip", [(0, 1), (1, 0)])
        return jnp.where(upper, jnp.zeros_like(got), got), jnp.where(upper, got, jnp.zeros_like(got))
    before = lax.ppermute(tail, "strip", [(i, i + 1) for i in range(count - 1)])
    after = lax.ppermute(head, "strip", [(i + 1, i) for i in range(count - 1)])
    return before, after


def bin_weights(edges, cell_count):
    cells = jnp.arange(cell_count, dtype=jnp.int32)
    inside = (cells[None, :] >= edges[:-1, None]) & (cells[None, :] < edges[1:, None])
    widths = (edges[1:] - edges[:-1]).astype(F32)
    return inside.astype(F32) / widths[:, None]


def strip_bins(edges, first_bin, bin_count, first_cell, cell_count):
    padded = jnp.concatenate([edges[:1], edges, edges[-1:]])
    window = lax.dynamic_slice_in_dim(padded, first_bin + 1, bin_count + 1)
    cells = first_cell + jnp.arange(cell_count, dtype=jnp.int32)
    inside = (cells[None, :] >= window[:-1, None]) & (cells[None, :] < window[1:, None])
    widths = jnp.maximum(window[1:] - window[:-1], 1).astype(F32)
    return inside.astype(F32) / widths[:, None]


def bit_of(axis, bit):
    return (lax.axis_index(axis) >> bit) & 1


def swap_halves(cells, axis, bit, own):
    size = lax.axis_size(axis)
    keep = lax.dynamic_index_in_dim(cells, own, 1, keepdims=False)
    send = lax.dynamic_index_in_dim(cells, 1 - own, 1, keepdims=False)
    got = lax.ppermute(send, axis, [(i, i ^ (1 << bit)) for i in range(size)])
    return (keep.astype(F32) + got.astype(F32)).astype(BF16)


def sum_everywhere(values):
    for axis in ("dp", "strip"):
        size = lax.axis_size(axis)
        step = 1
        while step < size:
            values = values + lax.ppermute(values, axis, [(i, i ^ step) for i in range(size)])
            step *= 2
    return values


def bits(axis):
    return int(math.log2(lax.axis_size(axis)))


def halve_dp(cells, base, bit):
    if cells.shape[0] % 2:
        cells = jnp.pad(cells, [(0, 1)] + [(0, 0)] * (cells.ndim - 1))
    own = (bit_of("dp", bit) - base) & 1
    cells = cells.reshape((cells.shape[0] // 2, 2) + cells.shape[1:])
    return swap_halves(cells, "dp", bit, own), (base + own) >> 1


def halve_strip(cells):
    for bit in range(bits("strip")):
        m, count = cells.shape[:2]
        cells = cells.reshape((m * count // 2, 2) + cells.shape[2:])
        cells = swap_halves(cells, "strip", bit, bit_of("strip", bit))
        cells = cells.reshape((m, count // 2) + cells.shape[1:])
    return cells


def shared_sum(matrix, offset, chunk, strip_first):
    strips = lax.axis_size("strip")
    rows, cols = matrix.shape
    chunk_rows = chunk // cols
    base = offset // (chunk * strips)
    front = (offset - base * chunk * strips) // cols
    groups = -(-(front + rows) // (chunk_rows * strips))
    back = groups * chunk_rows * strips - front - rows
    cells = jnp.pad(matrix, ((front, back), (0, 0))).reshape(groups, strips, chunk_rows, cols)
    cells, base = halve_dp(cells, base, 0)
    if strip_first:
        cells = halve_strip(cells)
        cells, base = halve_dp(cells, base, 1)
    else:
        cells, base = halve_dp(cells, base, 1)
        cells = halve_strip(cells)
    return cells.reshape(cells.shape[0], chunk), base


def owned_chunk(matrices, extras):
    data_count = lax.axis_size("dp")
    strips = lax.axis_size("strip")
    devices = data_count * strips
    chunk = sum(m.size for m in matrices) // devices
    span = data_count // 4
    placed = None
    offset = 0
    for order, matrix in enumerate(matrices):
        part, base = shared_sum(matrix, offset, chunk, order % 2 == 0)
        canvas = jnp.zeros((span + part.shape[0], chunk), BF16)
        canvas = lax.dynamic_update_slice(canvas, part, (base, 0))[:span]
        placed = canvas if placed is None else placed + canvas
        offset += matrix.size
    for bit in range(2, bits("dp")):
        placed = placed.reshape(placed.shape[0] // 2, 2, chunk)
        placed = swap_halves(placed, "dp", bit, bit_of("dp", bit))
    return share_of(placed.reshape(chunk).astype(F32), chunk, extras)


STEPS = {
    "core": ("dp", 1, lambda dp, strip: dp & 1),
    "x": ("strip", 1, lambda dp, strip: strip & 1),
    "y": ("dp", 2, lambda dp, strip: (dp >> 1) & 1),
    "z": ("dp", 4, lambda dp, strip: ((dp >> 2) ^ (dp >> 3)) & 1),
    "far": ("dp", 12, lambda dp, strip: (dp >> 3) & 1),
}
ORDERS = (("x", "y", "z"), ("y", "z", "x"), ("z", "x", "y"))


def across(step, value):
    axis, flip_bits, _ = STEPS[step]
    return lax.ppermute(value, axis, [(i, i ^ flip_bits) for i in range(lax.axis_size(axis))])


ANYWHERE = pl.BlockSpec(memory_space=pl.ANY)


def relay(live, values, after=()):
    def body(_, *refs):
        pass

    outs = [(v.shape, v.dtype, ANYWHERE) for v in values]
    alias = tuple((i, i) for i in range(len(values)))
    specs = [ANYWHERE] * len(values)
    return run("relay", body, (1,), live, tuple(values), specs, outs, after=after, alias=alias)


def split_sum(flat, sets, level, after, through):
    parts = len(ORDERS)
    rows = flat.units // parts
    count = sets[0][0][0].shape[0] // 2
    own = [STEPS[order[level]][2](lax.axis_index("dp"), lax.axis_index("strip")) for order in ORDERS]
    bits = jnp.stack(own).astype(jnp.int32)
    specs, args = [], []
    for number, (kept, arrived) in enumerate(sets):
        for part, order in enumerate(ORDERS):
            left = [name for name in ("z", "y", "x") if name not in order[:level]]
            low = len(left) - 1 - left.index(order[level])

            for flipped in (0, 1):

                def place(i, bit, part=part, low=low, flipped=flipped, first=number * count):
                    i = jnp.clip(i - first, 0, count - 1)
                    mine = bit[part] ^ flipped
                    index = ((i >> low) << (low + 1)) | (mine << low) | (i & ((1 << low) - 1))
                    return index, part if level == 0 else 0, 0

                for source in (kept, arrived):
                    args.append(source[0 if level == 0 else part])
                    specs.append(pl.BlockSpec((1, rows, BLOCK), place))
    given = len(args)

    def body(_, *refs):
        outs = refs[given + len(through) :]
        for number in range(len(sets)):
            ins = refs[number * 4 * parts : (number + 1) * 4 * parts]

            @pl.when(pl.program_id(0) // count == number)
            def _(ins=ins):
                for at in range(2 * parts):
                    total = ins[2 * at][...].astype(F32) + ins[2 * at + 1][...].astype(F32)
                    outs[at][...] = total.astype(BF16)

    out = pl.BlockSpec((1, rows, BLOCK), lambda i, bit: (i, 0, 0))
    done = run(
        "split_sum",
        body,
        (len(sets) * count,),
        bits,
        tuple(args) + tuple(through),
        specs + [ANYWHERE] * len(through),
        [((len(sets) * count, rows, BLOCK), BF16, out)] * (2 * parts)
        + [(v.shape, v.dtype, ANYWHERE) for v in through],
        after=after,
        alias=tuple((given + i, 2 * parts + i) for i in range(len(through))),
    )
    return done[0 : 2 * parts : 2], done[1 : 2 * parts : 2], done[2 * parts :]


class Bundle:
    def __init__(self, flat, kept, send):
        self.flat, self.level = flat, 0
        self.kept, self.arrived = [kept], [across("core", send)]

    def step(self, after, through=(), other=None):
        sets = [(b.kept, b.arrived) for b in (self, other) if b is not None]
        self.kept, sends, passed = split_sum(self.flat, sets, self.level, after, through)
        self.arrived = [across(order[self.level], v) for order, v in zip(ORDERS, sends)]
        self.level += 1
        return (self.kept[0],), passed

    def chunk(self):
        parts = [k.astype(F32) + a.astype(F32) for k, a in zip(self.kept, self.arrived)]
        low, high = jnp.concatenate(parts, axis=1).astype(BF16)
        is_upper = STEPS["far"][2](lax.axis_index("dp"), lax.axis_index("strip")) == 1
        got = across("far", jnp.where(is_upper, low, high))
        return jnp.where(is_upper, high, low).astype(F32) + got.astype(F32)


def row_major(flat, units):
    devices = lax.axis_size("dp") * lax.axis_size("strip")
    index = lax.axis_index("dp") * lax.axis_size("strip") + lax.axis_index("strip")
    kinds, kind_of = [], []
    for k in range(devices):
        kind = []
        for matrix, pieces in enumerate(flat.pieces):
            for chunk, _, rows, start in pieces:
                if chunk == k:
                    kind.append((start, rows, flat.shapes[matrix][1] // BLOCK))
        kind = tuple(kind)
        if kind not in kinds:
            kinds.append(kind)
        kind_of.append(kinds.index(kind))

    def ordered(kind):
        def branch(value):
            out = []
            for start, rows, blocks in kind:
                piece = value[start : start + rows * blocks].reshape(blocks, rows, BLOCK)
                out.append(piece.transpose(1, 0, 2).reshape(-1))
            return jnp.concatenate(out)

        return branch

    which = jnp.asarray(kind_of, jnp.int32)[index]
    return lax.switch(which, [ordered(kind) for kind in kinds], units)


def share_of(mine, chunk, extras):
    data_count = lax.axis_size("dp")
    strips = lax.axis_size("strip")
    devices = data_count * strips
    extra = extras.shape[0] // devices
    index = lax.axis_index("dp") * strips + lax.axis_index("strip")
    pieces = [mine]
    left = extras.shape[0]
    padded = jnp.pad(extras, (0, chunk))
    for hop in range(1, -(-left // chunk) + 1):
        size = min(left, chunk)
        left -= size
        following = lax.ppermute(
            mine[:size].astype(BF16),
            ("dp", "strip"),
            [(i + hop, i) for i in range(devices - hop)],
        ).astype(F32)
        past = index + hop - devices
        own_extras = lax.dynamic_slice(padded, (jnp.maximum(past, 0) * chunk,), (size,))
        pieces.append(jnp.where(past >= 0, own_extras, following))
    return lax.dynamic_slice(jnp.concatenate(pieces), (index * extra,), (chunk + extra,))


def per_device(
    low_tokens,
    high_map,
    counts,
    row_edges,
    col_edges,
    w_qkv,
    w_attn_out,
    w_fc1,
    w_fc2,
    vit_gains,
    vit_shifts,
    w_pw1,
    w_pw2,
    w_pool,
    dw_kernel,
    conv_gains,
    conv_shifts,
    w_gate,
    d_merged,
    d_conv,
):
    slots, tok_rows, width = low_tokens.shape
    rows, cols, channels = high_map.shape[1:]
    cells = rows * cols
    strips = lax.axis_size("strip")
    strip = lax.axis_index("strip")
    live = jnp.stack([counts[0], lax.axis_index("dp") & 1]).astype(jnp.int32)

    col_bins = bin_weights(col_edges, cols)
    side = col_bins.shape[0]
    own_bins = tok_rows // side
    near_bins = strip_bins(row_edges, strip * own_bins - 1, own_bins + 2, strip * rows, rows)
    bins = (near_bins[:, None, :, None] * col_bins[None, :, None, :]).astype(BF16)
    bins = bins.reshape((own_bins + 2) * side, cells)

    data_count = lax.axis_size("dp")
    devices = data_count * strips
    vit_flat = Flat([w.shape for w in (w_qkv, w_attn_out, w_fc1, w_fc2)], devices)
    conv_flat = Flat([w.shape for w in (w_pw1, w_pw2, w_pool)], devices)
    chunked = devices == 4 * BUNDLE and strips == 2 and vit_flat.even and conv_flat.even
    if not chunked:
        vit_flat = conv_flat = None

    def over_cores(value):
        return lax.ppermute(value, "dp", [(i, i ^ 1) for i in range(data_count)])

    own_count = counts[0]
    lead = own_count - over_cores(counts)[0]
    lends, borrows = lead >= 2, lead <= -2
    last_slot = own_count - 1
    live = own_count - lends.astype(jnp.int32) + borrows.astype(jnp.int32)
    live = jnp.stack([live, lax.axis_index("dp") & 1]).astype(jnp.int32)

    def lent(values):
        return over_cores(lax.dynamic_index_in_dim(values, last_slot, 0))

    def with_lent(values, guest):
        place = jnp.arange(slots) == jnp.where(borrows, own_count, slots)
        return jnp.where(place.reshape((slots,) + (1,) * (values.ndim - 1)), guest, values)

    guest_slot = jnp.minimum(own_count, slots - 1)

    def sent_home(values):
        return over_cores(lax.dynamic_index_in_dim(values, guest_slot, 0))

    def returned(values, home):
        at = jnp.where(lends, last_slot, guest_slot)
        there = lax.dynamic_index_in_dim(values, at, 0)
        there = jnp.where(lends, home, jnp.where(borrows, jnp.zeros_like(there), there))
        return lax.dynamic_update_slice_in_dim(values, there, at, 0)

    def shifted(value, by):
        return lax.ppermute(value, "strip", [(i, (i + by) % strips) for i in range(strips)])

    guest_map = lent(high_map)
    halos = from_both_sides(high_map[:, :REACH], high_map[:, -REACH:])
    guest_halos = from_both_sides(guest_map[:, :REACH], guest_map[:, -REACH:])
    top, bottom = (with_lent(h, g) for h, g in zip(halos, guest_halos))
    high_map = with_lent(high_map, guest_map)
    low_tokens = with_lent(low_tokens, lent(low_tokens))
    d_merged = with_lent(d_merged, lent(d_merged))
    d_conv = with_lent(d_conv, lent(d_conv))
    (low_tokens,) = relay(live, (low_tokens,), (top, bottom))
    tok_all = jnp.concatenate(
        [low_tokens] + [shifted(low_tokens, by) for by in range(1, strips)], axis=1
    )

    spatial, spatial_flip, conv_unit, conv_inverse = conv_front(
        live, top, high_map, bottom, dw_kernel, conv_gains, conv_shifts
    )
    act, slope, branch, high_out = conv_mlp(
        live, spatial, high_map.reshape(slots, cells, channels), w_pw1, w_pw2, conv_gains
    )
    own, before_part, after_part = pool(live, high_out, bins, side)
    first, last = from_both_sides(before_part, after_part)
    (high_out,) = relay(live, (high_out,), (own,))
    high_home = sent_home(high_out)
    normed, q, kv, probs, mixed, residual, inner, inner_flip = vit_front(
        live, tok_all, w_qkv, w_attn_out, vit_gains, vit_shifts, tok_rows, (high_out,)
    )
    lift, d_pooled, grad_pool, gate_sums = adapter(
        live, own, first, last, d_merged, w_pool, w_gate.reshape(1, channels), (inner, high_home)
    )
    near_before, near_after = from_both_sides(d_pooled[:, :side], d_pooled[:, -side:])
    d_post, d_branch, scale_sums = unpool(
        live,
        jnp.concatenate([near_before, d_pooled, near_after], axis=1),
        bins.T,
        d_conv.reshape(slots, cells, channels),
        branch,
        conv_gains,
    )
    grads2 = conv_second_grad(live, act, d_branch, grad_pool, conv_flat)
    order = (grads2[0],)
    if chunked:
        conv_upper = Bundle(conv_flat, grads2[2], *relay(live, grads2[3:]))
    merged, d_inner, *grads_fc = vit_mlp(
        live, inner, inner_flip, d_merged, residual, lift, w_fc1, w_fc2, vit_flat, order
    )
    order = (d_inner,)
    if chunked:
        order, (merged, send) = conv_upper.step(order, (merged, grads_fc[3]))
        vit_upper = Bundle(vit_flat, grads_fc[2], send)
    merged_home = sent_home(merged)
    d_spatial, *grads1 = conv_mlp_back(
        live, spatial_flip, slope, d_branch, w_pw1, w_pw2, conv_flat, tuple(grads2[:2]), order
    )
    order = (d_spatial,)
    if chunked:
        order, passed = conv_upper.step(order + (merged_home,), grads1[1:])
        conv_lower = Bundle(conv_flat, grads1[0], *passed)
    d_conv_in, norm_sums = conv_norm_back(
        live, d_spatial, conv_unit, conv_inverse, conv_gains, order
    )
    d_residual, d_mixed, inner_sums, *grads_out = vit_back(
        live, residual, d_inner, d_merged, mixed, w_attn_out, vit_gains, vit_flat,
        tuple(grads_fc[:2]), (d_conv_in,),
    )
    order = (d_mixed,)
    if chunked:
        order, (d_conv_in,) = conv_lower.step(order + tuple(conv_upper.arrived), (d_conv_in,))
    d_conv_in = d_conv_in.reshape(high_map.shape)
    d_before, d_after = from_both_sides(d_conv_in[:, :REACH], d_conv_in[:, -REACH:])
    d_q, d_k, d_v = attention_back(live, probs, q, kv, d_mixed, order)
    order = (d_q,)
    if chunked:
        order, _ = vit_upper.step(order + tuple(conv_lower.arrived) + (d_before, d_after))
    d_normed, *grads_qkv = qkv_back(
        live, normed, d_q, d_k, d_v, w_qkv, vit_flat, tuple(grads_out), order
    )
    order = (d_normed,)
    if chunked:
        order += tuple(vit_upper.arrived)
        order, passed = conv_lower.step(order, (grads_qkv[1], d_normed))
        vit_lower = Bundle(vit_flat, grads_qkv[0], passed[0])
        d_normed = passed[1]
    d_other = jnp.zeros(low_tokens.shape, BF16)
    for by in range(1, strips):
        part = d_normed[:, by * tok_rows : (by + 1) * tok_rows].astype(BF16)
        d_other = d_other + shifted(part, -by) if by > 1 else shifted(part, -by)
    grad_map = conv_back(
        live, d_before, d_conv_in, d_after, d_post.reshape(high_map.shape), dw_kernel, order
    )
    order = (grad_map,)
    if chunked:
        order += tuple(vit_lower.arrived)
        order, (grad_map,) = conv_lower.step(order, (grad_map,), conv_upper)
    map_home = sent_home(grad_map)
    kernel_sums = [kernel_back(live, top, high_map, bottom, d_conv_in, 0, order)]
    grad_tokens, token_sums = tokens_back(
        live, low_tokens, d_normed, d_other, d_residual, vit_gains, (kernel_sums[0],)
    )
    order = (grad_tokens,)
    if chunked:
        order, _ = vit_lower.step(order + tuple(conv_lower.arrived) + (map_home,))
    kernel_sums.append(kernel_back(live, top, high_map, bottom, d_conv_in, 1, order))
    order = tuple(vit_lower.arrived) if chunked else ()
    kernel_sums = jnp.concatenate(relay(live, kernel_sums, order), axis=1)

    vit_extras = jnp.concatenate([token_sums[0], inner_sums[0], token_sums[1], inner_sums[1]])
    conv_extras = jnp.concatenate(
        [
            kernel_sums[: KS * KS].reshape(-1),
            norm_sums[0],
            scale_sums[0],
            norm_sums[2],
            norm_sums[1],
            gate_sums[0],
        ]
    )
    extras = sum_everywhere(jnp.concatenate([vit_extras, conv_extras]))
    vit_extras, conv_extras = extras[: vit_extras.shape[0]], extras[vit_extras.shape[0] :]
    if chunked:
        order, _ = vit_lower.step((kernel_sums,), (), vit_upper)
        conv_mine = row_major(conv_flat, conv_lower.chunk())
        conv_out = share_of(conv_mine, conv_flat.chunk, conv_extras)
        vit_lower.step(order)
        vit_mine = row_major(vit_flat, vit_lower.chunk())
        vit_out = share_of(vit_mine, vit_flat.chunk, vit_extras)
    else:
        vit_out = owned_chunk([*grads_qkv, *grads_out, *grads_fc], vit_extras)
        conv_out = owned_chunk([*grads1, *grads2, grad_pool], conv_extras)
    return (
        returned(merged, merged_home),
        returned(high_out, high_home).reshape(high_map.shape),
        returned(grad_tokens, sent_home(grad_tokens)),
        returned(grad_map, map_home),
        vit_out,
        conv_out,
    )


def solution(mesh):
    images = P("dp", "strip", None)
    maps = P("dp", "strip", None, None)
    flat = P(("dp", "strip"))
    in_specs = (images, maps, P("dp")) + (P(),) * 15 + (images, maps)
    out_specs = (images, maps, images, maps, flat, flat)
    return jax.shard_map(
        per_device, mesh=mesh, in_specs=in_specs, out_specs=out_specs, check_vma=False
    )
```

```python
import math

import jax
import jax.numpy as jnp
from jax import lax
from jax.experimental import pallas as pl
from jax.experimental.pallas import tpu as pltpu
from jax.sharding import PartitionSpec as P

HEADS = 16
KS = 7
REACH = KS // 2
EPSILON = 1e-05
LANES = 128
EDGE = 8
BLOCK = 256
BUNDLE = 8
F32 = jnp.float32
BF16 = jnp.bfloat16
VMEM_BYTES = 60 * 1024 * 1024


def dot_nn(a, b):
    return jnp.dot(a, b, preferred_element_type=F32)


def dot_nt(a, b):
    return lax.dot_general(a, b, (((1,), (1,)), ((), ())), preferred_element_type=F32)


def dot_tn(a, b):
    return lax.dot_general(a, b, (((0,), (0,)), ((), ())), preferred_element_type=F32)


def flip(value):
    return value.astype(F32).T.astype(BF16)


def row_step(rows):
    for step in (128, 96, 64, 48, 32, 16):
        if rows % step == 0:
            return step
    return rows


def over_rows(rows, body):
    step = row_step(rows)

    def one(at, carry):
        body(pl.ds(pl.multiple_of(at * step, step), step))
        return carry

    if step == rows:
        body(pl.ds(0, rows))
    else:
        lax.fori_loop(0, rows // step, one, 0)


def lane_tile(at):
    return pl.ds(pl.multiple_of(at * LANES, LANES), LANES)


def unit(values):
    center = values - jnp.mean(values, axis=-1, keepdims=True)
    inverse = lax.rsqrt(jnp.mean(center * center, axis=-1, keepdims=True) + EPSILON)
    return center * inverse, inverse


def unit_back(unit_values, inverse, grad):
    return (
        grad
        - jnp.mean(grad, axis=-1, keepdims=True)
        - unit_values * jnp.mean(grad * unit_values, axis=-1, keepdims=True)
    ) * inverse


def gelu_pair(x):
    scale = math.sqrt(2.0 / math.pi)
    square = x * x
    bend = jnp.tanh(x * (scale + (scale * 0.044715) * square))
    half = 0.5 + 0.5 * bend
    slope = half + (0.5 * x) * (1.0 - bend * bend) * (scale + (3.0 * scale * 0.044715) * square)
    return x * half, slope


def col_sum(values):
    return jnp.sum(values, axis=0, keepdims=True)


ANYWHERE = pl.BlockSpec(memory_space=pl.ANY)


def held(at, live):
    return jnp.maximum(jnp.minimum(at, live[0] - 1), 0)


def slot(*shape):
    return pl.BlockSpec(
        (1,) + shape, lambda *g: (held(g[0], g[-1]),) + (0,) * len(shape)
    )


def every_slot(*shape):
    return pl.BlockSpec((1,) + shape, lambda *g: (g[0],) + (0,) * len(shape))


def whole(*shape):
    return pl.BlockSpec(shape, lambda *g: (0,) * len(shape), pipeline_mode=pl.Buffered(1))


def result(*shape):
    return pl.BlockSpec(shape, lambda *g: (0,) * len(shape))


def run(name, body, grid, live, args, in_specs, outs, scratch=(), after=(), alias=()):
    out_shape = [jax.ShapeDtypeStruct(shape, dtype) for shape, dtype, _ in outs]
    count = 1 + len(args)

    def without_order(*refs):
        body(*refs[:count], *refs[count + len(after) :])

    return pl.pallas_call(
        without_order,
        grid_spec=pltpu.PrefetchScalarGridSpec(
            num_scalar_prefetch=1,
            grid=grid,
            in_specs=list(in_specs) + [pl.BlockSpec(memory_space=pl.ANY)] * len(after),
            out_specs=[spec for _, _, spec in outs],
            scratch_shapes=list(scratch),
        ),
        out_shape=out_shape,
        input_output_aliases={1 + given: out for given, out in alias},
        compiler_params=pltpu.CompilerParams(
            dimension_semantics=("arbitrary",) * len(grid), vmem_limit_bytes=VMEM_BYTES
        ),
        cost_estimate=pl.CostEstimate(flops=0, bytes_accessed=0, transcendentals=0),
        name=name,
    )(live, *args, *after)


class Flat:
    def __init__(self, shapes, devices):
        self.shapes = shapes
        self.chunk = sum(r * c for r, c in shapes) // devices
        self.units = self.chunk // BLOCK
        self.pieces = []
        self.even = sum(r * c for r, c in shapes) % (devices * BLOCK * 3 * 16) == 0
        offset = 0
        for rows, cols in shapes:
            self.even &= self.chunk % cols == 0 and offset % cols == 0 and cols % BLOCK == 0
            found = []
            if self.even:
                height, begin = self.chunk // cols, offset // cols
                for k in range(devices):
                    low = max(k * height, begin)
                    high = min((k + 1) * height, begin + rows)
                    if low < high:
                        start = (low - k * height) * (cols // BLOCK)
                        found.append((k, low - begin, high - low, start))
                        self.even &= (high - low) % 8 == 0 and start % 16 == 0
                self.even &= bool(self.pieces) or found[-1][0] < 2 * BUNDLE
            self.pieces.append(found)
            offset += rows * cols

    def within(self, matrix, first, count):
        out = []
        for k, row, height, start in self.pieces[matrix]:
            low, high = max(row, first), min(row + height, first + count)
            if low < high:
                out.append((k, low, high - low, start + low - row, height))
        return out


def side_of(chunk):
    z1, z0, y = (chunk >> 4) & 1, (chunk >> 3) & 1, (chunk >> 2) & 1
    return z1, (chunk >> 1) & 1, (z0 ^ z1) * 4 + y * 2 + (chunk & 1)


def copy_out(own_core, refs, copies, sems, action):
    for at, (chunk, source, place, rows) in enumerate(copies):
        upper, core, index = side_of(chunk)
        for held_here, ref in ((True, refs[2 * upper]), (False, refs[2 * upper + 1])):

            @pl.when((own_core == core) == held_here)
            def _(ref=ref, at=at, source=source, place=place, rows=rows, index=index):
                target = ref.at[index, pl.ds(place, rows), :]
                getattr(pltpu.make_async_copy(source, target, sems.at[at]), action)()


def copy_all(own_core, refs, stage, flat, matrix, sems):
    copies = []
    for k, row, rows, start in flat.pieces[matrix]:
        for c in range(stage.shape[1] // BLOCK):
            copies.append((k, block_of(stage, row, rows, c), start + c * rows, rows))
    copy_out(own_core, refs, copies, sems, "start")
    copy_out(own_core, refs, copies, sems, "wait")


def copy_semaphores(flat, matrix):
    return pltpu.SemaphoreType.DMA((len(flat.pieces[matrix]) * flat.shapes[matrix][1] // BLOCK,))


def bundles(flat, count):
    shape = (BUNDLE, flat.units, BLOCK)
    return [(shape, BF16, pl.BlockSpec(memory_space=pl.ANY))] * count


def block_of(ref, first, rows, block):
    return ref.at[pl.ds(first, rows), pl.ds(block * BLOCK, BLOCK)]


def vit_front(live, tok_all, w_qkv, w_out, gains, shifts, tok_rows, after):
    slots, key_rows, width = tok_all.shape
    head = width // HEADS
    pairs = width // LANES
    per_tile = LANES // head

    def body(
        n, x_ref, wq_ref, wo_ref, g_ref, b_ref,
        normed_ref, q_ref, kv_ref, probs_ref, mixed_ref, res_ref, inner_ref, flip_ref,
    ):
        @pl.when(pl.program_id(0) < n[0])
        def _():
            def first_norm(rows):
                value, _ = unit(x_ref[0, rows, :].astype(F32))
                normed_ref[0, rows, :] = (value * g_ref[0:1, :] + b_ref[0:1, :]).astype(BF16)

            over_rows(key_rows, first_norm)
            q_ref[0] = dot_nn(normed_ref[0, 0:tok_rows, :], wq_ref[:, 0:width]).astype(BF16)
            for part in range(4):
                cols = slice(part * width // 2, (part + 1) * width // 2)
                w_cols = slice(width + cols.start, width + cols.stop)
                kv_ref[0, :, cols] = dot_nn(normed_ref[0], wq_ref[:, w_cols]).astype(BF16)

            lane = lax.broadcasted_iota(jnp.int32, (1, LANES), 1) // head

            def heads(pair, carry):
                q = q_ref[0, :, lane_tile(pair)] * jnp.asarray(1.0 / math.sqrt(head), BF16)
                k = kv_ref[0, :, lane_tile(pair)].astype(F32)
                v_flip = flip(kv_ref[0, :, lane_tile(pairs + pair)])
                mixed = []
                for h in range(per_tile):
                    scores = dot_nt(jnp.where(lane == h, k, 0.0).astype(BF16), q)
                    top = jnp.max(scores, axis=0, keepdims=True)
                    raised = jnp.exp(scores - top)
                    probs = (raised * (1.0 / col_sum(raised))).astype(BF16)
                    probs_ref[0, pair * per_tile + h] = probs
                    mixed.append(dot_nn(v_flip[h * head : (h + 1) * head, :], probs))
                mixed_ref[0, :, lane_tile(pair)] = jnp.concatenate(mixed, axis=0).T.astype(BF16)
                return carry

            lax.fori_loop(0, pairs, heads, 0)
            res_ref[0] = dot_nn(mixed_ref[0], wo_ref[...])

            def second_norm(rows):
                res = res_ref[0, rows, :] + x_ref[0, rows, :].astype(F32)
                res_ref[0, rows, :] = res
                value, _ = unit(res)
                inner_ref[0, rows, :] = (value * g_ref[1:2, :] + b_ref[1:2, :]).astype(BF16)

            over_rows(tok_rows, second_norm)
            flip_ref[0] = flip(inner_ref[0])

    return run(
        "vit_front",
        body,
        (slots,),
        live,
        (tok_all, w_qkv, w_out, gains, shifts),
        [slot(key_rows, width), whole(*w_qkv.shape), whole(*w_out.shape)]
        + [whole(*gains.shape), whole(*shifts.shape)],
        [
            ((slots, key_rows, width), BF16, slot(key_rows, width)),
            ((slots, tok_rows, width), BF16, slot(tok_rows, width)),
            ((slots, key_rows, 2 * width), BF16, slot(key_rows, 2 * width)),
            ((slots, HEADS, key_rows, tok_rows), BF16, slot(HEADS, key_rows, tok_rows)),
            ((slots, tok_rows, width), BF16, slot(tok_rows, width)),
            ((slots, tok_rows, width), F32, slot(tok_rows, width)),
            ((slots, tok_rows, width), BF16, slot(tok_rows, width)),
            ((slots, width, tok_rows), BF16, slot(width, tok_rows)),
        ],
        after=after,
    )


def vit_mlp(live, inner, inner_flip, d_mlp, residual, lift, w_fc1, w_fc2, flat, after):
    slots, tok_rows, width = inner.shape
    hidden = w_fc1.shape[1]
    block = 512
    steps = hidden // block
    blocks = width // BLOCK

    def body(
        n, x_ref, xt_ref, dm_ref, res_ref, lift_ref, w1_ref, w2_ref,
        merged_ref, din_ref, *rest,
    ):
        if flat is None:
            out1_ref, out2_ref, low, a1, a2 = rest
        else:
            refs, (low, a1, a2, stage1, stage2, sems1, sems2) = rest[:4], rest[4:]
        step = pl.program_id(0)

        @pl.when(step == 0)
        def _():
            low[...] = res_ref[...]
            din_ref[...] = jnp.zeros(din_ref.shape, F32)

        a1[...] = jnp.zeros(a1.shape, F32)
        a2[...] = jnp.zeros(a2.shape, F32)

        def one(at, carry):
            before = dot_nn(x_ref[at], w1_ref[...])
            d_act = dot_nt(dm_ref[at], w2_ref[...])
            act, slope = gelu_pair(before)
            act = act.astype(BF16)
            d_fc = (slope * d_act).astype(BF16)
            low[at] += dot_nn(act, w2_ref[...])
            a2[...] += dot_tn(act, dm_ref[at])
            a1[...] += dot_nn(xt_ref[at], d_fc)
            din_ref[at] += dot_nt(d_fc, w1_ref[...])
            return carry

        lax.fori_loop(0, n[0], one, 0)

        @pl.when(step == steps - 1)
        def _():
            def close(at, carry):
                merged_ref[at] = (low[at] + lift_ref[at]).astype(BF16)
                return carry

            def blank(at, carry):
                merged_ref[at] = jnp.zeros(merged_ref.shape[1:], BF16)
                return carry

            lax.fori_loop(0, n[0], close, 0)
            lax.fori_loop(n[0], slots, blank, 0)

        if flat is None:
            out1_ref[...] = a1[...].astype(BF16)
            out2_ref[...] = a2[...].astype(BF16)
            return

        def first_copies(at):
            out = []
            for c in range(block // BLOCK):
                for k, row, rows, start, height in flat.within(2, 0, width):
                    place = start + (at * (block // BLOCK) + c) * height
                    out.append((k, block_of(stage1, row, rows, c), pl.multiple_of(place, 16), rows))
            return out

        def second_copies(at):
            out = []
            for k, row, rows, start, height in flat.within(3, at * block, block):
                for c in range(blocks):
                    source = block_of(stage2, row - at * block, rows, c)
                    out.append((k, source, start + c * height, rows))
            return out

        def each(at, now, action):
            copy_out(n[1], refs, first_copies(now), sems1, action)
            for static in range(steps):

                @pl.when(now == static)
                def _(static=static):
                    copy_out(n[1], refs, second_copies(static), sems2, action)

        @pl.when(step > 0)
        def _():
            each(step, step - 1, "wait")

        stage1[...] = a1[...].astype(BF16)
        stage2[...] = a2[...].astype(BF16)
        each(step, step, "start")

        @pl.when(step == steps - 1)
        def _():
            each(step, step, "wait")

    wide = (slots, tok_rows, width)
    by_col = pl.BlockSpec((width, block), lambda j, n: (0, j))
    by_row = pl.BlockSpec((block, width), lambda j, n: (j, 0))
    scratch = [
        pltpu.VMEM(wide, F32),
        pltpu.VMEM((width, block), F32),
        pltpu.VMEM((block, width), F32),
    ]
    if flat is None:
        grads = [(w_fc1.shape, BF16, by_col), (w_fc2.shape, BF16, by_row)]
    else:
        grads = bundles(flat, 4)
        most = max(len(flat.within(3, at * block, block)) for at in range(steps))
        scratch += [
            pltpu.VMEM((width, block), BF16),
            pltpu.VMEM((block, width), BF16),
            pltpu.SemaphoreType.DMA((block // BLOCK * len(flat.pieces[2]),)),
            pltpu.SemaphoreType.DMA((most * blocks,)),
        ]
    return run(
        "vit_mlp",
        body,
        (steps,),
        live,
        (inner, inner_flip, d_mlp, residual, lift, w_fc1, w_fc2),
        [whole(*wide), whole(*inner_flip.shape)] + [whole(*wide)] * 3 + [by_col, by_row],
        [(wide, BF16, result(*wide)), (wide, F32, result(*wide))] + grads,
        scratch,
        after=after,
    )


def vit_back(live, residual, d_inner, d_merged, mixed, w_out, gains, flat, kept, after):
    slots, tok_rows, width = residual.shape

    def body(n, res_ref, din_ref, dm_ref, mix_ref, wo_ref, g_ref, *rest):
        if flat is None:
            dres_ref, dmix_ref, sums_ref, gout_ref, low, acc = rest
        else:
            _, _, dres_ref, dmix_ref, sums_ref, keep_ref, send_ref, low, acc, stage, sems = rest
        at = pl.program_id(0)

        @pl.when(at == 0)
        def _():
            acc[...] = jnp.zeros(acc.shape, F32)
            sums_ref[...] = jnp.zeros(sums_ref.shape, F32)

        @pl.when(at < n[0])
        def _():
            def back(rows):
                value, inverse = unit(res_ref[0, rows, :])
                e = din_ref[0, rows, :]
                sums_ref[0:1, :] += col_sum(e * value)
                sums_ref[1:2, :] += col_sum(e)
                d_res = dm_ref[0, rows, :].astype(F32) + unit_back(value, inverse, e * g_ref[1:2, :])
                dres_ref[0, rows, :] = d_res
                low[rows, :] = d_res.astype(BF16)

            over_rows(tok_rows, back)
            dmix_ref[0] = dot_nt(low[...], wo_ref[...]).astype(BF16)
            acc[...] += dot_tn(mix_ref[0], low[...])

        @pl.when(at == slots - 1)
        def _():
            if flat is None:
                gout_ref[...] = acc[...].astype(BF16)
            else:
                stage[...] = acc[...].astype(BF16)
                copy_all(n[1], (keep_ref, send_ref), stage, flat, 1, sems)

    wide = (slots, tok_rows, width)
    one = slot(tok_rows, width)
    args = (residual, d_inner, d_merged, mixed, w_out, gains)
    specs = [one, one, one, one, whole(*w_out.shape), whole(*gains.shape)]
    scratch = [pltpu.VMEM((tok_rows, width), BF16), pltpu.VMEM(w_out.shape, F32)]
    grads, alias = [(w_out.shape, BF16, result(*w_out.shape))], ()
    if flat is not None:
        args, specs, grads = args + kept, specs + [pl.BlockSpec(memory_space=pl.ANY)] * 2, bundles(flat, 2)
        scratch += [pltpu.VMEM(w_out.shape, BF16), copy_semaphores(flat, 1)]
        alias = ((6, 3), (7, 4))
    return run(
        "vit_back",
        body,
        (slots,),
        live,
        args,
        specs,
        [(wide, F32, one), (wide, BF16, one), ((8, width), F32, result(8, width))] + grads,
        scratch,
        after=after,
        alias=alias,
    )


def attention_back(live, probs, q, kv, d_mixed, after):
    slots, _, key_rows, tok_rows = probs.shape
    width = q.shape[2]
    head = width // HEADS
    pairs = width // LANES
    per_tile = LANES // head
    scale = 1.0 / math.sqrt(head)

    def body(n, p_ref, q_ref, k_ref, v_ref, dm_ref, dq_ref, dk_ref, dv_ref):
        @pl.when(pl.program_id(0) < n[0])
        def _():
            lane = lax.broadcasted_iota(jnp.int32, (1, LANES), 1) // head
            q = q_ref[0].astype(F32) * scale
            v = v_ref[0].astype(F32)
            dm = dm_ref[0].astype(F32)
            dm_low = dm_ref[0]
            k_flip = flip(k_ref[0].astype(F32) * scale)
            d_keys = jnp.zeros((key_rows, LANES), F32)
            d_values = jnp.zeros((key_rows, LANES), F32)
            d_query = []
            for h in range(per_tile):
                own = lane == h
                probs_low = p_ref[0, h]
                d_probs = dot_nt(jnp.where(own, v, 0.0).astype(BF16), dm_low)
                d_values += dot_nn(probs_low, jnp.where(own, dm, 0.0).astype(BF16))
                wide = probs_low.astype(F32)
                d_scores = (wide * (d_probs - col_sum(wide * d_probs))).astype(BF16)
                d_keys += dot_nn(d_scores, jnp.where(own, q, 0.0).astype(BF16))
                d_query.append(dot_nn(k_flip[h * head : (h + 1) * head, :], d_scores))
            dq_ref[0] = jnp.concatenate(d_query, axis=0).T.astype(BF16)
            dk_ref[0] = d_keys.astype(BF16)
            dv_ref[0] = d_values.astype(BF16)

    def held_pair(i, p, n):
        return jnp.where(i < n[0], p, pairs - 1)

    def at_pair(rows, shift=0):
        return pl.BlockSpec(
            (1, rows, LANES), lambda i, p, n: (held(i, n), 0, held_pair(i, p, n) + shift)
        )

    own = at_pair(tok_rows)
    keys = at_pair(key_rows)
    return run(
        "attention_back",
        body,
        (slots, pairs),
        live,
        (probs, q, kv, kv, d_mixed),
        [
            pl.BlockSpec(
                (1, per_tile, key_rows, tok_rows),
                lambda i, p, n: (held(i, n), held_pair(i, p, n), 0, 0),
            ),
            own,
            keys,
            at_pair(key_rows, pairs),
            own,
        ],
        [
            (q.shape, BF16, own),
            ((slots, key_rows, width), BF16, keys),
            ((slots, key_rows, width), BF16, keys),
        ],
        after=after,
    )


def qkv_back(live, normed, d_q, d_k, d_v, w_qkv, flat, kept, after):
    slots, key_rows, width = normed.shape
    tok_rows = d_q.shape[1]

    def body(n, x_ref, dq_ref, dk_ref, dv_ref, w_ref, *rest):
        if flat is None:
            dn_ref, gw_ref, x_flip, acc = rest
        else:
            _, _, dn_ref, keep_ref, send_ref, x_flip, acc, stage, sems = rest
        at = pl.program_id(0)

        @pl.when(at == 0)
        def _():
            acc[...] = jnp.zeros(acc.shape, F32)

        @pl.when(at < n[0])
        def _():
            x_flip[...] = flip(x_ref[0])
            dn_ref[0] = dot_nt(dk_ref[0], w_ref[:, width : 2 * width])
            dn_ref[0] += dot_nt(dv_ref[0], w_ref[:, 2 * width :])
            dn_ref[0, 0:tok_rows, :] += dot_nt(dq_ref[0], w_ref[:, 0:width])
            acc[:, 0:width] += dot_nn(x_flip[:, 0:tok_rows], dq_ref[0])
            acc[:, width : 2 * width] += dot_nn(x_flip[...], dk_ref[0])
            acc[:, 2 * width :] += dot_nn(x_flip[...], dv_ref[0])

        @pl.when(at == slots - 1)
        def _():
            if flat is None:
                gw_ref[...] = acc[...].astype(BF16)
            else:
                stage[...] = acc[...].astype(BF16)
                copy_all(n[1], (keep_ref, send_ref), stage, flat, 0, sems)

    keys = slot(key_rows, width)
    args = (normed, d_q, d_k, d_v, w_qkv)
    specs = [keys, slot(tok_rows, width), keys, keys, whole(*w_qkv.shape)]
    scratch = [pltpu.VMEM((width, key_rows), BF16), pltpu.VMEM(w_qkv.shape, F32)]
    grads, alias = [(w_qkv.shape, BF16, result(*w_qkv.shape))], ()
    if flat is not None:
        args, specs, grads = args + kept, specs + [pl.BlockSpec(memory_space=pl.ANY)] * 2, bundles(flat, 2)
        scratch += [pltpu.VMEM(w_qkv.shape, BF16), copy_semaphores(flat, 0)]
        alias = ((5, 1), (6, 2))
    return run(
        "qkv_back",
        body,
        (slots,),
        live,
        args,
        specs,
        [(normed.shape, F32, keys)] + grads,
        scratch,
        after=after,
        alias=alias,
    )


def tokens_back(live, tokens, d_norm, arrived, d_residual, gains, after):
    slots, tok_rows, width = tokens.shape

    def body(n, x_ref, dn_ref, more_ref, dres_ref, g_ref, out_ref, sums_ref):
        at = pl.program_id(0)

        @pl.when(at == 0)
        def _():
            sums_ref[...] = jnp.zeros(sums_ref.shape, F32)

        @pl.when(at < n[0])
        def _():
            def back(rows):
                value, inverse = unit(x_ref[0, rows, :].astype(F32))
                e = dn_ref[0, rows, :] + more_ref[0, rows, :].astype(F32)
                sums_ref[0:1, :] += col_sum(e * value)
                sums_ref[1:2, :] += col_sum(e)
                grad = dres_ref[0, rows, :] + unit_back(value, inverse, e * g_ref[0:1, :])
                out_ref[0, rows, :] = grad.astype(BF16)

            over_rows(tok_rows, back)

        @pl.when(at >= n[0])
        def _():
            out_ref[...] = jnp.zeros(out_ref.shape, BF16)

    one = slot(tok_rows, width)
    return run(
        "tokens_back",
        body,
        (slots,),
        live,
        (tokens, d_norm, arrived, d_residual, gains),
        [one, one, one, one, whole(*gains.shape)],
        [
            (tokens.shape, BF16, every_slot(tok_rows, width)),
            ((8, width), F32, result(8, width)),
        ],
        after=after,
    )


def stage_rows(frame, top_ref, mid_ref, bottom_ref, lanes):
    rows, cols = mid_ref.shape[1], mid_ref.shape[2]
    inside = slice(EDGE, EDGE + cols)
    frame[0:REACH, inside, :] = top_ref[0, :, :, lanes].astype(F32)
    frame[REACH : REACH + rows, inside, :] = mid_ref[0, :, :, lanes].astype(F32)
    frame[REACH + rows :, inside, :] = bottom_ref[0, :, :, lanes].astype(F32)


def depthwise_rows(frame, rows, cols, tap, flipped, emit):
    totals = {}
    for y in range(rows + 2 * REACH):
        for left in range(KS):
            shifted = frame[y, EDGE - REACH + left : EDGE - REACH + left + cols, :]
            for top in range(KS):
                out = y - top
                if 0 <= out < rows:
                    at = (KS - 1 - top) * KS + KS - 1 - left if flipped else top * KS + left
                    term = shifted * tap(at)
                    totals[out] = totals[out] + term if out in totals else term
        if y >= 2 * REACH:
            emit(y - 2 * REACH, totals.pop(y - 2 * REACH))


def conv_front(live, top, high, bottom, kernel, gains, shifts, after):
    slots, rows, cols, channels = high.shape
    cells = rows * cols

    def body(
        n, top_ref, mid_ref, bottom_ref, k_ref, g_ref, b_ref,
        spatial_ref, flip_ref, unit_ref, inv_ref, frame, middle,
    ):
        @pl.when(pl.program_id(0) < n[0])
        def _():
            frame[...] = jnp.zeros(frame.shape, F32)

            def tile(at, carry):
                lanes = lane_tile(at)
                stage_rows(frame, top_ref, mid_ref, bottom_ref, lanes)
                bias = b_ref[0:1, lanes]

                def emit(y, total):
                    middle[y * cols : (y + 1) * cols, lanes] = total + bias

                depthwise_rows(frame, rows, cols, lambda t: k_ref[t : t + 1, lanes], False, emit)
                return carry

            lax.fori_loop(0, channels // LANES, tile, 0)

            def norm(part):
                value, inverse = unit(middle[part, :])
                inv_ref[0, part, :] = inverse
                unit_ref[0, part, :] = value.astype(BF16)
                spatial_ref[0, part, :] = (value * g_ref[0:1, :] + b_ref[1:2, :]).astype(BF16)

            over_rows(cells, norm)
            flip_ref[0] = flip(spatial_ref[0])

    halo = slot(REACH, cols, channels)
    return run(
        "conv_front",
        body,
        (slots,),
        live,
        (top, high, bottom, kernel, gains, shifts),
        [halo, slot(rows, cols, channels), halo, whole(*kernel.shape)]
        + [whole(*gains.shape), whole(*shifts.shape)],
        [
            ((slots, cells, channels), BF16, slot(cells, channels)),
            ((slots, channels, cells), BF16, slot(channels, cells)),
            ((slots, cells, channels), BF16, slot(cells, channels)),
            ((slots, cells, 1), F32, slot(cells, 1)),
        ],
        [
            pltpu.VMEM((rows + 2 * REACH, cols + 2 * EDGE, LANES), F32),
            pltpu.VMEM((cells, channels), F32),
        ],
        after=after,
    )


def conv_mlp(live, spatial, high, w_pw1, w_pw2, gains, after):
    slots, cells, channels = spatial.shape
    hidden = w_pw1.shape[1]
    block = 1024
    steps = hidden // block

    def body(
        n, x_ref, high_ref, w1_ref, w2_ref, g_ref, act_ref, slope_ref, branch_ref, out_ref, acc
    ):
        at, step = pl.program_id(0), pl.program_id(1)

        @pl.when((at < n[0]) & (step == 0))
        def _():
            acc[...] = jnp.zeros(acc.shape, F32)

        @pl.when(at < n[0])
        def _():
            parts = [slice(0, cells // 2), slice(cells // 2, cells)]
            hidden_parts = [dot_nn(x_ref[0, rows, :], w1_ref[...]) for rows in parts]
            for rows, value in zip(parts, hidden_parts):
                act, slope = gelu_pair(value)
                act = act.astype(BF16)
                act_ref[0, rows, :] = act
                slope_ref[0, rows, :] = slope.astype(BF16)
                acc[rows, :] += dot_nn(act, w2_ref[...])

            @pl.when(step == steps - 1)
            def _():
                def close(rows):
                    branch = acc[rows, :]
                    branch_ref[0, rows, :] = branch.astype(BF16)
                    out_ref[0, rows, :] = (
                        high_ref[0, rows, :].astype(F32) + g_ref[1:2, :] * branch
                    ).astype(BF16)

                over_rows(cells, close)

        @pl.when((at >= n[0]) & (step == 0))
        def _():
            out_ref[...] = jnp.zeros(out_ref.shape, BF16)

    def held_step(i, j, n):
        return jnp.where(i < n[0], j, steps - 1)

    one = slot(cells, channels)
    hidden_block = pl.BlockSpec(
        (1, cells, block), lambda i, j, n: (held(i, n), 0, held_step(i, j, n))
    )
    return run(
        "conv_mlp",
        body,
        (slots, steps),
        live,
        (spatial, high, w_pw1, w_pw2, gains),
        [
            one,
            one,
            pl.BlockSpec((channels, block), lambda i, j, n: (0, held_step(i, j, n))),
            pl.BlockSpec((block, channels), lambda i, j, n: (held_step(i, j, n), 0)),
            whole(*gains.shape),
        ],
        [
            ((slots, cells, hidden), BF16, hidden_block),
            ((slots, cells, hidden), BF16, hidden_block),
            (spatial.shape, BF16, one),
            (spatial.shape, BF16, every_slot(cells, channels)),
        ],
        [pltpu.VMEM((cells, channels), F32)],
        after=after,
    )


def pool(live, high_out, bins, side):
    slots, cells, channels = high_out.shape
    tok_rows = bins.shape[0] - 2 * side

    def body(n, x_ref, p_ref, own_ref, before_ref, after_ref):
        @pl.when(pl.program_id(0) < n[0])
        def _():
            part = dot_nn(p_ref[...], x_ref[0])
            before_ref[0] = part[0:side].astype(BF16)
            own_ref[0] = part[side : side + tok_rows]
            after_ref[0] = part[side + tok_rows :].astype(BF16)

    return run(
        "pool",
        body,
        (slots,),
        live,
        (high_out, bins),
        [slot(cells, channels), whole(*bins.shape)],
        [
            ((slots, tok_rows, channels), F32, slot(tok_rows, channels)),
            ((slots, side, channels), BF16, slot(side, channels)),
            ((slots, side, channels), BF16, slot(side, channels)),
        ],
    )


def adapter(live, own, first, last, d_merged, w_pool, w_gate, after):
    slots, tok_rows, channels = own.shape
    side = first.shape[1]
    width = w_pool.shape[1]

    def body(
        n, own_ref, first_ref, last_ref, dm_ref, w_ref, gate_ref,
        lift_ref, dpool_ref, gw_ref, ggate_ref, acc,
    ):
        at = pl.program_id(0)

        @pl.when(at == 0)
        def _():
            acc[...] = jnp.zeros(acc.shape, F32)
            ggate_ref[...] = jnp.zeros(ggate_ref.shape, F32)

        @pl.when(at < n[0])
        def _():
            pooled_low = jnp.concatenate(
                [
                    own_ref[0, 0:side] + first_ref[0].astype(F32),
                    own_ref[0, side : tok_rows - side],
                    own_ref[0, tok_rows - side :] + last_ref[0].astype(F32),
                ],
                axis=0,
            ).astype(BF16)
            pooled = pooled_low.astype(F32)
            lifted = dot_nn(pooled_low, w_ref[...])
            logit = jnp.sum(pooled * gate_ref[...], axis=-1, keepdims=True)
            gate = 1.0 / (1.0 + jnp.exp(-logit))
            lift_ref[0] = gate * lifted
            d_top = dm_ref[0].astype(F32)
            d_logit = jnp.sum(d_top * lifted, axis=-1, keepdims=True) * gate * (1.0 - gate)
            d_lifted = (gate * d_top).astype(BF16)
            acc[...] += dot_tn(pooled_low, d_lifted)
            ggate_ref[0:1, :] += col_sum(d_logit * pooled)
            dpool_ref[0] = (dot_nt(d_lifted, w_ref[...]) + d_logit * gate_ref[...]).astype(BF16)

        @pl.when(at == slots - 1)
        def _():
            gw_ref[...] = acc[...].astype(BF16)

    edge = slot(side, channels)
    return run(
        "adapter",
        body,
        (slots,),
        live,
        (own, first, last, d_merged, w_pool, w_gate),
        [slot(tok_rows, channels), edge, edge, slot(tok_rows, width)]
        + [whole(*w_pool.shape), whole(*w_gate.shape)],
        [
            ((slots, tok_rows, width), F32, slot(tok_rows, width)),
            (own.shape, BF16, slot(tok_rows, channels)),
            (w_pool.shape, BF16, result(*w_pool.shape)),
            ((8, channels), F32, result(8, channels)),
        ],
        [pltpu.VMEM(w_pool.shape, F32)],
        after=after,
    )


def unpool(live, near, spread, d_conv, branch, gains):
    slots, near_rows, channels = near.shape
    cells = d_conv.shape[1]

    def body(n, near_ref, s_ref, dc_ref, branch_ref, g_ref, dpost_ref, dbranch_ref, sums_ref):
        at = pl.program_id(0)

        @pl.when(at == 0)
        def _():
            sums_ref[...] = jnp.zeros(sums_ref.shape, F32)

        @pl.when(at < n[0])
        def _():
            def part(rows):
                d_post = dc_ref[0, rows, :].astype(F32) + dot_nn(s_ref[rows, :], near_ref[0])
                sums_ref[0:1, :] += col_sum(d_post * branch_ref[0, rows, :].astype(F32))
                dpost_ref[0, rows, :] = d_post.astype(BF16)
                dbranch_ref[0, rows, :] = (g_ref[1:2, :] * d_post).astype(BF16)

            over_rows(cells, part)

    one = slot(cells, channels)
    return run(
        "unpool",
        body,
        (slots,),
        live,
        (near, spread, d_conv, branch, gains),
        [slot(near_rows, channels), whole(*spread.shape), one, one, whole(*gains.shape)],
        [
            (d_conv.shape, BF16, one),
            (d_conv.shape, BF16, one),
            ((8, channels), F32, result(8, channels)),
        ],
    )


def conv_mlp_back(live, spatial_flip, act, slope, d_branch, w_pw1, w_pw2, grad_pool, flat):
    slots, channels, cells = spatial_flip.shape
    hidden = w_pw1.shape[1]
    block = 2 * BLOCK
    steps = hidden // block
    blocks = channels // BLOCK

    def body(
        n, xt_ref, act_ref, slope_ref, db_ref, w1_ref, w2_ref, pool_ref, dsp_ref, *rest
    ):
        if flat is None:
            out1_ref, out2_ref, a1, a2, dsp, sem = rest
        else:
            refs, (a1, a2, dsp, sem, stage1, stage2, sems1, sems2, sems3) = rest[:4], rest[4:]
        step = pl.program_id(0)

        @pl.when(step == 0)
        def _():
            dsp[...] = jnp.zeros(dsp.shape, F32)

        a1[...] = jnp.zeros(a1.shape, F32)
        a2[...] = jnp.zeros(a2.shape, F32)

        def one(at, carry):
            d_hidden = dot_nt(db_ref[at], w2_ref[...])
            d_expand = (slope_ref[at].astype(F32) * d_hidden).astype(BF16)
            a2[...] += dot_tn(act_ref[at], db_ref[at])
            a1[...] += dot_nn(xt_ref[at], d_expand)
            dsp[at] += dot_nt(d_expand, w1_ref[...])
            return carry

        lax.fori_loop(0, n[0], one, 0)

        @pl.when(step == steps - 1)
        def _():
            out = pltpu.make_async_copy(dsp, dsp_ref, sem)
            out.start()
            out.wait()

        if flat is None:
            out1_ref[...] = a1[...].astype(BF16)
            out2_ref[...] = a2[...].astype(BF16)
            return

        def first_copies(at):
            out = []
            for index, (k, _, rows, start) in enumerate(flat.pieces[0]):
                place = pl.multiple_of(start + at * 2 * rows, 16)
                out.append((k, stage1.at[index, pl.ds(0, 2 * rows), :], place, 2 * rows))
            return out

        def second_copies(at):
            out = []
            for k, row, rows, start, height in flat.within(1, at * block, block):
                for c in range(blocks):
                    source = block_of(stage2, row - at * block, rows, c)
                    out.append((k, source, start + c * height, rows))
            return out

        def pool_copies():
            out = []
            for k, row, rows, start in flat.pieces[2]:
                for c in range(flat.shapes[2][1] // BLOCK):
                    out.append((k, block_of(pool_ref, row, rows, c), start + c * rows, rows))
            return out

        def firsts(now, action):
            copy_out(n[1], refs, first_copies(now), sems1, action)

        def seconds(now, action):
            for static in range(steps):

                @pl.when(now == static)
                def _(static=static):
                    copy_out(n[1], refs, second_copies(static), sems2, action)

        @pl.when(step == 0)
        def _():
            copy_out(n[1], refs, pool_copies(), sems3, "start")

        @pl.when(step > 0)
        def _():
            seconds(step - 1, "wait")
            firsts(step - 1, "wait")

        stage2[...] = a2[...].astype(BF16)
        seconds(step, "start")
        for index, (_, row, rows, _) in enumerate(flat.pieces[0]):
            part = a1[row : row + rows, :]
            both = jnp.concatenate([part[:, 0:BLOCK], part[:, BLOCK:]], axis=0)
            stage1[index, 0 : 2 * rows, :] = both.astype(BF16)
        firsts(step, "start")

        @pl.when(step == steps - 1)
        def _():
            seconds(step, "wait")
            firsts(step, "wait")
            copy_out(n[1], refs, pool_copies(), sems3, "wait")

    by_col = pl.BlockSpec((channels, block), lambda j, n: (0, j))
    by_row = pl.BlockSpec((block, channels), lambda j, n: (j, 0))
    by_hidden = pl.BlockSpec((slots, cells, block), lambda j, n: (0, 0, j))
    wide = (slots, cells, channels)
    scratch = [
        pltpu.VMEM((channels, block), F32),
        pltpu.VMEM((block, channels), F32),
        pltpu.VMEM(wide, F32),
        pltpu.SemaphoreType.DMA,
    ]
    if flat is None:
        grads = [(w_pw1.shape, BF16, by_col), (w_pw2.shape, BF16, by_row)]
    else:
        grads = bundles(flat, 4)
        most = max(len(flat.within(1, at * block, block)) for at in range(steps))
        tall = max(rows for _, _, rows, _ in flat.pieces[0])
        scratch += [
            pltpu.VMEM((len(flat.pieces[0]), 2 * tall, BLOCK), BF16),
            pltpu.VMEM((block, channels), BF16),
            pltpu.SemaphoreType.DMA((len(flat.pieces[0]),)),
            pltpu.SemaphoreType.DMA((most * blocks,)),
            copy_semaphores(flat, 2),
        ]
    return run(
        "conv_mlp_back",
        body,
        (steps,),
        live,
        (spatial_flip, act, slope, d_branch, w_pw1, w_pw2, grad_pool),
        [whole(*spatial_flip.shape), by_hidden, by_hidden, whole(*wide), by_col, by_row, ANYWHERE],
        [(wide, F32, ANYWHERE)] + grads,
        scratch,
    )


def conv_norm_back(live, d_spatial, unit_values, inverse, gains, after):
    slots, cells, channels = d_spatial.shape

    def body(n, e_ref, u_ref, inv_ref, g_ref, out_ref, sums_ref):
        at = pl.program_id(0)

        @pl.when(at == 0)
        def _():
            sums_ref[...] = jnp.zeros(sums_ref.shape, F32)

        @pl.when(at < n[0])
        def _():
            def part(rows):
                e = e_ref[0, rows, :]
                value = u_ref[0, rows, :].astype(F32)
                sums_ref[0:1, :] += col_sum(e * value)
                sums_ref[1:2, :] += col_sum(e)
                grad = unit_back(value, inv_ref[0, rows, :], e * g_ref[0:1, :])
                sums_ref[2:3, :] += col_sum(grad)
                out_ref[0, rows, :] = grad.astype(BF16)

            over_rows(cells, part)

    one = slot(cells, channels)
    return run(
        "conv_norm_back",
        body,
        (slots,),
        live,
        (d_spatial, unit_values, inverse, gains),
        [one, one, slot(cells, 1), whole(*gains.shape)],
        [(d_spatial.shape, BF16, one), ((8, channels), F32, result(8, channels))],
        after=after,
    )


def conv_back(live, d_top, d_mid, d_bottom, d_post, kernel, after):
    slots, rows, cols, channels = d_mid.shape

    def body(n, dt_ref, dm_ref, db_ref, dpost_ref, k_ref, out_ref, frame):
        at = pl.program_id(0)

        @pl.when(at < n[0])
        def _():
            frame[...] = jnp.zeros(frame.shape, F32)

            def tile(tile_at, carry):
                lanes = lane_tile(tile_at)
                stage_rows(frame, dt_ref, dm_ref, db_ref, lanes)

                def emit(y, total):
                    grad = total + dpost_ref[0, y, :, lanes].astype(F32)
                    out_ref[0, y, :, lanes] = grad.astype(BF16)

                depthwise_rows(frame, rows, cols, lambda t: k_ref[t : t + 1, lanes], True, emit)
                return carry

            lax.fori_loop(0, channels // LANES, tile, 0)

        @pl.when(at >= n[0])
        def _():
            out_ref[...] = jnp.zeros(out_ref.shape, BF16)

    halo = slot(REACH, cols, channels)
    one = slot(rows, cols, channels)
    return run(
        "conv_back",
        body,
        (slots,),
        live,
        (d_top, d_mid, d_bottom, d_post, kernel),
        [halo, one, halo, one, whole(*kernel.shape)],
        [(d_mid.shape, BF16, every_slot(rows, cols, channels))],
        [pltpu.VMEM((rows + 2 * REACH, cols + 2 * EDGE, LANES), F32)],
        after=after,
    )[0]


def kernel_back(live, top, high, bottom, d_mid, half, after):
    slots, rows, cols, channels = high.shape
    channels = channels // 2

    def body(n, top_ref, mid_ref, bottom_ref, dm_ref, gk_ref, frame, d_rows):
        at = pl.program_id(0)

        @pl.when(at == 0)
        def _():
            gk_ref[...] = jnp.zeros(gk_ref.shape, F32)

        @pl.when(at < n[0])
        def _():
            frame[...] = jnp.zeros(frame.shape, F32)

            def tile(tile_at, carry):
                lanes = lane_tile(tile_at)
                stage_rows(frame, top_ref, mid_ref, bottom_ref, lanes)
                d_rows[...] = dm_ref[0, :, :, lanes].astype(F32)
                for left in range(KS):
                    totals = [None] * KS
                    grads = {}
                    begin = EDGE - REACH + left
                    for y in range(rows + 2 * REACH):
                        shifted = frame[y, begin : begin + cols, :].reshape(cols // 8, 8, LANES)
                        if y < rows:
                            grads[y] = d_rows[y].reshape(cols // 8, 8, LANES)
                        for tap_row in range(KS):
                            row = y - tap_row
                            if 0 <= row < rows:
                                term = jnp.sum(shifted * grads[row], axis=0)
                                old = totals[tap_row]
                                totals[tap_row] = term if old is None else old + term
                        grads.pop(y - KS + 1, None)
                    for tap_row in range(KS):
                        tap = tap_row * KS + left
                        gk_ref[tap : tap + 1, lanes] += col_sum(totals[tap_row])
                return carry

            lax.fori_loop(0, channels // LANES, tile, 0)

    def half_slot(*shape):
        return pl.BlockSpec((1,) + shape, lambda i, n: (held(i, n), 0, 0, half))

    halo = half_slot(REACH, cols, channels)
    one = half_slot(rows, cols, channels)
    return run(
        "kernel_back",
        body,
        (slots,),
        live,
        (top, high, bottom, d_mid),
        [halo, one, halo, one],
        [((64, channels), F32, result(64, channels))],
        [
            pltpu.VMEM((rows + 2 * REACH, cols + 2 * EDGE, LANES), F32),
            pltpu.VMEM((rows, cols, LANES), F32),
        ],
        after=after,
    )[0]


def from_both_sides(head, tail):
    count = lax.axis_size("strip")
    if count == 2:
        upper = lax.axis_index("strip") == 0
        got = lax.ppermute(jnp.where(upper, tail, head), "strip", [(0, 1), (1, 0)])
        return jnp.where(upper, jnp.zeros_like(got), got), jnp.where(upper, got, jnp.zeros_like(got))
    before = lax.ppermute(tail, "strip", [(i, i + 1) for i in range(count - 1)])
    after = lax.ppermute(head, "strip", [(i + 1, i) for i in range(count - 1)])
    return before, after


def bin_weights(edges, cell_count):
    cells = jnp.arange(cell_count, dtype=jnp.int32)
    inside = (cells[None, :] >= edges[:-1, None]) & (cells[None, :] < edges[1:, None])
    widths = (edges[1:] - edges[:-1]).astype(F32)
    return inside.astype(F32) / widths[:, None]


def strip_bins(edges, first_bin, bin_count, first_cell, cell_count):
    padded = jnp.concatenate([edges[:1], edges, edges[-1:]])
    window = lax.dynamic_slice_in_dim(padded, first_bin + 1, bin_count + 1)
    cells = first_cell + jnp.arange(cell_count, dtype=jnp.int32)
    inside = (cells[None, :] >= window[:-1, None]) & (cells[None, :] < window[1:, None])
    widths = jnp.maximum(window[1:] - window[:-1], 1).astype(F32)
    return inside.astype(F32) / widths[:, None]


def bit_of(axis, bit):
    return (lax.axis_index(axis) >> bit) & 1


def swap_halves(cells, axis, bit, own):
    size = lax.axis_size(axis)
    keep = lax.dynamic_index_in_dim(cells, own, 1, keepdims=False)
    send = lax.dynamic_index_in_dim(cells, 1 - own, 1, keepdims=False)
    got = lax.ppermute(send, axis, [(i, i ^ (1 << bit)) for i in range(size)])
    return (keep.astype(F32) + got.astype(F32)).astype(BF16)


def sum_everywhere(values):
    for axis in ("dp", "strip"):
        size = lax.axis_size(axis)
        step = 1
        while step < size:
            values = values + lax.ppermute(values, axis, [(i, i ^ step) for i in range(size)])
            step *= 2
    return values


def bits(axis):
    return int(math.log2(lax.axis_size(axis)))


def halve_dp(cells, base, bit):
    if cells.shape[0] % 2:
        cells = jnp.pad(cells, [(0, 1)] + [(0, 0)] * (cells.ndim - 1))
    own = (bit_of("dp", bit) - base) & 1
    cells = cells.reshape((cells.shape[0] // 2, 2) + cells.shape[1:])
    return swap_halves(cells, "dp", bit, own), (base + own) >> 1


def halve_strip(cells):
    for bit in range(bits("strip")):
        m, count = cells.shape[:2]
        cells = cells.reshape((m * count // 2, 2) + cells.shape[2:])
        cells = swap_halves(cells, "strip", bit, bit_of("strip", bit))
        cells = cells.reshape((m, count // 2) + cells.shape[1:])
    return cells


def shared_sum(matrix, offset, chunk, strip_first):
    strips = lax.axis_size("strip")
    rows, cols = matrix.shape
    chunk_rows = chunk // cols
    base = offset // (chunk * strips)
    front = (offset - base * chunk * strips) // cols
    groups = -(-(front + rows) // (chunk_rows * strips))
    back = groups * chunk_rows * strips - front - rows
    cells = jnp.pad(matrix, ((front, back), (0, 0))).reshape(groups, strips, chunk_rows, cols)
    cells, base = halve_dp(cells, base, 0)
    if strip_first:
        cells = halve_strip(cells)
        cells, base = halve_dp(cells, base, 1)
    else:
        cells, base = halve_dp(cells, base, 1)
        cells = halve_strip(cells)
    return cells.reshape(cells.shape[0], chunk), base


def owned_chunk(matrices, extras):
    data_count = lax.axis_size("dp")
    strips = lax.axis_size("strip")
    devices = data_count * strips
    chunk = sum(m.size for m in matrices) // devices
    span = data_count // 4
    placed = None
    offset = 0
    for order, matrix in enumerate(matrices):
        part, base = shared_sum(matrix, offset, chunk, order % 2 == 0)
        canvas = jnp.zeros((span + part.shape[0], chunk), BF16)
        canvas = lax.dynamic_update_slice(canvas, part, (base, 0))[:span]
        placed = canvas if placed is None else placed + canvas
        offset += matrix.size
    for bit in range(2, bits("dp")):
        placed = placed.reshape(placed.shape[0] // 2, 2, chunk)
        placed = swap_halves(placed, "dp", bit, bit_of("dp", bit))
    return share_of(placed.reshape(chunk).astype(F32), chunk, extras)


STEPS = {
    "core": ("dp", 1, lambda dp, strip: dp & 1),
    "x": ("strip", 1, lambda dp, strip: strip & 1),
    "y": ("dp", 2, lambda dp, strip: (dp >> 1) & 1),
    "z": ("dp", 4, lambda dp, strip: ((dp >> 2) ^ (dp >> 3)) & 1),
    "far": ("dp", 12, lambda dp, strip: (dp >> 3) & 1),
}
ORDERS = (("x", "y", "z"), ("y", "z", "x"), ("z", "x", "y"))


def across(step, value):
    axis, flip_bits, _ = STEPS[step]
    return lax.ppermute(value, axis, [(i, i ^ flip_bits) for i in range(lax.axis_size(axis))])


def relay(live, values, after=()):
    def body(_, *refs):
        pass

    outs = [(v.shape, v.dtype, ANYWHERE) for v in values]
    alias = tuple((i, i) for i in range(len(values)))
    specs = [ANYWHERE] * len(values)
    return run("relay", body, (1,), live, tuple(values), specs, outs, after=after, alias=alias)


def split_sum(flat, sets, level, after, through):
    parts = len(ORDERS)
    rows = flat.units // parts
    count = sets[0][0][0].shape[0] // 2
    own = [STEPS[order[level]][2](lax.axis_index("dp"), lax.axis_index("strip")) for order in ORDERS]
    bits = jnp.stack(own).astype(jnp.int32)
    specs, args = [], []
    for number, (kept, arrived) in enumerate(sets):
        for part, order in enumerate(ORDERS):
            left = [name for name in ("z", "y", "x") if name not in order[:level]]
            low = len(left) - 1 - left.index(order[level])

            for flipped in (0, 1):

                def place(i, bit, part=part, low=low, flipped=flipped, first=number * count):
                    i = jnp.clip(i - first, 0, count - 1)
                    mine = bit[part] ^ flipped
                    index = ((i >> low) << (low + 1)) | (mine << low) | (i & ((1 << low) - 1))
                    return index, part if level == 0 else 0, 0

                for source in (kept, arrived):
                    args.append(source[0 if level == 0 else part])
                    specs.append(pl.BlockSpec((1, rows, BLOCK), place))
    given = len(args)

    def body(_, *refs):
        outs = refs[given + len(through) :]
        for number in range(len(sets)):
            ins = refs[number * 4 * parts : (number + 1) * 4 * parts]

            @pl.when(pl.program_id(0) // count == number)
            def _(ins=ins):
                for at in range(2 * parts):
                    total = ins[2 * at][...].astype(F32) + ins[2 * at + 1][...].astype(F32)
                    outs[at][...] = total.astype(BF16)

    out = pl.BlockSpec((1, rows, BLOCK), lambda i, bit: (i, 0, 0))
    done = run(
        "split_sum",
        body,
        (len(sets) * count,),
        bits,
        tuple(args) + tuple(through),
        specs + [ANYWHERE] * len(through),
        [((len(sets) * count, rows, BLOCK), BF16, out)] * (2 * parts)
        + [(v.shape, v.dtype, ANYWHERE) for v in through],
        after=after,
        alias=tuple((given + i, 2 * parts + i) for i in range(len(through))),
    )
    return done[0 : 2 * parts : 2], done[1 : 2 * parts : 2], done[2 * parts :]


class Bundle:
    def __init__(self, flat, kept, send):
        self.flat, self.level = flat, 0
        self.kept, self.arrived = [kept], [across("core", send)]

    def step(self, after, through=(), other=None):
        sets = [(b.kept, b.arrived) for b in (self, other) if b is not None]
        self.kept, sends, passed = split_sum(self.flat, sets, self.level, after, through)
        self.arrived = [across(order[self.level], v) for order, v in zip(ORDERS, sends)]
        self.level += 1
        return (self.kept[0],), passed

    def last_step(self):
        parts = [k.astype(F32) + a.astype(F32) for k, a in zip(self.kept, self.arrived)]
        low, high = jnp.concatenate(parts, axis=1).astype(BF16)
        is_upper = STEPS["far"][2](lax.axis_index("dp"), lax.axis_index("strip")) == 1
        self.kept = [jnp.where(is_upper, high, low)]
        self.arrived = [across("far", jnp.where(is_upper, low, high))]

    def chunk(self):
        return self.kept[0].astype(F32) + self.arrived[0].astype(F32)


def row_major(flat, units):
    devices = lax.axis_size("dp") * lax.axis_size("strip")
    index = lax.axis_index("dp") * lax.axis_size("strip") + lax.axis_index("strip")
    kinds, kind_of = [], []
    for k in range(devices):
        kind = []
        for matrix, pieces in enumerate(flat.pieces):
            for chunk, _, rows, start in pieces:
                if chunk == k:
                    kind.append((start, rows, flat.shapes[matrix][1] // BLOCK))
        kind = tuple(kind)
        if kind not in kinds:
            kinds.append(kind)
        kind_of.append(kinds.index(kind))

    def ordered(kind):
        def branch(value):
            out = []
            for start, rows, blocks in kind:
                piece = value[start : start + rows * blocks].reshape(blocks, rows, BLOCK)
                out.append(piece.transpose(1, 0, 2).reshape(-1))
            return jnp.concatenate(out)

        return branch

    which = jnp.asarray(kind_of, jnp.int32)[index]
    return lax.switch(which, [ordered(kind) for kind in kinds], units)


def share_of(mine, chunk, extras):
    data_count = lax.axis_size("dp")
    strips = lax.axis_size("strip")
    devices = data_count * strips
    extra = extras.shape[0] // devices
    index = lax.axis_index("dp") * strips + lax.axis_index("strip")
    pieces = [mine]
    left = extras.shape[0]
    padded = jnp.pad(extras, (0, chunk))
    for hop in range(1, -(-left // chunk) + 1):
        size = min(left, chunk)
        left -= size
        following = lax.ppermute(
            mine[:size].astype(BF16),
            ("dp", "strip"),
            [(i + hop, i) for i in range(devices - hop)],
        ).astype(F32)
        past = index + hop - devices
        own_extras = lax.dynamic_slice(padded, (jnp.maximum(past, 0) * chunk,), (size,))
        pieces.append(jnp.where(past >= 0, own_extras, following))
    return lax.dynamic_slice(jnp.concatenate(pieces), (index * extra,), (chunk + extra,))


def per_device(
    low_tokens,
    high_map,
    counts,
    row_edges,
    col_edges,
    w_qkv,
    w_attn_out,
    w_fc1,
    w_fc2,
    vit_gains,
    vit_shifts,
    w_pw1,
    w_pw2,
    w_pool,
    dw_kernel,
    conv_gains,
    conv_shifts,
    w_gate,
    d_merged,
    d_conv,
):
    slots, tok_rows, width = low_tokens.shape
    rows, cols, channels = high_map.shape[1:]
    cells = rows * cols
    strips = lax.axis_size("strip")
    strip = lax.axis_index("strip")
    live = jnp.stack([counts[0], lax.axis_index("dp") & 1]).astype(jnp.int32)

    col_bins = bin_weights(col_edges, cols)
    side = col_bins.shape[0]
    own_bins = tok_rows // side
    near_bins = strip_bins(row_edges, strip * own_bins - 1, own_bins + 2, strip * rows, rows)
    bins = (near_bins[:, None, :, None] * col_bins[None, :, None, :]).astype(BF16)
    bins = bins.reshape((own_bins + 2) * side, cells)

    data_count = lax.axis_size("dp")
    devices = data_count * strips
    vit_flat = Flat([w.shape for w in (w_qkv, w_attn_out, w_fc1, w_fc2)], devices)
    conv_flat = Flat([w.shape for w in (w_pw1, w_pw2, w_pool)], devices)
    chunked = devices == 4 * BUNDLE and strips == 2 and vit_flat.even and conv_flat.even
    if not chunked:
        vit_flat = conv_flat = None

    def over_cores(value):
        return lax.ppermute(value, "dp", [(i, i ^ 1) for i in range(data_count)])

    def over_y(value):
        return lax.ppermute(value, "dp", [(i, i ^ 2) for i in range(data_count)])

    own_count = counts[0]
    lead = own_count - over_cores(counts)[0]
    lends, borrows = lead >= 2, lead <= -2
    after_cores = own_count - lends.astype(jnp.int32) + borrows.astype(jnp.int32)
    lead_y = after_cores - over_y(after_cores.reshape(1))[0]
    lends_y, borrows_y = lead_y >= 2, lead_y <= -2
    lent_slot = own_count - 1
    lent_slot_y = lent_slot - lends.astype(jnp.int32)
    kept_count = own_count - lends.astype(jnp.int32) - lends_y.astype(jnp.int32)
    guest_slot = kept_count
    guest_slot_y = kept_count + borrows.astype(jnp.int32)
    live = guest_slot_y + borrows_y.astype(jnp.int32)
    live = jnp.stack([live, lax.axis_index("dp") & 1]).astype(jnp.int32)

    def at_slot(condition, place, like):
        return (condition & (jnp.arange(slots) == place)).reshape((slots,) + (1,) * (like.ndim - 1))

    def one_slot(values, place):
        return lax.dynamic_index_in_dim(values, jnp.clip(place, 0, slots - 1), 0)

    def loans(values):
        return one_slot(values, lent_slot), one_slot(values, lent_slot_y)

    def taken(pair):
        return over_cores(pair[0]), over_y(pair[1])

    def with_guests(values, guests):
        values = jnp.where(at_slot(borrows, guest_slot, values), guests[0], values)
        return jnp.where(at_slot(borrows_y, guest_slot_y, values), guests[1], values)

    def sent_home(values):
        return over_cores(one_slot(values, guest_slot)), over_y(one_slot(values, guest_slot_y))

    def returned(values, home):
        own = (jnp.arange(slots) < kept_count).reshape((slots,) + (1,) * (values.ndim - 1))
        out = jnp.where(own, values, jnp.zeros_like(values))
        out = jnp.where(at_slot(lends, lent_slot, values), home[0], out)
        return jnp.where(at_slot(lends_y, lent_slot_y, values), home[1], out)

    def shifted(value, by):
        return lax.ppermute(value, "strip", [(i, (i + by) % strips) for i in range(strips)])

    edge_rows = jnp.concatenate([high_map[:, :REACH], high_map[:, -REACH:]], axis=1)
    guest_rows = jnp.concatenate(taken(loans(edge_rows)))
    guest_maps = taken(loans(high_map))
    halos = from_both_sides(high_map[:, :REACH], high_map[:, -REACH:])
    guest_halos = from_both_sides(guest_rows[:, :REACH], guest_rows[:, REACH:])
    top, bottom = (with_guests(h, (g[:1], g[1:])) for h, g in zip(halos, guest_halos))
    high_map = with_guests(high_map, guest_maps)
    both = [jnp.concatenate(pair, axis=1) for pair in zip(loans(low_tokens), loans(d_merged))]
    payloads = relay(live, both + list(loans(d_conv)), (top, bottom, high_map))
    both = taken(payloads[:2])
    low_tokens = with_guests(low_tokens, [guest[:, :tok_rows] for guest in both])
    d_merged = with_guests(d_merged, [guest[:, tok_rows:] for guest in both])
    d_conv = with_guests(d_conv, taken(payloads[2:]))
    tok_all = jnp.concatenate(
        [low_tokens] + [shifted(low_tokens, by) for by in range(1, strips)], axis=1
    )

    spatial, spatial_flip, conv_unit, conv_inverse = conv_front(
        live, top, high_map, bottom, dw_kernel, conv_gains, conv_shifts, tuple(payloads[:1])
    )
    act, slope, branch, high_out = conv_mlp(
        live, spatial, high_map.reshape(slots, cells, channels), w_pw1, w_pw2, conv_gains,
        (low_tokens, d_merged),
    )
    own, before_part, after_part = pool(live, high_out, bins, side)
    first, last = from_both_sides(*relay(live, (before_part, after_part), (d_conv,)))
    lift, d_pooled, grad_pool, gate_sums = adapter(
        live, own, first, last, d_merged, w_pool, w_gate.reshape(1, channels), ()
    )
    (high_out,) = relay(live, (high_out,), (d_pooled,))
    high_home = sent_home(high_out)
    near_before, near_after = from_both_sides(d_pooled[:, :side], d_pooled[:, -side:])
    d_post, d_branch, scale_sums = unpool(
        live,
        jnp.concatenate([near_before, d_pooled, near_after], axis=1),
        bins.T,
        d_conv.reshape(slots, cells, channels),
        branch,
        conv_gains,
    )
    d_spatial, *grads_conv = conv_mlp_back(
        live, spatial_flip, act, slope, d_branch, w_pw1, w_pw2, grad_pool, conv_flat
    )
    order = (d_spatial,) + high_home
    if chunked:
        sends = relay(live, (grads_conv[1], grads_conv[3]), high_home + (tok_all,))
        conv_lower = Bundle(conv_flat, grads_conv[0], sends[0])
        conv_upper = Bundle(conv_flat, grads_conv[2], sends[1])
        order = (conv_lower.kept[0],) + high_home
    d_conv_in, norm_sums = conv_norm_back(
        live, d_spatial, conv_unit, conv_inverse, conv_gains, order
    )
    normed, q, kv, probs, mixed, residual, inner, inner_flip = vit_front(
        live, tok_all, w_qkv, w_attn_out, vit_gains, vit_shifts, tok_rows, (d_conv_in,)
    )
    order = (inner,)
    if chunked:
        order, (d_conv_in,) = conv_lower.step(order, (d_conv_in,), conv_upper)
    d_conv_in = d_conv_in.reshape(high_map.shape)
    d_before, d_after = from_both_sides(d_conv_in[:, :REACH], d_conv_in[:, -REACH:])
    merged, d_inner, *grads_fc = vit_mlp(
        live, inner, inner_flip, d_merged, residual, lift, w_fc1, w_fc2, vit_flat, order
    )
    order = (d_inner, d_before, d_after)
    if chunked:
        order, (send,) = conv_lower.step(order, (grads_fc[3],))
        vit_upper = Bundle(vit_flat, grads_fc[2], send)
    d_residual, d_mixed, inner_sums, *grads_out = vit_back(
        live, residual, d_inner, d_merged, mixed, w_attn_out, vit_gains, vit_flat,
        tuple(grads_fc[:2]), order,
    )
    d_q, d_k, d_v = attention_back(live, probs, q, kv, d_mixed, (d_residual,))
    order = (d_q,)
    if chunked:
        order, (merged,) = conv_lower.step(order + tuple(vit_upper.arrived), (merged,))
    merged_home = sent_home(merged)
    d_normed, *grads_qkv = qkv_back(
        live, normed, d_q, d_k, d_v, w_qkv, vit_flat, tuple(grads_out), order
    )
    order = (d_normed,) + merged_home
    if chunked:
        order += tuple(conv_lower.arrived)
        order, (send,) = vit_upper.step(order, (grads_qkv[1],))
        vit_lower = Bundle(vit_flat, grads_qkv[0], send)
        conv_lower.last_step()
    grad_map = conv_back(
        live, d_before, d_conv_in, d_after, d_post.reshape(high_map.shape), dw_kernel, order
    )
    order = (grad_map,)
    if chunked:
        order = tuple(vit_upper.arrived)
        order, (grad_map,) = vit_lower.step(order, (grad_map,))
    map_home = sent_home(grad_map)
    (d_normed,) = relay(live, (d_normed,), order)
    d_other = jnp.zeros(low_tokens.shape, BF16)
    for by in range(1, strips):
        part = d_normed[:, by * tok_rows : (by + 1) * tok_rows].astype(BF16)
        d_other = d_other + shifted(part, -by) if by > 1 else shifted(part, -by)
    kernel_sums = [kernel_back(live, top, high_map, bottom, d_conv_in, 0, (d_normed,))]
    kernel_sums.append(kernel_back(live, top, high_map, bottom, d_conv_in, 1, (kernel_sums[0],)))
    order = (*vit_lower.arrived, *conv_lower.arrived) if chunked else ()
    kernel_sums = relay(live, kernel_sums, order)
    grad_tokens, token_sums = tokens_back(
        live, low_tokens, d_normed, d_other, d_residual, vit_gains, (kernel_sums[0],)
    )
    kernel_sums = jnp.concatenate(kernel_sums, axis=1)

    vit_extras = jnp.concatenate([token_sums[0], inner_sums[0], token_sums[1], inner_sums[1]])
    conv_extras = jnp.concatenate(
        [
            kernel_sums[: KS * KS].reshape(-1),
            norm_sums[0],
            scale_sums[0],
            norm_sums[2],
            norm_sums[1],
            gate_sums[0],
        ]
    )
    extras = sum_everywhere(jnp.concatenate([vit_extras, conv_extras]))
    vit_extras, conv_extras = extras[: vit_extras.shape[0]], extras[vit_extras.shape[0] :]
    if chunked:
        order, _ = vit_lower.step((token_sums,), (), vit_upper)
        conv_out = share_of(row_major(conv_flat, conv_lower.chunk()), conv_flat.chunk, conv_extras)
        vit_lower.step(order)
        vit_lower.last_step()
        vit_mine = row_major(vit_flat, vit_lower.chunk())
        vit_out = share_of(vit_mine, vit_flat.chunk, vit_extras)
    else:
        vit_out = owned_chunk([*grads_qkv, *grads_out, *grads_fc], vit_extras)
        conv_out = owned_chunk([*grads_conv, grad_pool], conv_extras)
    return (
        returned(merged, merged_home),
        returned(high_out, high_home).reshape(high_map.shape),
        returned(grad_tokens, sent_home(grad_tokens)),
        returned(grad_map, map_home),
        vit_out,
        conv_out,
    )


def solution(mesh):
    images = P("dp", "strip", None)
    maps = P("dp", "strip", None, None)
    flat = P(("dp", "strip"))
    in_specs = (images, maps, P("dp")) + (P(),) * 15 + (images, maps)
    out_specs = (images, maps, images, maps, flat, flat)
    return jax.shard_map(
        per_device, mesh=mesh, in_specs=in_specs, out_specs=out_specs, check_vma=False
    )
```

```python
import math

import jax
import jax.numpy as jnp
from jax import lax
from jax.experimental import pallas as pl
from jax.experimental.pallas import tpu as pltpu
from jax.sharding import PartitionSpec as P

HEADS = 16
KS = 7
REACH = KS // 2
EPSILON = 1e-05
LANES = 128
EDGE = 8
BLOCK = 256
BUNDLE = 8
F32 = jnp.float32
BF16 = jnp.bfloat16
VMEM_BYTES = 60 * 1024 * 1024


def dot_nn(a, b):
    return jnp.dot(a, b, preferred_element_type=F32)


def dot_nt(a, b):
    return lax.dot_general(a, b, (((1,), (1,)), ((), ())), preferred_element_type=F32)


def dot_tn(a, b):
    return lax.dot_general(a, b, (((0,), (0,)), ((), ())), preferred_element_type=F32)


def flip(value):
    return value.astype(F32).T.astype(BF16)


def row_step(rows):
    for step in (128, 96, 64, 48, 32, 16):
        if rows % step == 0:
            return step
    return rows


def over_rows(rows, body):
    step = row_step(rows)

    def one(at, carry):
        body(pl.ds(pl.multiple_of(at * step, step), step))
        return carry

    if step == rows:
        body(pl.ds(0, rows))
    else:
        lax.fori_loop(0, rows // step, one, 0)


def lane_tile(at):
    return pl.ds(pl.multiple_of(at * LANES, LANES), LANES)


def unit(values):
    center = values - jnp.mean(values, axis=-1, keepdims=True)
    inverse = lax.rsqrt(jnp.mean(center * center, axis=-1, keepdims=True) + EPSILON)
    return center * inverse, inverse


def unit_back(unit_values, inverse, grad):
    return (
        grad
        - jnp.mean(grad, axis=-1, keepdims=True)
        - unit_values * jnp.mean(grad * unit_values, axis=-1, keepdims=True)
    ) * inverse


def gelu_pair(x):
    scale = math.sqrt(2.0 / math.pi)
    square = x * x
    bend = jnp.tanh(x * (scale + (scale * 0.044715) * square))
    half = 0.5 + 0.5 * bend
    slope = half + (0.5 * x) * (1.0 - bend * bend) * (scale + (3.0 * scale * 0.044715) * square)
    return x * half, slope


def col_sum(values):
    return jnp.sum(values, axis=0, keepdims=True)


ANYWHERE = pl.BlockSpec(memory_space=pl.ANY)


def held(at, live):
    return jnp.maximum(jnp.minimum(at, live[0] - 1), 0)


def slot(*shape):
    return pl.BlockSpec(
        (1,) + shape, lambda *g: (held(g[0], g[-1]),) + (0,) * len(shape)
    )


def every_slot(*shape):
    return pl.BlockSpec((1,) + shape, lambda *g: (g[0],) + (0,) * len(shape))


def whole(*shape):
    return pl.BlockSpec(shape, lambda *g: (0,) * len(shape), pipeline_mode=pl.Buffered(1))


def result(*shape):
    return pl.BlockSpec(shape, lambda *g: (0,) * len(shape))


def run(name, body, grid, live, args, in_specs, outs, scratch=(), after=(), alias=()):
    out_shape = [jax.ShapeDtypeStruct(shape, dtype) for shape, dtype, _ in outs]
    count = 1 + len(args)

    def without_order(*refs):
        body(*refs[:count], *refs[count + len(after) :])

    return pl.pallas_call(
        without_order,
        grid_spec=pltpu.PrefetchScalarGridSpec(
            num_scalar_prefetch=1,
            grid=grid,
            in_specs=list(in_specs) + [pl.BlockSpec(memory_space=pl.ANY)] * len(after),
            out_specs=[spec for _, _, spec in outs],
            scratch_shapes=list(scratch),
        ),
        out_shape=out_shape,
        input_output_aliases={1 + given: out for given, out in alias},
        compiler_params=pltpu.CompilerParams(
            dimension_semantics=("arbitrary",) * len(grid), vmem_limit_bytes=VMEM_BYTES
        ),
        cost_estimate=pl.CostEstimate(flops=0, bytes_accessed=0, transcendentals=0),
        name=name,
    )(live, *args, *after)


class Flat:
    def __init__(self, shapes, devices):
        self.shapes = shapes
        self.chunk = sum(r * c for r, c in shapes) // devices
        self.units = self.chunk // BLOCK
        self.pieces = []
        self.even = sum(r * c for r, c in shapes) % (devices * BLOCK * 3 * 16) == 0
        offset = 0
        for rows, cols in shapes:
            self.even &= self.chunk % cols == 0 and offset % cols == 0 and cols % BLOCK == 0
            found = []
            if self.even:
                height, begin = self.chunk // cols, offset // cols
                for k in range(devices):
                    low = max(k * height, begin)
                    high = min((k + 1) * height, begin + rows)
                    if low < high:
                        start = (low - k * height) * (cols // BLOCK)
                        found.append((k, low - begin, high - low, start))
                        self.even &= (high - low) % 8 == 0 and start % 16 == 0
                self.even &= bool(self.pieces) or found[-1][0] < 2 * BUNDLE
            self.pieces.append(found)
            offset += rows * cols

    def within(self, matrix, first, count):
        out = []
        for k, row, height, start in self.pieces[matrix]:
            low, high = max(row, first), min(row + height, first + count)
            if low < high:
                out.append((k, low, high - low, start + low - row, height))
        return out


def side_of(chunk):
    z1, z0, y = (chunk >> 4) & 1, (chunk >> 3) & 1, (chunk >> 2) & 1
    return z1, (chunk >> 1) & 1, (z0 ^ z1) * 4 + y * 2 + (chunk & 1)


def copy_out(own_core, refs, copies, sems, action):
    for at, (chunk, source, place, rows) in enumerate(copies):
        upper, core, index = side_of(chunk)
        for held_here, ref in ((True, refs[2 * upper]), (False, refs[2 * upper + 1])):

            @pl.when((own_core == core) == held_here)
            def _(ref=ref, at=at, source=source, place=place, rows=rows, index=index):
                target = ref.at[index, pl.ds(place, rows), :]
                getattr(pltpu.make_async_copy(source, target, sems.at[at]), action)()


def copy_all(own_core, refs, stage, flat, matrix, sems):
    copies = []
    for k, row, rows, start in flat.pieces[matrix]:
        for c in range(stage.shape[1] // BLOCK):
            copies.append((k, block_of(stage, row, rows, c), start + c * rows, rows))
    copy_out(own_core, refs, copies, sems, "start")
    copy_out(own_core, refs, copies, sems, "wait")


def copy_semaphores(flat, matrix):
    return pltpu.SemaphoreType.DMA((len(flat.pieces[matrix]) * flat.shapes[matrix][1] // BLOCK,))


def bundles(flat, count):
    shape = (BUNDLE, flat.units, BLOCK)
    return [(shape, BF16, pl.BlockSpec(memory_space=pl.ANY))] * count


def block_of(ref, first, rows, block):
    return ref.at[pl.ds(first, rows), pl.ds(block * BLOCK, BLOCK)]


def vit_front(live, tok_all, w_qkv, w_out, gains, shifts, tok_rows, after):
    slots, key_rows, width = tok_all.shape
    head = width // HEADS
    pairs = width // LANES
    per_tile = LANES // head

    def body(
        n, x_ref, wq_ref, wo_ref, g_ref, b_ref,
        normed_ref, q_ref, kv_ref, probs_ref, mixed_ref, res_ref, inner_ref, flip_ref,
    ):
        @pl.when(pl.program_id(0) < n[0])
        def _():
            def first_norm(rows):
                value, _ = unit(x_ref[0, rows, :].astype(F32))
                normed_ref[0, rows, :] = (value * g_ref[0:1, :] + b_ref[0:1, :]).astype(BF16)

            over_rows(key_rows, first_norm)
            q_ref[0] = dot_nn(normed_ref[0, 0:tok_rows, :], wq_ref[:, 0:width]).astype(BF16)
            for part in range(4):
                cols = slice(part * width // 2, (part + 1) * width // 2)
                w_cols = slice(width + cols.start, width + cols.stop)
                kv_ref[0, :, cols] = dot_nn(normed_ref[0], wq_ref[:, w_cols]).astype(BF16)

            lane = lax.broadcasted_iota(jnp.int32, (1, LANES), 1) // head

            def heads(pair, carry):
                q = q_ref[0, :, lane_tile(pair)] * jnp.asarray(1.0 / math.sqrt(head), BF16)
                k = kv_ref[0, :, lane_tile(pair)].astype(F32)
                v_flip = flip(kv_ref[0, :, lane_tile(pairs + pair)])
                mixed = []
                for h in range(per_tile):
                    scores = dot_nt(jnp.where(lane == h, k, 0.0).astype(BF16), q)
                    top = jnp.max(scores, axis=0, keepdims=True)
                    raised = jnp.exp(scores - top)
                    probs = (raised * (1.0 / col_sum(raised))).astype(BF16)
                    probs_ref[0, pair * per_tile + h] = probs
                    mixed.append(dot_nn(v_flip[h * head : (h + 1) * head, :], probs))
                mixed_ref[0, :, lane_tile(pair)] = jnp.concatenate(mixed, axis=0).T.astype(BF16)
                return carry

            lax.fori_loop(0, pairs, heads, 0)
            res_ref[0] = dot_nn(mixed_ref[0], wo_ref[...])

            def second_norm(rows):
                res = res_ref[0, rows, :] + x_ref[0, rows, :].astype(F32)
                res_ref[0, rows, :] = res
                value, _ = unit(res)
                inner_ref[0, rows, :] = (value * g_ref[1:2, :] + b_ref[1:2, :]).astype(BF16)

            over_rows(tok_rows, second_norm)
            flip_ref[0] = flip(inner_ref[0])

    return run(
        "vit_front",
        body,
        (slots,),
        live,
        (tok_all, w_qkv, w_out, gains, shifts),
        [slot(key_rows, width), whole(*w_qkv.shape), whole(*w_out.shape)]
        + [whole(*gains.shape), whole(*shifts.shape)],
        [
            ((slots, key_rows, width), BF16, slot(key_rows, width)),
            ((slots, tok_rows, width), BF16, slot(tok_rows, width)),
            ((slots, key_rows, 2 * width), BF16, slot(key_rows, 2 * width)),
            ((slots, HEADS, key_rows, tok_rows), BF16, slot(HEADS, key_rows, tok_rows)),
            ((slots, tok_rows, width), BF16, slot(tok_rows, width)),
            ((slots, tok_rows, width), F32, slot(tok_rows, width)),
            ((slots, tok_rows, width), BF16, slot(tok_rows, width)),
            ((slots, width, tok_rows), BF16, slot(width, tok_rows)),
        ],
        after=after,
    )


def vit_mlp(live, inner, inner_flip, d_mlp, residual, lift, w_fc1, w_fc2, flat, after):
    slots, tok_rows, width = inner.shape
    hidden = w_fc1.shape[1]
    block = 512
    steps = hidden // block
    blocks = width // BLOCK

    def body(
        n, x_ref, xt_ref, dm_ref, res_ref, lift_ref, w1_ref, w2_ref,
        merged_ref, din_ref, *rest,
    ):
        if flat is None:
            out1_ref, out2_ref, low, a1, a2 = rest
        else:
            refs, (low, a1, a2, stage1, stage2, sems1, sems2) = rest[:4], rest[4:]
        step = pl.program_id(0)

        @pl.when(step == 0)
        def _():
            low[...] = res_ref[...]
            din_ref[...] = jnp.zeros(din_ref.shape, F32)

        a1[...] = jnp.zeros(a1.shape, F32)
        a2[...] = jnp.zeros(a2.shape, F32)

        def one(at, carry):
            before = dot_nn(x_ref[at], w1_ref[...])
            d_act = dot_nt(dm_ref[at], w2_ref[...])
            act, slope = gelu_pair(before)
            act = act.astype(BF16)
            d_fc = (slope * d_act).astype(BF16)
            low[at] += dot_nn(act, w2_ref[...])
            a2[...] += dot_tn(act, dm_ref[at])
            a1[...] += dot_nn(xt_ref[at], d_fc)
            din_ref[at] += dot_nt(d_fc, w1_ref[...])
            return carry

        lax.fori_loop(0, n[0], one, 0)

        @pl.when(step == steps - 1)
        def _():
            def close(at, carry):
                merged_ref[at] = (low[at] + lift_ref[at]).astype(BF16)
                return carry

            def blank(at, carry):
                merged_ref[at] = jnp.zeros(merged_ref.shape[1:], BF16)
                return carry

            lax.fori_loop(0, n[0], close, 0)
            lax.fori_loop(n[0], slots, blank, 0)

        if flat is None:
            out1_ref[...] = a1[...].astype(BF16)
            out2_ref[...] = a2[...].astype(BF16)
            return

        def first_copies(at):
            out = []
            for c in range(block // BLOCK):
                for k, row, rows, start, height in flat.within(2, 0, width):
                    place = start + (at * (block // BLOCK) + c) * height
                    out.append((k, block_of(stage1, row, rows, c), pl.multiple_of(place, 16), rows))
            return out

        def second_copies(at):
            out = []
            for k, row, rows, start, height in flat.within(3, at * block, block):
                for c in range(blocks):
                    source = block_of(stage2, row - at * block, rows, c)
                    out.append((k, source, start + c * height, rows))
            return out

        def each(at, now, action):
            copy_out(n[1], refs, first_copies(now), sems1, action)
            for static in range(steps):

                @pl.when(now == static)
                def _(static=static):
                    copy_out(n[1], refs, second_copies(static), sems2, action)

        @pl.when(step > 0)
        def _():
            each(step, step - 1, "wait")

        stage1[...] = a1[...].astype(BF16)
        stage2[...] = a2[...].astype(BF16)
        each(step, step, "start")

        @pl.when(step == steps - 1)
        def _():
            each(step, step, "wait")

    wide = (slots, tok_rows, width)
    by_col = pl.BlockSpec((width, block), lambda j, n: (0, j))
    by_row = pl.BlockSpec((block, width), lambda j, n: (j, 0))
    scratch = [
        pltpu.VMEM(wide, F32),
        pltpu.VMEM((width, block), F32),
        pltpu.VMEM((block, width), F32),
    ]
    if flat is None:
        grads = [(w_fc1.shape, BF16, by_col), (w_fc2.shape, BF16, by_row)]
    else:
        grads = bundles(flat, 4)
        most = max(len(flat.within(3, at * block, block)) for at in range(steps))
        scratch += [
            pltpu.VMEM((width, block), BF16),
            pltpu.VMEM((block, width), BF16),
            pltpu.SemaphoreType.DMA((block // BLOCK * len(flat.pieces[2]),)),
            pltpu.SemaphoreType.DMA((most * blocks,)),
        ]
    return run(
        "vit_mlp",
        body,
        (steps,),
        live,
        (inner, inner_flip, d_mlp, residual, lift, w_fc1, w_fc2),
        [whole(*wide), whole(*inner_flip.shape)] + [whole(*wide)] * 3 + [by_col, by_row],
        [(wide, BF16, result(*wide)), (wide, F32, result(*wide))] + grads,
        scratch,
        after=after,
    )


def vit_back(live, residual, d_inner, d_merged, mixed, w_out, gains, flat, kept, after):
    slots, tok_rows, width = residual.shape

    def body(n, res_ref, din_ref, dm_ref, mix_ref, wo_ref, g_ref, *rest):
        if flat is None:
            dres_ref, dmix_ref, sums_ref, gout_ref, low, acc = rest
        else:
            _, _, dres_ref, dmix_ref, sums_ref, keep_ref, send_ref, low, acc, stage, sems = rest
        at = pl.program_id(0)

        @pl.when(at == 0)
        def _():
            acc[...] = jnp.zeros(acc.shape, F32)
            sums_ref[...] = jnp.zeros(sums_ref.shape, F32)

        @pl.when(at < n[0])
        def _():
            def back(rows):
                value, inverse = unit(res_ref[0, rows, :])
                e = din_ref[0, rows, :]
                sums_ref[0:1, :] += col_sum(e * value)
                sums_ref[1:2, :] += col_sum(e)
                d_res = dm_ref[0, rows, :].astype(F32) + unit_back(value, inverse, e * g_ref[1:2, :])
                dres_ref[0, rows, :] = d_res
                low[rows, :] = d_res.astype(BF16)

            over_rows(tok_rows, back)
            dmix_ref[0] = dot_nt(low[...], wo_ref[...]).astype(BF16)
            acc[...] += dot_tn(mix_ref[0], low[...])

        @pl.when(at == slots - 1)
        def _():
            if flat is None:
                gout_ref[...] = acc[...].astype(BF16)
            else:
                stage[...] = acc[...].astype(BF16)
                copy_all(n[1], (keep_ref, send_ref), stage, flat, 1, sems)

    wide = (slots, tok_rows, width)
    one = slot(tok_rows, width)
    args = (residual, d_inner, d_merged, mixed, w_out, gains)
    specs = [one, one, one, one, whole(*w_out.shape), whole(*gains.shape)]
    scratch = [pltpu.VMEM((tok_rows, width), BF16), pltpu.VMEM(w_out.shape, F32)]
    grads, alias = [(w_out.shape, BF16, result(*w_out.shape))], ()
    if flat is not None:
        args, specs, grads = args + kept, specs + [pl.BlockSpec(memory_space=pl.ANY)] * 2, bundles(flat, 2)
        scratch += [pltpu.VMEM(w_out.shape, BF16), copy_semaphores(flat, 1)]
        alias = ((6, 3), (7, 4))
    return run(
        "vit_back",
        body,
        (slots,),
        live,
        args,
        specs,
        [(wide, F32, one), (wide, BF16, one), ((8, width), F32, result(8, width))] + grads,
        scratch,
        after=after,
        alias=alias,
    )


def attention_back(live, probs, q, kv, d_mixed, after):
    slots, _, key_rows, tok_rows = probs.shape
    width = q.shape[2]
    head = width // HEADS
    pairs = width // LANES
    per_tile = LANES // head
    scale = 1.0 / math.sqrt(head)

    def body(n, p_ref, q_ref, k_ref, v_ref, dm_ref, dq_ref, dk_ref, dv_ref):
        @pl.when(pl.program_id(0) < n[0])
        def _():
            lane = lax.broadcasted_iota(jnp.int32, (1, LANES), 1) // head
            q = q_ref[0].astype(F32) * scale
            v = v_ref[0].astype(F32)
            dm = dm_ref[0].astype(F32)
            dm_low = dm_ref[0]
            k_flip = flip(k_ref[0].astype(F32) * scale)
            d_keys = jnp.zeros((key_rows, LANES), F32)
            d_values = jnp.zeros((key_rows, LANES), F32)
            d_query = []
            for h in range(per_tile):
                own = lane == h
                probs_low = p_ref[0, h]
                d_probs = dot_nt(jnp.where(own, v, 0.0).astype(BF16), dm_low)
                d_values += dot_nn(probs_low, jnp.where(own, dm, 0.0).astype(BF16))
                wide = probs_low.astype(F32)
                d_scores = (wide * (d_probs - col_sum(wide * d_probs))).astype(BF16)
                d_keys += dot_nn(d_scores, jnp.where(own, q, 0.0).astype(BF16))
                d_query.append(dot_nn(k_flip[h * head : (h + 1) * head, :], d_scores))
            dq_ref[0] = jnp.concatenate(d_query, axis=0).T.astype(BF16)
            dk_ref[0] = d_keys.astype(BF16)
            dv_ref[0] = d_values.astype(BF16)

    def held_pair(i, p, n):
        return jnp.where(i < n[0], p, pairs - 1)

    def at_pair(rows, shift=0):
        return pl.BlockSpec(
            (1, rows, LANES), lambda i, p, n: (held(i, n), 0, held_pair(i, p, n) + shift)
        )

    own = at_pair(tok_rows)
    keys = at_pair(key_rows)
    return run(
        "attention_back",
        body,
        (slots, pairs),
        live,
        (probs, q, kv, kv, d_mixed),
        [
            pl.BlockSpec(
                (1, per_tile, key_rows, tok_rows),
                lambda i, p, n: (held(i, n), held_pair(i, p, n), 0, 0),
            ),
            own,
            keys,
            at_pair(key_rows, pairs),
            own,
        ],
        [
            (q.shape, BF16, own),
            ((slots, key_rows, width), BF16, keys),
            ((slots, key_rows, width), BF16, keys),
        ],
        after=after,
    )


def qkv_back(live, normed, d_q, d_k, d_v, w_qkv, flat, kept, after):
    slots, key_rows, width = normed.shape
    tok_rows = d_q.shape[1]

    def body(n, x_ref, dq_ref, dk_ref, dv_ref, w_ref, *rest):
        if flat is None:
            dn_ref, gw_ref, x_flip, acc = rest
        else:
            _, _, dn_ref, keep_ref, send_ref, x_flip, acc, stage, sems = rest
        at = pl.program_id(0)

        @pl.when(at == 0)
        def _():
            acc[...] = jnp.zeros(acc.shape, F32)

        @pl.when(at < n[0])
        def _():
            x_flip[...] = flip(x_ref[0])
            dn_ref[0] = dot_nt(dk_ref[0], w_ref[:, width : 2 * width])
            dn_ref[0] += dot_nt(dv_ref[0], w_ref[:, 2 * width :])
            dn_ref[0, 0:tok_rows, :] += dot_nt(dq_ref[0], w_ref[:, 0:width])
            acc[:, 0:width] += dot_nn(x_flip[:, 0:tok_rows], dq_ref[0])
            acc[:, width : 2 * width] += dot_nn(x_flip[...], dk_ref[0])
            acc[:, 2 * width :] += dot_nn(x_flip[...], dv_ref[0])

        @pl.when(at == slots - 1)
        def _():
            if flat is None:
                gw_ref[...] = acc[...].astype(BF16)
            else:
                stage[...] = acc[...].astype(BF16)
                copy_all(n[1], (keep_ref, send_ref), stage, flat, 0, sems)

    keys = slot(key_rows, width)
    args = (normed, d_q, d_k, d_v, w_qkv)
    specs = [keys, slot(tok_rows, width), keys, keys, whole(*w_qkv.shape)]
    scratch = [pltpu.VMEM((width, key_rows), BF16), pltpu.VMEM(w_qkv.shape, F32)]
    grads, alias = [(w_qkv.shape, BF16, result(*w_qkv.shape))], ()
    if flat is not None:
        args, specs, grads = args + kept, specs + [pl.BlockSpec(memory_space=pl.ANY)] * 2, bundles(flat, 2)
        scratch += [pltpu.VMEM(w_qkv.shape, BF16), copy_semaphores(flat, 0)]
        alias = ((5, 1), (6, 2))
    return run(
        "qkv_back",
        body,
        (slots,),
        live,
        args,
        specs,
        [(normed.shape, F32, keys)] + grads,
        scratch,
        after=after,
        alias=alias,
    )


def tokens_back(live, tokens, d_norm, arrived, d_residual, gains, after):
    slots, tok_rows, width = tokens.shape

    def body(n, x_ref, dn_ref, more_ref, dres_ref, g_ref, out_ref, sums_ref):
        at = pl.program_id(0)

        @pl.when(at == 0)
        def _():
            sums_ref[...] = jnp.zeros(sums_ref.shape, F32)

        @pl.when(at < n[0])
        def _():
            def back(rows):
                value, inverse = unit(x_ref[0, rows, :].astype(F32))
                e = dn_ref[0, rows, :] + more_ref[0, rows, :].astype(F32)
                sums_ref[0:1, :] += col_sum(e * value)
                sums_ref[1:2, :] += col_sum(e)
                grad = dres_ref[0, rows, :] + unit_back(value, inverse, e * g_ref[0:1, :])
                out_ref[0, rows, :] = grad.astype(BF16)

            over_rows(tok_rows, back)

        @pl.when(at >= n[0])
        def _():
            out_ref[...] = jnp.zeros(out_ref.shape, BF16)

    one = slot(tok_rows, width)
    return run(
        "tokens_back",
        body,
        (slots,),
        live,
        (tokens, d_norm, arrived, d_residual, gains),
        [one, one, one, one, whole(*gains.shape)],
        [
            (tokens.shape, BF16, every_slot(tok_rows, width)),
            ((8, width), F32, result(8, width)),
        ],
        after=after,
    )


def stage_rows(frame, top_ref, mid_ref, bottom_ref, lanes):
    rows, cols = mid_ref.shape[1], mid_ref.shape[2]
    inside = slice(EDGE, EDGE + cols)
    frame[0:REACH, inside, :] = top_ref[0, :, :, lanes].astype(F32)
    frame[REACH : REACH + rows, inside, :] = mid_ref[0, :, :, lanes].astype(F32)
    frame[REACH + rows :, inside, :] = bottom_ref[0, :, :, lanes].astype(F32)


def depthwise_rows(frame, rows, cols, tap, flipped, emit):
    totals = {}
    for y in range(rows + 2 * REACH):
        for left in range(KS):
            shifted = frame[y, EDGE - REACH + left : EDGE - REACH + left + cols, :]
            for top in range(KS):
                out = y - top
                if 0 <= out < rows:
                    at = (KS - 1 - top) * KS + KS - 1 - left if flipped else top * KS + left
                    term = shifted * tap(at)
                    totals[out] = totals[out] + term if out in totals else term
        if y >= 2 * REACH:
            emit(y - 2 * REACH, totals.pop(y - 2 * REACH))


def conv_front(live, top, high, bottom, kernel, gains, shifts, after):
    slots, rows, cols, channels = high.shape
    cells = rows * cols

    def body(
        n, top_ref, mid_ref, bottom_ref, k_ref, g_ref, b_ref,
        spatial_ref, flip_ref, unit_ref, inv_ref, frame, middle,
    ):
        @pl.when(pl.program_id(0) < n[0])
        def _():
            frame[...] = jnp.zeros(frame.shape, F32)

            def tile(at, carry):
                lanes = lane_tile(at)
                stage_rows(frame, top_ref, mid_ref, bottom_ref, lanes)
                bias = b_ref[0:1, lanes]

                def emit(y, total):
                    middle[y * cols : (y + 1) * cols, lanes] = total + bias

                depthwise_rows(frame, rows, cols, lambda t: k_ref[t : t + 1, lanes], False, emit)
                return carry

            lax.fori_loop(0, channels // LANES, tile, 0)

            def norm(part):
                value, inverse = unit(middle[part, :])
                inv_ref[0, part, :] = inverse
                unit_ref[0, part, :] = value.astype(BF16)
                spatial_ref[0, part, :] = (value * g_ref[0:1, :] + b_ref[1:2, :]).astype(BF16)

            over_rows(cells, norm)
            flip_ref[0] = flip(spatial_ref[0])

    halo = slot(REACH, cols, channels)
    return run(
        "conv_front",
        body,
        (slots,),
        live,
        (top, high, bottom, kernel, gains, shifts),
        [halo, slot(rows, cols, channels), halo, whole(*kernel.shape)]
        + [whole(*gains.shape), whole(*shifts.shape)],
        [
            ((slots, cells, channels), BF16, slot(cells, channels)),
            ((slots, channels, cells), BF16, slot(channels, cells)),
            ((slots, cells, channels), BF16, slot(cells, channels)),
            ((slots, cells, 1), F32, slot(cells, 1)),
        ],
        [
            pltpu.VMEM((rows + 2 * REACH, cols + 2 * EDGE, LANES), F32),
            pltpu.VMEM((cells, channels), F32),
        ],
        after=after,
    )


def conv_mlp(live, spatial, high, w_pw1, w_pw2, gains, after):
    slots, cells, channels = spatial.shape
    hidden = w_pw1.shape[1]
    block = 1024
    steps = hidden // block

    def body(
        n, x_ref, high_ref, w1_ref, w2_ref, g_ref, act_ref, slope_ref, branch_ref, out_ref, acc
    ):
        at, step = pl.program_id(0), pl.program_id(1)

        @pl.when((at < n[0]) & (step == 0))
        def _():
            acc[...] = jnp.zeros(acc.shape, F32)

        @pl.when(at < n[0])
        def _():
            parts = [slice(0, cells // 2), slice(cells // 2, cells)]
            hidden_parts = [dot_nn(x_ref[0, rows, :], w1_ref[...]) for rows in parts]
            for rows, value in zip(parts, hidden_parts):
                act, slope = gelu_pair(value)
                act = act.astype(BF16)
                act_ref[0, rows, :] = act
                slope_ref[0, rows, :] = slope.astype(BF16)
                acc[rows, :] += dot_nn(act, w2_ref[...])

            @pl.when(step == steps - 1)
            def _():
                def close(rows):
                    branch = acc[rows, :]
                    branch_ref[0, rows, :] = branch.astype(BF16)
                    out_ref[0, rows, :] = (
                        high_ref[0, rows, :].astype(F32) + g_ref[1:2, :] * branch
                    ).astype(BF16)

                over_rows(cells, close)

        @pl.when((at >= n[0]) & (step == 0))
        def _():
            out_ref[...] = jnp.zeros(out_ref.shape, BF16)

    def held_step(i, j, n):
        return jnp.where(i < n[0], j, steps - 1)

    one = slot(cells, channels)
    hidden_block = pl.BlockSpec(
        (1, cells, block), lambda i, j, n: (held(i, n), 0, held_step(i, j, n))
    )
    return run(
        "conv_mlp",
        body,
        (slots, steps),
        live,
        (spatial, high, w_pw1, w_pw2, gains),
        [
            one,
            one,
            pl.BlockSpec((channels, block), lambda i, j, n: (0, held_step(i, j, n))),
            pl.BlockSpec((block, channels), lambda i, j, n: (held_step(i, j, n), 0)),
            whole(*gains.shape),
        ],
        [
            ((slots, cells, hidden), BF16, hidden_block),
            ((slots, cells, hidden), BF16, hidden_block),
            (spatial.shape, BF16, one),
            (spatial.shape, BF16, every_slot(cells, channels)),
        ],
        [pltpu.VMEM((cells, channels), F32)],
        after=after,
    )


def pool(live, high_out, bins, side):
    slots, cells, channels = high_out.shape
    tok_rows = bins.shape[0] - 2 * side

    def body(n, x_ref, p_ref, own_ref, before_ref, after_ref):
        @pl.when(pl.program_id(0) < n[0])
        def _():
            part = dot_nn(p_ref[...], x_ref[0])
            before_ref[0] = part[0:side].astype(BF16)
            own_ref[0] = part[side : side + tok_rows]
            after_ref[0] = part[side + tok_rows :].astype(BF16)

    return run(
        "pool",
        body,
        (slots,),
        live,
        (high_out, bins),
        [slot(cells, channels), whole(*bins.shape)],
        [
            ((slots, tok_rows, channels), F32, slot(tok_rows, channels)),
            ((slots, side, channels), BF16, slot(side, channels)),
            ((slots, side, channels), BF16, slot(side, channels)),
        ],
    )


def adapter(live, own, first, last, d_merged, w_pool, w_gate, after):
    slots, tok_rows, channels = own.shape
    side = first.shape[1]
    width = w_pool.shape[1]

    def body(
        n, own_ref, first_ref, last_ref, dm_ref, w_ref, gate_ref,
        lift_ref, dpool_ref, gw_ref, ggate_ref, acc,
    ):
        at = pl.program_id(0)

        @pl.when(at == 0)
        def _():
            acc[...] = jnp.zeros(acc.shape, F32)
            ggate_ref[...] = jnp.zeros(ggate_ref.shape, F32)

        @pl.when(at < n[0])
        def _():
            pooled_low = jnp.concatenate(
                [
                    own_ref[0, 0:side] + first_ref[0].astype(F32),
                    own_ref[0, side : tok_rows - side],
                    own_ref[0, tok_rows - side :] + last_ref[0].astype(F32),
                ],
                axis=0,
            ).astype(BF16)
            pooled = pooled_low.astype(F32)
            lifted = dot_nn(pooled_low, w_ref[...])
            logit = jnp.sum(pooled * gate_ref[...], axis=-1, keepdims=True)
            gate = 1.0 / (1.0 + jnp.exp(-logit))
            lift_ref[0] = gate * lifted
            d_top = dm_ref[0].astype(F32)
            d_logit = jnp.sum(d_top * lifted, axis=-1, keepdims=True) * gate * (1.0 - gate)
            d_lifted = (gate * d_top).astype(BF16)
            acc[...] += dot_tn(pooled_low, d_lifted)
            ggate_ref[0:1, :] += col_sum(d_logit * pooled)
            dpool_ref[0] = (dot_nt(d_lifted, w_ref[...]) + d_logit * gate_ref[...]).astype(BF16)

        @pl.when(at == slots - 1)
        def _():
            gw_ref[...] = acc[...].astype(BF16)

    edge = slot(side, channels)
    return run(
        "adapter",
        body,
        (slots,),
        live,
        (own, first, last, d_merged, w_pool, w_gate),
        [slot(tok_rows, channels), edge, edge, slot(tok_rows, width)]
        + [whole(*w_pool.shape), whole(*w_gate.shape)],
        [
            ((slots, tok_rows, width), F32, slot(tok_rows, width)),
            (own.shape, BF16, slot(tok_rows, channels)),
            (w_pool.shape, BF16, result(*w_pool.shape)),
            ((8, channels), F32, result(8, channels)),
        ],
        [pltpu.VMEM(w_pool.shape, F32)],
        after=after,
    )


def unpool(live, near, spread, d_conv, branch, gains):
    slots, near_rows, channels = near.shape
    cells = d_conv.shape[1]

    def body(n, near_ref, s_ref, dc_ref, branch_ref, g_ref, dpost_ref, dbranch_ref, sums_ref):
        at = pl.program_id(0)

        @pl.when(at == 0)
        def _():
            sums_ref[...] = jnp.zeros(sums_ref.shape, F32)

        @pl.when(at < n[0])
        def _():
            def part(rows):
                d_post = dc_ref[0, rows, :].astype(F32) + dot_nn(s_ref[rows, :], near_ref[0])
                sums_ref[0:1, :] += col_sum(d_post * branch_ref[0, rows, :].astype(F32))
                dpost_ref[0, rows, :] = d_post.astype(BF16)
                dbranch_ref[0, rows, :] = (g_ref[1:2, :] * d_post).astype(BF16)

            over_rows(cells, part)

    one = slot(cells, channels)
    return run(
        "unpool",
        body,
        (slots,),
        live,
        (near, spread, d_conv, branch, gains),
        [slot(near_rows, channels), whole(*spread.shape), one, one, whole(*gains.shape)],
        [
            (d_conv.shape, BF16, one),
            (d_conv.shape, BF16, one),
            ((8, channels), F32, result(8, channels)),
        ],
    )


def conv_mlp_back(live, spatial_flip, act, slope, d_branch, w_pw1, w_pw2, grad_pool, flat, after):
    slots, channels, cells = spatial_flip.shape
    hidden = w_pw1.shape[1]
    block = 2 * BLOCK
    steps = hidden // block
    blocks = channels // BLOCK

    def body(
        n, xt_ref, act_ref, slope_ref, db_ref, w1_ref, w2_ref, pool_ref, dsp_ref, *rest
    ):
        if flat is None:
            out1_ref, out2_ref, a1, a2, dsp, sem = rest
        else:
            refs, (a1, a2, dsp, sem, stage1, stage2, sems1, sems2, sems3) = rest[:4], rest[4:]
        step = pl.program_id(0)

        @pl.when(step == 0)
        def _():
            dsp[...] = jnp.zeros(dsp.shape, F32)

        a1[...] = jnp.zeros(a1.shape, F32)
        a2[...] = jnp.zeros(a2.shape, F32)

        def one(at, carry):
            d_hidden = dot_nt(db_ref[at], w2_ref[...])
            d_expand = (slope_ref[at].astype(F32) * d_hidden).astype(BF16)
            a2[...] += dot_tn(act_ref[at], db_ref[at])
            a1[...] += dot_nn(xt_ref[at], d_expand)
            dsp[at] += dot_nt(d_expand, w1_ref[...])
            return carry

        lax.fori_loop(0, n[0], one, 0)

        @pl.when(step == steps - 1)
        def _():
            out = pltpu.make_async_copy(dsp, dsp_ref, sem)
            out.start()
            out.wait()

        if flat is None:
            out1_ref[...] = a1[...].astype(BF16)
            out2_ref[...] = a2[...].astype(BF16)
            return

        def first_copies(at):
            out = []
            for index, (k, _, rows, start) in enumerate(flat.pieces[0]):
                place = pl.multiple_of(start + at * 2 * rows, 16)
                out.append((k, stage1.at[index, pl.ds(0, 2 * rows), :], place, 2 * rows))
            return out

        def second_copies(at):
            out = []
            for k, row, rows, start, height in flat.within(1, at * block, block):
                for c in range(blocks):
                    source = block_of(stage2, row - at * block, rows, c)
                    out.append((k, source, start + c * height, rows))
            return out

        def pool_copies():
            out = []
            for k, row, rows, start in flat.pieces[2]:
                for c in range(flat.shapes[2][1] // BLOCK):
                    out.append((k, block_of(pool_ref, row, rows, c), start + c * rows, rows))
            return out

        def firsts(now, action):
            copy_out(n[1], refs, first_copies(now), sems1, action)

        def seconds(now, action):
            for static in range(steps):

                @pl.when(now == static)
                def _(static=static):
                    copy_out(n[1], refs, second_copies(static), sems2, action)

        @pl.when(step == 0)
        def _():
            copy_out(n[1], refs, pool_copies(), sems3, "start")

        @pl.when(step > 0)
        def _():
            seconds(step - 1, "wait")
            firsts(step - 1, "wait")

        stage2[...] = a2[...].astype(BF16)
        seconds(step, "start")
        for index, (_, row, rows, _) in enumerate(flat.pieces[0]):
            part = a1[row : row + rows, :]
            both = jnp.concatenate([part[:, 0:BLOCK], part[:, BLOCK:]], axis=0)
            stage1[index, 0 : 2 * rows, :] = both.astype(BF16)
        firsts(step, "start")

        @pl.when(step == steps - 1)
        def _():
            seconds(step, "wait")
            firsts(step, "wait")
            copy_out(n[1], refs, pool_copies(), sems3, "wait")

    by_col = pl.BlockSpec((channels, block), lambda j, n: (0, j))
    by_row = pl.BlockSpec((block, channels), lambda j, n: (j, 0))
    by_hidden = pl.BlockSpec((slots, cells, block), lambda j, n: (0, 0, j))
    wide = (slots, cells, channels)
    scratch = [
        pltpu.VMEM((channels, block), F32),
        pltpu.VMEM((block, channels), F32),
        pltpu.VMEM(wide, F32),
        pltpu.SemaphoreType.DMA,
    ]
    if flat is None:
        grads = [(w_pw1.shape, BF16, by_col), (w_pw2.shape, BF16, by_row)]
    else:
        grads = bundles(flat, 4)
        most = max(len(flat.within(1, at * block, block)) for at in range(steps))
        tall = max(rows for _, _, rows, _ in flat.pieces[0])
        scratch += [
            pltpu.VMEM((len(flat.pieces[0]), 2 * tall, BLOCK), BF16),
            pltpu.VMEM((block, channels), BF16),
            pltpu.SemaphoreType.DMA((len(flat.pieces[0]),)),
            pltpu.SemaphoreType.DMA((most * blocks,)),
            copy_semaphores(flat, 2),
        ]
    return run(
        "conv_mlp_back",
        body,
        (steps,),
        live,
        (spatial_flip, act, slope, d_branch, w_pw1, w_pw2, grad_pool),
        [whole(*spatial_flip.shape), by_hidden, by_hidden, whole(*wide), by_col, by_row, ANYWHERE],
        [(wide, F32, ANYWHERE)] + grads,
        scratch,
        after=after,
    )


def conv_norm_back(live, d_spatial, unit_values, inverse, gains, after):
    slots, cells, channels = d_spatial.shape

    def body(n, e_ref, u_ref, inv_ref, g_ref, out_ref, sums_ref):
        at = pl.program_id(0)

        @pl.when(at == 0)
        def _():
            sums_ref[...] = jnp.zeros(sums_ref.shape, F32)

        @pl.when(at < n[0])
        def _():
            def part(rows):
                e = e_ref[0, rows, :]
                value = u_ref[0, rows, :].astype(F32)
                sums_ref[0:1, :] += col_sum(e * value)
                sums_ref[1:2, :] += col_sum(e)
                grad = unit_back(value, inv_ref[0, rows, :], e * g_ref[0:1, :])
                sums_ref[2:3, :] += col_sum(grad)
                out_ref[0, rows, :] = grad.astype(BF16)

            over_rows(cells, part)

    one = slot(cells, channels)
    return run(
        "conv_norm_back",
        body,
        (slots,),
        live,
        (d_spatial, unit_values, inverse, gains),
        [one, one, slot(cells, 1), whole(*gains.shape)],
        [(d_spatial.shape, BF16, one), ((8, channels), F32, result(8, channels))],
        after=after,
    )


def conv_back(live, d_top, d_mid, d_bottom, d_post, kernel, after):
    slots, rows, cols, channels = d_mid.shape

    def body(n, dt_ref, dm_ref, db_ref, dpost_ref, k_ref, out_ref, frame):
        at = pl.program_id(0)

        @pl.when(at < n[0])
        def _():
            frame[...] = jnp.zeros(frame.shape, F32)

            def tile(tile_at, carry):
                lanes = lane_tile(tile_at)
                stage_rows(frame, dt_ref, dm_ref, db_ref, lanes)

                def emit(y, total):
                    grad = total + dpost_ref[0, y, :, lanes].astype(F32)
                    out_ref[0, y, :, lanes] = grad.astype(BF16)

                depthwise_rows(frame, rows, cols, lambda t: k_ref[t : t + 1, lanes], True, emit)
                return carry

            lax.fori_loop(0, channels // LANES, tile, 0)

        @pl.when(at >= n[0])
        def _():
            out_ref[...] = jnp.zeros(out_ref.shape, BF16)

    halo = slot(REACH, cols, channels)
    one = slot(rows, cols, channels)
    return run(
        "conv_back",
        body,
        (slots,),
        live,
        (d_top, d_mid, d_bottom, d_post, kernel),
        [halo, one, halo, one, whole(*kernel.shape)],
        [(d_mid.shape, BF16, every_slot(rows, cols, channels))],
        [pltpu.VMEM((rows + 2 * REACH, cols + 2 * EDGE, LANES), F32)],
        after=after,
    )[0]


def kernel_back(live, top, high, bottom, d_mid, half, after):
    slots, rows, cols, channels = high.shape
    channels = channels // 2

    def body(n, top_ref, mid_ref, bottom_ref, dm_ref, gk_ref, frame, d_rows):
        at = pl.program_id(0)

        @pl.when(at == 0)
        def _():
            gk_ref[...] = jnp.zeros(gk_ref.shape, F32)

        @pl.when(at < n[0])
        def _():
            frame[...] = jnp.zeros(frame.shape, F32)

            def tile(tile_at, carry):
                lanes = lane_tile(tile_at)
                stage_rows(frame, top_ref, mid_ref, bottom_ref, lanes)
                d_rows[...] = dm_ref[0, :, :, lanes].astype(F32)
                for left in range(KS):
                    totals = [None] * KS
                    grads = {}
                    begin = EDGE - REACH + left
                    for y in range(rows + 2 * REACH):
                        shifted = frame[y, begin : begin + cols, :].reshape(cols // 8, 8, LANES)
                        if y < rows:
                            grads[y] = d_rows[y].reshape(cols // 8, 8, LANES)
                        for tap_row in range(KS):
                            row = y - tap_row
                            if 0 <= row < rows:
                                term = jnp.sum(shifted * grads[row], axis=0)
                                old = totals[tap_row]
                                totals[tap_row] = term if old is None else old + term
                        grads.pop(y - KS + 1, None)
                    for tap_row in range(KS):
                        tap = tap_row * KS + left
                        gk_ref[tap : tap + 1, lanes] += col_sum(totals[tap_row])
                return carry

            lax.fori_loop(0, channels // LANES, tile, 0)

    def half_slot(*shape):
        return pl.BlockSpec((1,) + shape, lambda i, n: (held(i, n), 0, 0, half))

    halo = half_slot(REACH, cols, channels)
    one = half_slot(rows, cols, channels)
    return run(
        "kernel_back",
        body,
        (slots,),
        live,
        (top, high, bottom, d_mid),
        [halo, one, halo, one],
        [((64, channels), F32, result(64, channels))],
        [
            pltpu.VMEM((rows + 2 * REACH, cols + 2 * EDGE, LANES), F32),
            pltpu.VMEM((rows, cols, LANES), F32),
        ],
        after=after,
    )[0]


def from_both_sides(head, tail):
    count = lax.axis_size("strip")
    if count == 2:
        upper = lax.axis_index("strip") == 0
        got = lax.ppermute(jnp.where(upper, tail, head), "strip", [(0, 1), (1, 0)])
        return jnp.where(upper, jnp.zeros_like(got), got), jnp.where(upper, got, jnp.zeros_like(got))
    before = lax.ppermute(tail, "strip", [(i, i + 1) for i in range(count - 1)])
    after = lax.ppermute(head, "strip", [(i + 1, i) for i in range(count - 1)])
    return before, after


def bin_weights(edges, cell_count):
    cells = jnp.arange(cell_count, dtype=jnp.int32)
    inside = (cells[None, :] >= edges[:-1, None]) & (cells[None, :] < edges[1:, None])
    widths = (edges[1:] - edges[:-1]).astype(F32)
    return inside.astype(F32) / widths[:, None]


def strip_bins(edges, first_bin, bin_count, first_cell, cell_count):
    padded = jnp.concatenate([edges[:1], edges, edges[-1:]])
    window = lax.dynamic_slice_in_dim(padded, first_bin + 1, bin_count + 1)
    cells = first_cell + jnp.arange(cell_count, dtype=jnp.int32)
    inside = (cells[None, :] >= window[:-1, None]) & (cells[None, :] < window[1:, None])
    widths = jnp.maximum(window[1:] - window[:-1], 1).astype(F32)
    return inside.astype(F32) / widths[:, None]


def bit_of(axis, bit):
    return (lax.axis_index(axis) >> bit) & 1


def swap_halves(cells, axis, bit, own):
    size = lax.axis_size(axis)
    keep = lax.dynamic_index_in_dim(cells, own, 1, keepdims=False)
    send = lax.dynamic_index_in_dim(cells, 1 - own, 1, keepdims=False)
    got = lax.ppermute(send, axis, [(i, i ^ (1 << bit)) for i in range(size)])
    return (keep.astype(F32) + got.astype(F32)).astype(BF16)


def sum_over(axis, values, steps=None, above=1):
    size = lax.axis_size(axis)
    if steps is None:
        steps = [1 << bit for bit in range(bits(axis)) if 1 << bit >= above]
    for step in steps:
        values = values + lax.ppermute(values, axis, [(i, i ^ step) for i in range(size)])
    return values


def bits(axis):
    return int(math.log2(lax.axis_size(axis)))


def halve_dp(cells, base, bit):
    if cells.shape[0] % 2:
        cells = jnp.pad(cells, [(0, 1)] + [(0, 0)] * (cells.ndim - 1))
    own = (bit_of("dp", bit) - base) & 1
    cells = cells.reshape((cells.shape[0] // 2, 2) + cells.shape[1:])
    return swap_halves(cells, "dp", bit, own), (base + own) >> 1


def halve_strip(cells):
    for bit in range(bits("strip")):
        m, count = cells.shape[:2]
        cells = cells.reshape((m * count // 2, 2) + cells.shape[2:])
        cells = swap_halves(cells, "strip", bit, bit_of("strip", bit))
        cells = cells.reshape((m, count // 2) + cells.shape[1:])
    return cells


def shared_sum(matrix, offset, chunk, strip_first):
    strips = lax.axis_size("strip")
    rows, cols = matrix.shape
    chunk_rows = chunk // cols
    base = offset // (chunk * strips)
    front = (offset - base * chunk * strips) // cols
    groups = -(-(front + rows) // (chunk_rows * strips))
    back = groups * chunk_rows * strips - front - rows
    cells = jnp.pad(matrix, ((front, back), (0, 0))).reshape(groups, strips, chunk_rows, cols)
    cells, base = halve_dp(cells, base, 0)
    if strip_first:
        cells = halve_strip(cells)
        cells, base = halve_dp(cells, base, 1)
    else:
        cells, base = halve_dp(cells, base, 1)
        cells = halve_strip(cells)
    return cells.reshape(cells.shape[0], chunk), base


def owned_chunk(matrices, extras):
    data_count = lax.axis_size("dp")
    strips = lax.axis_size("strip")
    devices = data_count * strips
    chunk = sum(m.size for m in matrices) // devices
    span = data_count // 4
    placed = None
    offset = 0
    for order, matrix in enumerate(matrices):
        part, base = shared_sum(matrix, offset, chunk, order % 2 == 0)
        canvas = jnp.zeros((span + part.shape[0], chunk), BF16)
        canvas = lax.dynamic_update_slice(canvas, part, (base, 0))[:span]
        placed = canvas if placed is None else placed + canvas
        offset += matrix.size
    for bit in range(2, bits("dp")):
        placed = placed.reshape(placed.shape[0] // 2, 2, chunk)
        placed = swap_halves(placed, "dp", bit, bit_of("dp", bit))
    return share_of(placed.reshape(chunk).astype(F32), chunk, extras)


STEPS = {
    "core": ("dp", 1, lambda dp, strip: dp & 1),
    "x": ("strip", 1, lambda dp, strip: strip & 1),
    "y": ("dp", 2, lambda dp, strip: (dp >> 1) & 1),
    "z": ("dp", 4, lambda dp, strip: ((dp >> 2) ^ (dp >> 3)) & 1),
    "far": ("dp", 12, lambda dp, strip: (dp >> 3) & 1),
}
ORDERS = (("x", "y", "z"), ("y", "z", "x"), ("z", "x", "y"))


def across(step, value):
    axis, flip_bits, _ = STEPS[step]
    return lax.ppermute(value, axis, [(i, i ^ flip_bits) for i in range(lax.axis_size(axis))])


def relay(live, values, after=()):
    def body(_, *refs):
        pass

    outs = [(v.shape, v.dtype, ANYWHERE) for v in values]
    alias = tuple((i, i) for i in range(len(values)))
    specs = [ANYWHERE] * len(values)
    return run("relay", body, (1,), live, tuple(values), specs, outs, after=after, alias=alias)


def split_sum(flat, sets, level, after, through):
    parts = len(ORDERS)
    rows = flat.units // parts
    count = sets[0][0][0].shape[0] // 2
    own = [STEPS[order[level]][2](lax.axis_index("dp"), lax.axis_index("strip")) for order in ORDERS]
    bits = jnp.stack(own).astype(jnp.int32)
    specs, args = [], []
    for number, (kept, arrived) in enumerate(sets):
        for part, order in enumerate(ORDERS):
            left = [name for name in ("z", "y", "x") if name not in order[:level]]
            low = len(left) - 1 - left.index(order[level])

            for flipped in (0, 1):

                def place(i, bit, part=part, low=low, flipped=flipped, first=number * count):
                    i = jnp.clip(i - first, 0, count - 1)
                    mine = bit[part] ^ flipped
                    index = ((i >> low) << (low + 1)) | (mine << low) | (i & ((1 << low) - 1))
                    return index, part if level == 0 else 0, 0

                for source in (kept, arrived):
                    args.append(source[0 if level == 0 else part])
                    specs.append(pl.BlockSpec((1, rows, BLOCK), place))
    given = len(args)

    def body(_, *refs):
        outs = refs[given + len(through) :]
        for number in range(len(sets)):
            ins = refs[number * 4 * parts : (number + 1) * 4 * parts]

            @pl.when(pl.program_id(0) // count == number)
            def _(ins=ins):
                for at in range(2 * parts):
                    total = ins[2 * at][...].astype(F32) + ins[2 * at + 1][...].astype(F32)
                    outs[at][...] = total.astype(BF16)

    out = pl.BlockSpec((1, rows, BLOCK), lambda i, bit: (i, 0, 0))
    done = run(
        "split_sum",
        body,
        (len(sets) * count,),
        bits,
        tuple(args) + tuple(through),
        specs + [ANYWHERE] * len(through),
        [((len(sets) * count, rows, BLOCK), BF16, out)] * (2 * parts)
        + [(v.shape, v.dtype, ANYWHERE) for v in through],
        after=after,
        alias=tuple((given + i, 2 * parts + i) for i in range(len(through))),
    )
    return done[0 : 2 * parts : 2], done[1 : 2 * parts : 2], done[2 * parts :]


class Bundle:
    def __init__(self, flat, kept, send):
        self.flat, self.level = flat, 0
        self.kept, self.arrived = [kept], [across("core", send)]

    def step(self, after, through=(), other=None):
        sets = [(b.kept, b.arrived) for b in (self, other) if b is not None]
        self.kept, sends, passed = split_sum(self.flat, sets, self.level, after, through)
        self.arrived = [across(order[self.level], v) for order, v in zip(ORDERS, sends)]
        self.level += 1
        return (self.kept[0],), passed

    def last_step(self):
        parts = [k.astype(F32) + a.astype(F32) for k, a in zip(self.kept, self.arrived)]
        low, high = jnp.concatenate(parts, axis=1).astype(BF16)
        is_upper = STEPS["far"][2](lax.axis_index("dp"), lax.axis_index("strip")) == 1
        self.kept = [jnp.where(is_upper, high, low)]
        self.arrived = [across("far", jnp.where(is_upper, low, high))]

    def chunk(self):
        return self.kept[0].astype(F32) + self.arrived[0].astype(F32)


def row_major(flat, units):
    devices = lax.axis_size("dp") * lax.axis_size("strip")
    index = lax.axis_index("dp") * lax.axis_size("strip") + lax.axis_index("strip")
    kinds, kind_of = [], []
    for k in range(devices):
        kind = []
        for matrix, pieces in enumerate(flat.pieces):
            for chunk, _, rows, start in pieces:
                if chunk == k:
                    kind.append((start, rows, flat.shapes[matrix][1] // BLOCK))
        kind = tuple(kind)
        if kind not in kinds:
            kinds.append(kind)
        kind_of.append(kinds.index(kind))

    def ordered(kind):
        def branch(value):
            out = []
            for start, rows, blocks in kind:
                piece = value[start : start + rows * blocks].reshape(blocks, rows, BLOCK)
                out.append(piece.transpose(1, 0, 2).reshape(-1))
            return jnp.concatenate(out)

        return branch

    which = jnp.asarray(kind_of, jnp.int32)[index]
    return lax.switch(which, [ordered(kind) for kind in kinds], units)


def share_of(mine, chunk, extras):
    data_count = lax.axis_size("dp")
    strips = lax.axis_size("strip")
    devices = data_count * strips
    extra = extras.shape[0] // devices
    index = lax.axis_index("dp") * strips + lax.axis_index("strip")
    pieces = [mine]
    left = extras.shape[0]
    padded = jnp.pad(extras, (0, chunk))
    for hop in range(1, -(-left // chunk) + 1):
        size = min(left, chunk)
        left -= size
        following = lax.ppermute(
            mine[:size].astype(BF16),
            ("dp", "strip"),
            [(i + hop, i) for i in range(devices - hop)],
        ).astype(F32)
        past = index + hop - devices
        own_extras = lax.dynamic_slice(padded, (jnp.maximum(past, 0) * chunk,), (size,))
        pieces.append(jnp.where(past >= 0, own_extras, following))
    return lax.dynamic_slice(jnp.concatenate(pieces), (index * extra,), (chunk + extra,))


def per_device(
    low_tokens,
    high_map,
    counts,
    row_edges,
    col_edges,
    w_qkv,
    w_attn_out,
    w_fc1,
    w_fc2,
    vit_gains,
    vit_shifts,
    w_pw1,
    w_pw2,
    w_pool,
    dw_kernel,
    conv_gains,
    conv_shifts,
    w_gate,
    d_merged,
    d_conv,
):
    slots, tok_rows, width = low_tokens.shape
    rows, cols, channels = high_map.shape[1:]
    cells = rows * cols
    strips = lax.axis_size("strip")
    strip = lax.axis_index("strip")
    live = jnp.stack([counts[0], lax.axis_index("dp") & 1]).astype(jnp.int32)

    col_bins = bin_weights(col_edges, cols)
    side = col_bins.shape[0]
    own_bins = tok_rows // side
    near_bins = strip_bins(row_edges, strip * own_bins - 1, own_bins + 2, strip * rows, rows)
    bins = (near_bins[:, None, :, None] * col_bins[None, :, None, :]).astype(BF16)
    bins = bins.reshape((own_bins + 2) * side, cells)

    data_count = lax.axis_size("dp")
    devices = data_count * strips
    vit_flat = Flat([w.shape for w in (w_qkv, w_attn_out, w_fc1, w_fc2)], devices)
    conv_flat = Flat([w.shape for w in (w_pw1, w_pw2, w_pool)], devices)
    chunked = devices == 4 * BUNDLE and strips == 2 and vit_flat.even and conv_flat.even
    if not chunked:
        vit_flat = conv_flat = None

    def over_cores(value):
        return lax.ppermute(value, "dp", [(i, i ^ 1) for i in range(data_count)])

    def over_y(value):
        return lax.ppermute(value, "dp", [(i, i ^ 2) for i in range(data_count)])

    own_count = counts[0]
    lead = own_count - over_cores(counts)[0]
    lends, borrows = lead >= 2, lead <= -2
    after_cores = own_count - lends.astype(jnp.int32) + borrows.astype(jnp.int32)
    lead_y = after_cores - over_y(after_cores.reshape(1))[0]
    lends_y, borrows_y = lead_y >= 2, lead_y <= -2
    lent_slot = own_count - 1
    lent_slot_y = lent_slot - lends.astype(jnp.int32)
    kept_count = own_count - lends.astype(jnp.int32) - lends_y.astype(jnp.int32)
    guest_slot = kept_count
    guest_slot_y = kept_count + borrows.astype(jnp.int32)
    live = guest_slot_y + borrows_y.astype(jnp.int32)
    live = jnp.stack([live, lax.axis_index("dp") & 1]).astype(jnp.int32)

    def at_slot(condition, place, like):
        return (condition & (jnp.arange(slots) == place)).reshape((slots,) + (1,) * (like.ndim - 1))

    def one_slot(values, place):
        return lax.dynamic_index_in_dim(values, jnp.clip(place, 0, slots - 1), 0)

    def loans(values):
        return one_slot(values, lent_slot), one_slot(values, lent_slot_y)

    def taken(pair):
        return over_cores(pair[0]), over_y(pair[1])

    def with_guests(values, guests):
        values = jnp.where(at_slot(borrows, guest_slot, values), guests[0], values)
        return jnp.where(at_slot(borrows_y, guest_slot_y, values), guests[1], values)

    def sent_home(values):
        return over_cores(one_slot(values, guest_slot)), over_y(one_slot(values, guest_slot_y))

    def returned(values, home):
        own = (jnp.arange(slots) < kept_count).reshape((slots,) + (1,) * (values.ndim - 1))
        out = jnp.where(own, values, jnp.zeros_like(values))
        out = jnp.where(at_slot(lends, lent_slot, values), home[0], out)
        return jnp.where(at_slot(lends_y, lent_slot_y, values), home[1], out)

    def shifted(value, by):
        return lax.ppermute(value, "strip", [(i, (i + by) % strips) for i in range(strips)])

    edge_rows = jnp.concatenate([high_map[:, :REACH], high_map[:, -REACH:]], axis=1)
    guest_rows = jnp.concatenate(taken(loans(edge_rows)))
    guest_maps = taken(loans(high_map))
    halos = from_both_sides(high_map[:, :REACH], high_map[:, -REACH:])
    guest_halos = from_both_sides(guest_rows[:, :REACH], guest_rows[:, REACH:])
    top, bottom = (with_guests(h, (g[:1], g[1:])) for h, g in zip(halos, guest_halos))
    high_map = with_guests(high_map, guest_maps)
    both = [jnp.concatenate(pair, axis=1) for pair in zip(loans(low_tokens), loans(d_merged))]
    payloads = relay(live, both + list(loans(d_conv)), (top, bottom, high_map))
    both = taken(payloads[:2])
    low_tokens = with_guests(low_tokens, [guest[:, :tok_rows] for guest in both])
    d_merged = with_guests(d_merged, [guest[:, tok_rows:] for guest in both])
    d_conv = with_guests(d_conv, taken(payloads[2:]))
    spatial, spatial_flip, conv_unit, conv_inverse = conv_front(
        live, top, high_map, bottom, dw_kernel, conv_gains, conv_shifts, tuple(payloads[:1])
    )
    act, slope, branch, high_out = conv_mlp(
        live, spatial, high_map.reshape(slots, cells, channels), w_pw1, w_pw2, conv_gains,
        (low_tokens, d_merged),
    )
    own, before_part, after_part = pool(live, high_out, bins, side)
    first, last = from_both_sides(*relay(live, (before_part, after_part), (d_conv,)))
    lift, d_pooled, grad_pool, gate_sums = adapter(
        live, own, first, last, d_merged, w_pool, w_gate.reshape(1, channels), ()
    )
    (high_out,) = relay(live, (high_out,), (d_pooled,))
    high_home = sent_home(high_out)
    near_before, near_after = from_both_sides(d_pooled[:, :side], d_pooled[:, -side:])
    d_post, d_branch, scale_sums = unpool(
        live,
        jnp.concatenate([near_before, d_pooled, near_after], axis=1),
        bins.T,
        d_conv.reshape(slots, cells, channels),
        branch,
        conv_gains,
    )
    (low_tokens,) = relay(live, (low_tokens,), (d_branch,))
    tok_all = jnp.concatenate(
        [low_tokens] + [shifted(low_tokens, by) for by in range(1, strips)], axis=1
    )
    d_spatial, *grads_conv = conv_mlp_back(
        live, spatial_flip, act, slope, d_branch, w_pw1, w_pw2, grad_pool, conv_flat, (low_tokens,)
    )
    order = (d_spatial,) + high_home
    if chunked:
        sends = relay(live, (grads_conv[1], grads_conv[3]), high_home + (tok_all,))
        conv_lower = Bundle(conv_flat, grads_conv[0], sends[0])
        conv_upper = Bundle(conv_flat, grads_conv[2], sends[1])
        order = (conv_lower.kept[0],) + high_home
    d_conv_in, norm_sums = conv_norm_back(
        live, d_spatial, conv_unit, conv_inverse, conv_gains, order
    )
    normed, q, kv, probs, mixed, residual, inner, inner_flip = vit_front(
        live, tok_all, w_qkv, w_attn_out, vit_gains, vit_shifts, tok_rows, (d_conv_in,)
    )
    order = (inner,)
    if chunked:
        order, (d_conv_in,) = conv_lower.step(order, (d_conv_in,), conv_upper)
    d_conv_in = d_conv_in.reshape(high_map.shape)
    d_before, d_after = from_both_sides(d_conv_in[:, :REACH], d_conv_in[:, -REACH:])
    merged, d_inner, *grads_fc = vit_mlp(
        live, inner, inner_flip, d_merged, residual, lift, w_fc1, w_fc2, vit_flat, order
    )
    order = (d_inner, d_before, d_after)
    if chunked:
        order, (send,) = conv_lower.step(order, (grads_fc[3],))
        vit_upper = Bundle(vit_flat, grads_fc[2], send)
    d_residual, d_mixed, inner_sums, *grads_out = vit_back(
        live, residual, d_inner, d_merged, mixed, w_attn_out, vit_gains, vit_flat,
        tuple(grads_fc[:2]), order,
    )
    d_q, d_k, d_v = attention_back(live, probs, q, kv, d_mixed, (d_residual,))
    order = (d_q,)
    if chunked:
        order, _ = conv_lower.step(order + tuple(vit_upper.arrived))
    kernel_sums = [kernel_back(live, top, high_map, bottom, d_conv_in, 0, order)]
    order = (kernel_sums[0],)
    if chunked:
        order, (merged,) = vit_upper.step(order + tuple(conv_lower.arrived), (merged,))
        conv_lower.last_step()
    merged_home = sent_home(merged)
    kernel_sums.append(kernel_back(live, top, high_map, bottom, d_conv_in, 1, order))
    if chunked:
        _, kernel_sums = vit_upper.step(tuple(vit_upper.arrived), kernel_sums)
    kernel_sums = jnp.concatenate(kernel_sums, axis=1)
    conv_extras = jnp.concatenate(
        [
            kernel_sums[: KS * KS].reshape(-1),
            norm_sums[0],
            scale_sums[0],
            norm_sums[2],
            norm_sums[1],
            gate_sums[0],
        ]
    )
    conv_extras = sum_over("dp", conv_extras, (1, 2))
    d_normed, *grads_qkv = qkv_back(
        live, normed, d_q, d_k, d_v, w_qkv, vit_flat, tuple(grads_out), (kernel_sums,)
    )
    order = (conv_extras,)
    if chunked:
        order += tuple(vit_upper.arrived)
        d_normed, send = relay(live, (d_normed, grads_qkv[1]), order)
        vit_lower = Bundle(vit_flat, grads_qkv[0], send)
    d_other = jnp.zeros(low_tokens.shape, BF16)
    for by in range(1, strips):
        part = d_normed[:, by * tok_rows : (by + 1) * tok_rows].astype(BF16)
        d_other = d_other + shifted(part, -by) if by > 1 else shifted(part, -by)
    grad_map = conv_back(
        live, d_before, d_conv_in, d_after, d_post.reshape(high_map.shape), dw_kernel, (d_normed,)
    )
    order = (grad_map,)
    if chunked:
        order = (d_other, *merged_home)
        order, (grad_map, conv_extras) = vit_lower.step(order, (grad_map, conv_extras))
    grad_tokens, token_sums = tokens_back(
        live, low_tokens, d_normed, d_other, d_residual, vit_gains, order
    )
    if chunked:
        order = (token_sums, *conv_lower.arrived)
        order, (grad_tokens,) = vit_lower.step(order, (grad_tokens,))
        order, (grad_map,) = vit_lower.step(order, (grad_map,), vit_upper)
        vit_lower.last_step()
    map_home, tokens_home = sent_home(grad_map), sent_home(grad_tokens)

    vit_extras = jnp.concatenate([token_sums[0], inner_sums[0], token_sums[1], inner_sums[1]])
    vit_extras = sum_over("strip", sum_over("dp", vit_extras, (1, 2)))
    vit_extras, conv_extras = (sum_over("dp", v, above=4) for v in (vit_extras, conv_extras))
    conv_extras = sum_over("strip", conv_extras)
    if chunked:
        conv_out = share_of(row_major(conv_flat, conv_lower.chunk()), conv_flat.chunk, conv_extras)
        vit_out = share_of(row_major(vit_flat, vit_lower.chunk()), vit_flat.chunk, vit_extras)
    else:
        vit_out = owned_chunk([*grads_qkv, *grads_out, *grads_fc], vit_extras)
        conv_out = owned_chunk([*grads_conv, grad_pool], conv_extras)
    return (
        returned(merged, merged_home),
        returned(high_out, high_home).reshape(high_map.shape),
        returned(grad_tokens, tokens_home),
        returned(grad_map, map_home),
        vit_out,
        conv_out,
    )


def solution(mesh):
    images = P("dp", "strip", None)
    maps = P("dp", "strip", None, None)
    flat = P(("dp", "strip"))
    in_specs = (images, maps, P("dp")) + (P(),) * 15 + (images, maps)
    out_specs = (images, maps, images, maps, flat, flat)
    return jax.shard_map(
        per_device, mesh=mesh, in_specs=in_specs, out_specs=out_specs, check_vma=False
    )
```
